128 devices in a mesh: seq: 32 (over z, y, core), head: 4 (over x).
Axes of the slice: x: 4, y: 4, z: 4, core: 2. Of those that a mesh axis runs over, the one named last changes fastest.
Arguments:
- queries: bfloat16 [32768, 8, 128], P('seq', 'head'), may hold values from -6 to 6
- key_rows: bfloat16 [32768, 8, 128], P('seq', 'head'), may hold values from -6 to 6
- value_rows: bfloat16 [32768, 8, 128], P('seq', 'head'), may hold values from -6 to 6
- level_weights: float32 [16, 8, 32768], P(None, 'head', 'seq'), may hold values from 0.25 to 2
- out_weight: bfloat16 [8, 128, 2048], P('head'), may hold values from -0.1875 to 0.1875
- out_grad: bfloat16 [32768, 2048], P('seq', 'head'), may hold values from -6 to 6
Outputs:
- layer_out: bfloat16 [32768, 2048], P('seq', 'head')
- query_grad: bfloat16 [32768, 8, 128], P('seq', 'head')
- key_grad: bfloat16 [32768, 8, 128], P('seq', 'head')
- value_grad: bfloat16 [32768, 8, 128], P('seq', 'head')
- weight_grad: float32 [16, 8, 32768], P(None, 'head', 'seq')
The draws below stay inside these ranges and needn't reach their ends.
All inputs are finite; a program needn't handle non-finite values.
Results may differ from the reference program's by a relative error of at most 0.017.
Values may be sent and summed in bfloat16 or wider, within the bound.
A program may use at most 192 MiB of HBM per device.

```python
import math
import jax
import jax.numpy as jnp
from jax import lax

D = 2048
HEADS = 8
HD = 128
TOK_DEV = 1024
TOKENS = 32768
TOK_BITS = 10
DEV_BITS = 5
LEVELS = 16
N_SEQ = 32
N_HEAD = 4


def steps_of(own_key, dims, shards, least, top_value):
    level, own = 1.0, jax.random.fold_in(own_key, 6)
    for dim, shards_of in shards:
        draws = jnp.exp(jax.random.uniform(jax.random.fold_in(own, dim), (shards_of,), jnp.float32, least / len(shards), top_value / len(shards)))
        level = level * jnp.repeat(draws, dims[dim] // shards_of).reshape([-1 if axis == dim else 1 for axis in range(len(dims))])
    return level


def noise(rng, extent, scale, reach, pieces=(), held_as=jnp.bfloat16):
    result = scale * jax.random.normal(rng, extent, jnp.float32)
    if pieces:
        result = result * steps_of(rng, extent, pieces, -0.22, 0.18)
    return jnp.clip(result, -reach, reach).astype(held_as)


def setup_inputs(seed: int = 0) -> dict:
    key_of = jax.random.split(jax.random.key(seed), 7)
    queries = noise(key_of[0], (TOKENS, HEADS, HD), 1.0, 6.0, ((0, 32), (1, 4)))
    key_rows = noise(key_of[1], (TOKENS, HEADS, HD), 1.0, 6.0, ((0, 32), (1, 4)))
    value_rows = noise(key_of[2], (TOKENS, HEADS, HD), 1.0, 6.0, ((0, 32), (1, 4)))
    level_weights = jnp.clip(jnp.exp(math.log(2.0) - 2.0794415 * jax.random.uniform(key_of[3], (LEVELS, HEADS, TOKENS), jnp.float32) ** steps_of(key_of[3], (LEVELS, HEADS, TOKENS), ((1, 4), (2, 32)), -0.2, 0.2)), 0.25, 2.0)
    out_weight = noise(key_of[4], (HEADS, HD, D), (HEADS * HD) ** -0.5, 0.1875, ((0, 4),))
    out_grad = noise(key_of[5], (TOKENS, D), 1.0, 6.0, ((0, 32), (1, 4)))
    return dict(queries=queries, key_rows=key_rows, value_rows=value_rows, level_weights=level_weights, out_weight=out_weight, out_grad=out_grad)


LEVEL_GAIN = 0.02
HIGHEST = lax.Precision.HIGHEST


def bit_length(number, bit_count):
    counted = jnp.zeros(number.shape, jnp.int32)
    for offset in range(bit_count):
        counted = counted + ((number >> offset) > 0).astype(jnp.int32)
    return counted


def level_scales(levels):
    index_list = jnp.arange(levels, dtype=jnp.int32)
    return LEVEL_GAIN * jnp.exp2(-0.5 * jnp.maximum(index_list - 1, 0).astype(jnp.float32))


def rounded(values):
    narrow = lax.optimization_barrier(values.astype(jnp.bfloat16))
    return narrow.astype(jnp.float32)


def block_terms(operands):
    query_f, key_f, value_f, grad_f, weighted, states, total_grad = operands
    local_levels = TOK_BITS + 1
    scales = level_scales(LEVELS)
    positions = jnp.arange(TOK_DEV, dtype=jnp.int32)
    level_map = bit_length(positions[:, None] ^ positions[None, :], TOK_BITS)
    level_map = jnp.where(positions[None, :] <= positions[:, None], level_map, -1)
    mixing = jnp.zeros((HEADS, TOK_DEV, TOK_DEV), jnp.float32)
    for level_id in range(local_levels):
        mixing = jnp.where((level_map == level_id)[None], weighted[level_id][:, :, None], mixing)
    scores = jnp.einsum("ihd,jhd->hij", query_f, key_f)
    near_scores = rounded(mixing * scores)
    near_out = jnp.einsum("hij,jhd->ihd", near_scores, value_f)
    grad_scores = jnp.einsum("ihd,jhd->hij", grad_f, value_f)
    near_grads = rounded(mixing * grad_scores)
    query_near = jnp.einsum("hij,jhd->ihd", near_grads, key_f)
    key_near = jnp.einsum("hij,ihd->jhd", near_grads, query_f)
    value_near = jnp.einsum("hij,ihd->jhd", near_scores, grad_f)
    product = scores * grad_scores
    near_weight = jnp.stack([jnp.sum(jnp.where((level_map == level_id)[None], product, 0.0), axis=2)
                             for level_id in range(local_levels)])
    near_weight = near_weight * scales[:local_levels][:, None, None]
    cross_weights = weighted[local_levels:]
    query_states = jnp.einsum("ihd,chde->cihe", query_f, states, precision=HIGHEST)
    out_cross = jnp.einsum("chi,cihe->ihe", cross_weights, query_states, precision=HIGHEST)
    grad_states = jnp.einsum("ihe,chde->cihd", grad_f, states, precision=HIGHEST)
    query_cross = jnp.einsum("chi,cihd->ihd", cross_weights, grad_states, precision=HIGHEST)
    far_weight = scales[local_levels:][:, None, None] * jnp.einsum("cihe,ihe->chi", query_states, grad_f, precision=HIGHEST)
    key_cross = jnp.einsum("jhe,hde->jhd", value_f, total_grad, precision=HIGHEST)
    value_cross = jnp.einsum("jhd,hde->jhe", key_f, total_grad, precision=HIGHEST)
    heads_out = (near_out + out_cross).astype(jnp.bfloat16)
    query_grad = (query_near + query_cross).astype(jnp.bfloat16)
    key_grad = (key_near + key_cross).astype(jnp.bfloat16)
    value_grad = (value_near + value_cross).astype(jnp.bfloat16)
    weight_grad = jnp.concatenate([near_weight, far_weight], axis=0)
    return heads_out, query_grad, key_grad, value_grad, weight_grad


def reference(queries, key_rows, value_rows, level_weights, out_weight, out_grad):
    local_levels = TOK_BITS + 1
    scales = level_scales(LEVELS)
    weighted = level_weights * scales[:, None, None]
    out_f = out_weight.astype(jnp.float32)
    head_grad = jnp.einsum("tc,hdc->thd", out_grad.astype(jnp.float32), out_f).astype(jnp.bfloat16)
    block_shape = (N_SEQ, TOK_DEV, HEADS, HD)
    query_b = queries.astype(jnp.float32).reshape(block_shape)
    key_b = key_rows.astype(jnp.float32).reshape(block_shape)
    value_b = value_rows.astype(jnp.float32).reshape(block_shape)
    grad_b = head_grad.astype(jnp.float32).reshape(block_shape)
    weighted_b = jnp.transpose(weighted.reshape(LEVELS, HEADS, N_SEQ, TOK_DEV), (2, 0, 1, 3))
    totals = jnp.einsum("bjhd,bjhe->bhde", key_b, value_b, precision=HIGHEST)
    cross_b = jnp.transpose(weighted_b[:, local_levels:], (0, 1, 3, 2))
    scaled_queries = cross_b[..., None] * query_b[:, None]
    level_grads = jnp.einsum("bcihd,bihe->bchde", scaled_queries, grad_b, precision=HIGHEST)
    block_ids = jnp.arange(N_SEQ, dtype=jnp.int32)
    depth_map = bit_length(block_ids[:, None] ^ block_ids[None, :], DEV_BITS)
    level_ids = jnp.arange(1, DEV_BITS + 1, dtype=jnp.int32)
    below = ((block_ids[None, :] < block_ids[:, None])[:, None, :]
             & (depth_map[:, None, :] == level_ids[None, :, None])).astype(jnp.float32)
    states = jnp.einsum("dce,ehxy->dchxy", below, totals, precision=HIGHEST)
    total_grad = jnp.einsum("dce,dchxy->ehxy", below, level_grads, precision=HIGHEST)
    heads_out, query_grad, key_grad, value_grad, weight_grad = lax.map(
        block_terms, (query_b, key_b, value_b, grad_b, weighted_b, states, total_grad))
    flat_shape = (TOKENS, HEADS, HD)
    heads_out = heads_out.reshape(flat_shape)
    group_size = HEADS // N_HEAD
    layer_sum = jnp.zeros((TOKENS, D), jnp.float32)
    for group_id in range(N_HEAD):
        lower = group_id * group_size
        partial_sum = jnp.einsum("thd,hdc->tc", heads_out[:, lower:lower + group_size].astype(jnp.float32),
                                 out_f[lower:lower + group_size])
        layer_sum = layer_sum + rounded(partial_sum)
    layer_out = layer_sum.astype(jnp.bfloat16)
    weight_grad = jnp.transpose(weight_grad, (1, 2, 0, 3)).reshape(LEVELS, HEADS, TOKENS)
    return (layer_out, query_grad.reshape(flat_shape), key_grad.reshape(flat_shape),
            value_grad.reshape(flat_shape), weight_grad)
```

```python
import functools

import jax
import jax.numpy as jnp
from jax import lax
from jax.experimental import pallas as pl
from jax.experimental.pallas import tpu as pltpu
from jax.sharding import PartitionSpec as P

MESH = pl.DeviceIdType.MESH
F32 = jnp.float32
BF16 = jnp.bfloat16
LEVEL_GAIN = 0.02
BLK = 128
DIAG_LEVELS = 8
LOCAL_LEVELS = 11


def scale_of(level):
    return LEVEL_GAIN * 2.0 ** (-0.5 * max(level - 1, 0))


LOCAL_PAIRS = [(0, 1, 1), (0, 3, 1), (0, 5, 1), (0, 7, 1), (1, 2, 2), (1, 6, 2), (2, 4, 4)]


def mm(a, b):
    return jnp.dot(a, b, preferred_element_type=F32)


def mm_nt(a, b):
    return lax.dot_general(a, b, (((1,), (1,)), ((), ())), preferred_element_type=F32)


def kernel(
    dev_bits, q_ref, k_ref, v_ref, lw_ref, w_hbm, og_ref,
    lo_ref, dq_ref, dk_ref, dv_ref, wg_ref,
    wall, wsc, lev_ref, qt, kt, vt, gt, wq, st_ref, mix_ref, near, tb, tl, tlt, ot,
    sb, rb, cb, rcb, tst, tstt, lg, xf, llg,
    p2, alone, pf, summed, r1, rdir, hall, dqa, dka, dva, acc,
    own_sem, w_send, w_recv, f_send, f_recv, b_send, b_recv, c_send, c_recv, r_send, r_recv, h_send, h_recv,
):
    me_s = lax.axis_index("seq")
    me_h = lax.axis_index("head")
    core = lax.rem(me_s, 2)
    right, left, across = lax.rem(me_h + 1, 4), lax.rem(me_h + 3, 4), lax.rem(me_h + 2, 4)

    def partner(step):
        bit = 1 << step
        has = lax.rem(lax.div(me_s, bit), 2)
        return me_s + bit - 2 * bit * has, has

    def send(src, dst, send_sem, recv_sem, seq, head):
        copy = pltpu.make_async_remote_copy(
            src_ref=src, dst_ref=dst, send_sem=send_sem, recv_sem=recv_sem,
            device_id=(seq, head), device_id_type=MESH,
        )
        copy.start()
        return copy

    barrier = pltpu.get_barrier_semaphore()
    for other in (right, left, across):
        pl.semaphore_signal(barrier, inc=1, device_id=(me_s, other), device_id_type=MESH)
    for step in range(dev_bits):
        pl.semaphore_signal(barrier, inc=1, device_id=(partner(step)[0], me_h), device_id_type=MESH)
    pl.semaphore_wait(barrier, 3 + dev_bits)

    own = pltpu.make_async_copy(w_hbm.at[:, pl.ds(pl.multiple_of(me_h * 512, 512), 512)], wall.at[0], own_sem)
    half = pl.ds(pl.multiple_of(core * 128, 128), 128)
    w_copies = {}
    for k in (2, 1, 3):
        to = lax.rem(me_h + k, 4)
        w_copies[k] = send(
            w_hbm.at[half, pl.ds(pl.multiple_of(to * 512, 512), 512)], wall.at[k, half],
            w_send.at[k - 1], w_recv.at[k - 1], me_s, to)
    own.start()
    sibling = partner(0)[0]
    f_copies = {}

    def forward_weights(k):
        w_copies[k].wait_recv()
        f_copies[k] = send(wall.at[k, half], wall.at[k, half], f_send.at[k - 1], f_recv.at[k - 1], sibling, me_h)

    row_id = lax.broadcasted_iota(jnp.int32, (BLK, BLK), 0)
    col_id = lax.broadcasted_iota(jnp.int32, (BLK, BLK), 1)
    apart = row_id ^ col_id
    level = jnp.zeros((BLK, BLK), jnp.int32)
    for bit in range(7):
        level = level + ((apart >> bit) > 0).astype(jnp.int32)
    lev_ref[...] = jnp.where(row_id <= col_id, level, -1)

    def cols_of(b):
        return pl.ds(pl.multiple_of(b * BLK, BLK), BLK)

    @pl.loop(0, 8)
    def _(b):
        cols = cols_of(b)
        for h in range(2):
            lanes = slice(h * 128, h * 128 + 128)
            kb, vb = k_ref[cols, lanes].T, v_ref[cols, lanes].T
            kt[h, :, cols] = kb
            vt[h, :, cols] = vb
            tb[h, b] = mm_nt(kb, vb)

    total = []
    for h in range(2):
        t = [tb[h, b] for b in range(8)]
        pairs = [t[2 * i] + t[2 * i + 1] for i in range(4)]
        quads = [pairs[0] + pairs[1], pairs[2] + pairs[3]]
        for slot, value in enumerate([t[0], t[2], t[4], t[6], pairs[0], pairs[2], quads[0]]):
            tl[h, slot] = value.astype(BF16)
            tlt[h, slot] = value.T.astype(BF16)
        xf[h] = quads[0] + quads[1]

    b_copies = []

    def send_states(step):
        for h in range(2):
            sb[step, h] = xf[h].astype(BF16)
        b_copies.append(send(sb.at[step], rb.at[step], b_send.at[step], b_recv.at[step], partner(step)[0], me_h))

    def take_states(step):
        b_copies[step].wait_recv()
        has = partner(step)[1].astype(F32)
        for h in range(2):
            got = rb[step, h].astype(F32)
            xf[h] = xf[h] + got
            kept = got * has
            tst[h, step] = kept.astype(BF16)
            tstt[h, :, step * 128:step * 128 + 128] = kept.T.astype(BF16)

    send_states(0)
    forward_weights(2)

    for h in range(2):
        for l in range(LOCAL_LEVELS + dev_bits):
            wsc[h, l:l + 1, :] = lw_ref[l, h:h + 1, :] * scale_of(l)

    @pl.loop(0, 8)
    def _(b):
        cols = cols_of(b)
        for h in range(2):
            qb = q_ref[cols, h * 128:h * 128 + 128].T
            qt[h, :, cols] = qb
            qf = qb.astype(F32)
            for c in range(3 + dev_bits):
                wq[h, c, :, cols] = (qf * wsc[h, DIAG_LEVELS + c:DIAG_LEVELS + c + 1, cols]).astype(BF16)

    right_msgs, left_msgs = {}, {}

    def send_right(i, src, dst):
        right_msgs[i] = send(src, dst, r_send.at[i], r_recv.at[i], me_s, right)

    def send_left(i, src, dst):
        left_msgs[i] = send(src, dst, r_send.at[6 + i], r_recv.at[6 + i], me_s, left)

    def partial_grad(k, u, j):
        rows = slice(u * 512 + j * 256, u * 512 + j * 256 + 256)
        return mm_nt(wall[k], og_ref[rows, :])

    f_copies[2].wait_recv()
    for u in range(2):
        for j in range(2):
            part = partial_grad(2, u, j).astype(BF16)
            p2[0, u, :, j * 256:j * 256 + 256] = part[:128]
            p2[1, u, :, j * 256:j * 256 + 256] = part[128:]
        send_right(u, p2.at[0, u], r1.at[0, u])
        send_left(u, p2.at[1, u], r1.at[1, u])

    forward_weights(1)
    forward_weights(3)
    take_states(0)
    send_states(1)

    def diag_forward(b):
        cols = cols_of(b)
        for h in range(2):
            lev = lev_ref[...]
            mix = jnp.zeros((BLK, BLK), F32)
            for l in range(DIAG_LEVELS):
                mix = jnp.where(lev == l, wsc[h, l:l + 1, cols], mix)
            scores = mm(k_ref[cols, h * 128:h * 128 + 128], qt[h, :, cols])
            weighted = (mix * scores).astype(BF16)
            st_ref[h, b] = scores
            mix_ref[h, b] = mix
            near[h, b] = weighted
            ot[h, :, cols] = mm(vt[h, :, cols], weighted)

    pl.loop(0, 4)(diag_forward)
    f_copies[1].wait_recv()
    f_copies[3].wait_recv()
    for u in range(2):
        for j in range(2):
            at = slice(j * 256, j * 256 + 256)
            part = partial_grad(3, u, j)
            pf[0, u, :, at] = part[:128]
            alone[0, u, :, at] = part[128:].astype(BF16)
            part = partial_grad(1, u, j)
            alone[1, u, :, at] = part[:128].astype(BF16)
            pf[1, u, :, at] = part[128:]
        send_right(2 + u, alone.at[0, u], rdir.at[0, 1, u])
        send_left(2 + u, alone.at[1, u], rdir.at[1, 0, u])
    take_states(1)
    send_states(2)
    pl.loop(4, 8)(diag_forward)

    for u in range(2):
        right_msgs[u].wait_recv()
        summed[0, u] = (pf[0, u] + r1[0, u].astype(F32)).astype(BF16)
        send_right(4 + u, summed.at[0, u], rdir.at[0, 0, u])
        left_msgs[u].wait_recv()
        summed[1, u] = (pf[1, u] + r1[1, u].astype(F32)).astype(BF16)
        send_left(4 + u, summed.at[1, u], rdir.at[1, 1, u])
    take_states(2)
    if dev_bits > 3:
        send_states(3)

    for h in range(2):
        for slot, (c, first, size) in enumerate(LOCAL_PAIRS):
            at = slice(first * BLK, (first + size) * BLK)
            ot[h, :, at] = ot[h, :, at] + mm(tlt[h, slot], wq[h, c, :, at])

    own.wait()
    for u in range(2):
        for j in range(2):
            at = slice(j * 256, j * 256 + 256)
            part = partial_grad(0, u, j)
            pf[0, u, :, at] = part[:128]
            pf[1, u, :, at] = part[128:]
    for step in range(3, dev_bits):
        take_states(step)
        if step + 1 < dev_bits:
            send_states(step + 1)

    @pl.loop(0, 8)
    def _(b):
        cols = cols_of(b)
        for h in range(2):
            far = mm(tstt[h], wq[h, 3:, :, cols].reshape(dev_bits * 128, BLK))
            hall[0, cols, h * 128:h * 128 + 128] = (ot[h, :, cols] + far).T.astype(BF16)

    h_copies = {}

    def send_heads(i, slot, part, to_slot, head):
        rows = slice(part * 512, part * 512 + 512)
        h_copies[i] = send(hall.at[slot, rows], hall.at[to_slot, rows], h_send.at[i], h_recv.at[i], me_s, head)

    send_heads(0, 0, 0, 1, right)
    send_heads(1, 0, 1, 3, left)
    send_heads(2, 0, 1, 1, right)
    send_heads(3, 0, 0, 3, left)

    for u in range(2):
        at = slice(u * 512, u * 512 + 512)
        right_msgs[2 + u].wait_recv()
        left_msgs[2 + u].wait_recv()
        right_msgs[4 + u].wait_recv()
        left_msgs[4 + u].wait_recv()
        for h in range(2):
            gt[h, :, at] = (pf[h, u] + rdir[0, h, u].astype(F32) + rdir[1, h, u].astype(F32)).astype(BF16)

    for h in range(2):
        grads = mm_nt(wq[h, 3:].reshape(dev_bits * 128, 1024), gt[h])
        for step in range(dev_bits):
            lg[h, step] = grads[step * 128:step * 128 + 128]
        xf[h] = jnp.zeros((128, 128), F32)

    c_copies = {}

    def send_grads(step):
        to, has = partner(step)
        for h in range(2):
            cb[step, h] = (xf[h] + lg[h, step] * has.astype(F32)).astype(BF16)
        c_copies[step] = send(cb.at[step], rcb.at[step], c_send.at[step], c_recv.at[step], to, me_h)

    def take_grads(step):
        c_copies[step].wait_recv()
        for h in range(2):
            xf[h] = xf[h] + rcb[step, h].astype(F32)

    def diag_backward(b):
        cols = cols_of(b)
        for h in range(2):
            lev = lev_ref[...]
            gb = gt[h, :, cols]
            grad_scores = mm(v_ref[cols, h * 128:h * 128 + 128], gb)
            weighted = (mix_ref[h, b] * grad_scores).astype(BF16)
            product = grad_scores * st_ref[h, b]
            dqa[h, :, cols] = mm(kt[h, :, cols], weighted)
            dka[h, :, cols] = mm_nt(qt[h, :, cols], weighted)
            dva[h, :, cols] = mm_nt(gb, near[h, b])
            for l in range(DIAG_LEVELS):
                summed_l = jnp.sum(jnp.where(lev == l, product, 0.0), axis=0, keepdims=True)
                wg_ref[l, h:h + 1, cols] = summed_l * scale_of(l)

    def far_backward(b):
        cols = cols_of(b)
        for h in range(2):
            gb = gt[h, :, cols]
            qf = qt[h, :, cols].astype(F32)
            sums = dqa[h, :, cols]
            for step in range(dev_bits):
                l = LOCAL_LEVELS + step
                got = mm(tst[h, step], gb)
                sums = sums + got * wsc[h, l:l + 1, cols]
                wg_ref[l, h:h + 1, cols] = jnp.sum(got * qf, axis=0, keepdims=True) * scale_of(l)
            dqa[h, :, cols] = sums

    def local_backward(h):
        for l in range(DIAG_LEVELS, LOCAL_LEVELS):
            wg_ref[l, h:h + 1, :] = jnp.zeros((1, 1024), F32)
        for slot, (c, first, size) in enumerate(LOCAL_PAIRS):
            at = slice(first * BLK, (first + size) * BLK)
            l = DIAG_LEVELS + c
            gb = gt[h, :, at]
            got = mm(tl[h, slot], gb)
            dqa[h, :, at] = dqa[h, :, at] + got * wsc[h, l:l + 1, at]
            wg_ref[l, h:h + 1, at] = jnp.sum(got * qt[h, :, at].astype(F32), axis=0, keepdims=True) * scale_of(l)
            llg[h, slot] = mm_nt(wq[h, c, :, at], gb)

    work = [
        lambda: pl.loop(0, 4)(diag_backward),
        lambda: pl.loop(4, 8)(diag_backward),
        lambda: pl.loop(0, 4)(far_backward),
        lambda: pl.loop(4, 8)(far_backward),
        lambda: [local_backward(h) for h in range(2)],
    ]
    relayed = 0
    for step in reversed(range(dev_bits)):
        send_grads(step)
        if work:
            work.pop(0)()
        take_grads(step)
        if step == dev_bits - 2:
            h_copies[0].wait_recv()
            send_heads(4, 1, 0, 2, right)
            h_copies[1].wait_recv()
            send_heads(5, 3, 1, 2, left)
    for item in work:
        item()

    @pl.loop(0, 8)
    def _(b):
        cols = cols_of(b)
        for h in range(2):
            dq_ref[cols, h * 128:h * 128 + 128] = dqa[h, :, cols].T.astype(BF16)

    for b in range(8):
        at = slice(b * BLK, b * BLK + BLK)
        for h in range(2):
            x = xf[h]
            for slot, (c, first, size) in enumerate(LOCAL_PAIRS):
                if first - size <= b < first:
                    x = x + llg[h, slot]
            dk = dka[h, :, at] + mm(x.astype(BF16), vt[h, :, at])
            dv = dva[h, :, at] + mm(x.T.astype(BF16), kt[h, :, at])
            dk_ref[at, h * 128:h * 128 + 128] = dk.T.astype(BF16)
            dv_ref[at, h * 128:h * 128 + 128] = dv.T.astype(BF16)

    @pl.loop(0, 4)
    def _(b):
        rows = pl.ds(pl.multiple_of(b * 256, 256), 256)
        acc[rows, :] = mm(hall[0, rows, :], wall[0])

    h_copies[2].wait_recv()
    h_copies[3].wait_recv()

    @pl.loop(0, 4)
    def _(b):
        rows = pl.ds(pl.multiple_of(b * 256, 256), 256)
        acc[rows, :] = acc[rows, :] + mm(hall[1, rows, :], wall[1]) + mm(hall[3, rows, :], wall[3])

    h_copies[4].wait_recv()
    h_copies[5].wait_recv()

    @pl.loop(0, 4)
    def _(b):
        rows = pl.ds(pl.multiple_of(b * 256, 256), 256)
        lo_ref[rows, :] = (acc[rows, :] + mm(hall[2, rows, :], wall[2])).astype(BF16)

    for group in (w_copies, f_copies, right_msgs, left_msgs, h_copies, c_copies):
        for copy in group.values():
            copy.wait_send()
    for copy in b_copies:
        copy.wait_send()


def per_device(queries, key_rows, value_rows, level_weights, out_weight, out_grad):
    dev_bits = lax.axis_size("seq").bit_length() - 1
    dma = pltpu.SemaphoreType.DMA
    vmem = pltpu.VMEM
    full = pl.BlockSpec(memory_space=pltpu.VMEM)
    stack = 3 + dev_bits
    outs = pl.pallas_call(
        functools.partial(kernel, dev_bits),
        out_shape=(
            jax.ShapeDtypeStruct((1024, 512), BF16),
            jax.ShapeDtypeStruct((1024, 256), BF16),
            jax.ShapeDtypeStruct((1024, 256), BF16),
            jax.ShapeDtypeStruct((1024, 256), BF16),
            jax.ShapeDtypeStruct(level_weights.shape, F32),
        ),
        in_specs=[full, full, full, full, pl.BlockSpec(memory_space=pl.ANY), full],
        out_specs=[full] * 5,
        scratch_shapes=[
            vmem((4, 256, 512), BF16),
            vmem((2, LOCAL_LEVELS + dev_bits, 1024), F32),
            vmem((BLK, BLK), jnp.int32),
            vmem((2, 128, 1024), BF16),
            vmem((2, 128, 1024), BF16),
            vmem((2, 128, 1024), BF16),
            vmem((2, 128, 1024), BF16),
            vmem((2, stack, 128, 1024), BF16),
            vmem((2, 8, BLK, BLK), F32),
            vmem((2, 8, BLK, BLK), F32),
            vmem((2, 8, BLK, BLK), BF16),
            vmem((2, 8, 128, 128), F32),
            vmem((2, 7, 128, 128), BF16),
            vmem((2, 7, 128, 128), BF16),
            vmem((2, 128, 1024), F32),
            vmem((dev_bits, 2, 128, 128), BF16),
            vmem((dev_bits, 2, 128, 128), BF16),
            vmem((dev_bits, 2, 128, 128), BF16),
            vmem((dev_bits, 2, 128, 128), BF16),
            vmem((2, dev_bits, 128, 128), BF16),
            vmem((2, 128, dev_bits * 128), BF16),
            vmem((2, dev_bits, 128, 128), F32),
            vmem((2, 128, 128), F32),
            vmem((2, 7, 128, 128), F32),
            vmem((2, 2, 128, 512), BF16),
            vmem((2, 2, 128, 512), BF16),
            vmem((2, 2, 128, 512), F32),
            vmem((2, 2, 128, 512), BF16),
            vmem((2, 2, 128, 512), BF16),
            vmem((2, 2, 2, 128, 512), BF16),
            vmem((4, 1024, 256), BF16),
            vmem((2, 128, 1024), F32),
            vmem((2, 128, 1024), F32),
            vmem((2, 128, 1024), F32),
            vmem((1024, 512), F32),
            dma,
            dma((3,)), dma((3,)), dma((3,)), dma((3,)),
            dma((dev_bits,)), dma((dev_bits,)), dma((dev_bits,)), dma((dev_bits,)),
            dma((12,)), dma((12,)), dma((6,)), dma((6,)),
        ],
        compiler_params=pltpu.CompilerParams(
            collective_id=0, has_side_effects=True, vmem_limit_bytes=56 * 1024 * 1024),
        cost_estimate=pl.CostEstimate(flops=6 * 10**9, bytes_accessed=8 * 2**20, transcendentals=0),
    )(
        queries.reshape(1024, 256), key_rows.reshape(1024, 256), value_rows.reshape(1024, 256),
        level_weights, out_weight.reshape(256, 2048), out_grad,
    )
    layer_out, dq, dk, dv, wg = outs
    shape = queries.shape
    return layer_out, dq.reshape(shape), dk.reshape(shape), dv.reshape(shape), wg


def solution(mesh):
    in_specs = (
        P("seq", "head", None),
        P("seq", "head", None),
        P("seq", "head", None),
        P(None, "head", "seq"),
        P("head", None, None),
        P("seq", "head"),
    )
    out_specs = (
        P("seq", "head"),
        P("seq", "head", None),
        P("seq", "head", None),
        P("seq", "head", None),
        P(None, "head", "seq"),
    )
    return jax.shard_map(
        per_device, mesh=mesh, in_specs=in_specs, out_specs=out_specs, check_vma=False
    )
```

```python
import functools

import jax
import jax.numpy as jnp
from jax import lax
from jax.experimental import pallas as pl
from jax.experimental.pallas import tpu as pltpu
from jax.sharding import PartitionSpec as P

MESH = pl.DeviceIdType.MESH
F32 = jnp.float32
BF16 = jnp.bfloat16
LEVEL_GAIN = 0.02
BLK = 128
DIAG_LEVELS = 8
DEV_BITS = 5
PHASES = ((0,), (1, 2, 3), (4, 5, 6))
LOCAL_LEVELS = 11


def scale_of(level):
    return LEVEL_GAIN * 2.0 ** (-0.5 * max(level - 1, 0))


LOCAL_PAIRS = [(0, 1, 1), (0, 3, 1), (0, 5, 1), (0, 7, 1), (1, 2, 2), (1, 6, 2), (2, 4, 4)]


def mm(a, b):
    return jnp.dot(a, b, preferred_element_type=F32)


def mm_nt(a, b):
    return lax.dot_general(a, b, (((1,), (1,)), ((), ())), preferred_element_type=F32)


def kernel(
    q_in, k_in, v_in, lw_in, w_hbm, og_in,
    lo_out, dq_out, dk_out, dv_out, wg_out,
    q_ref, k_ref, v_ref, lw_ref, og_ref, lo_ref, dq_ref, dk_ref, dv_ref, wg_ref, kn, vn,
    wall, wsc, lev_ref, qt, kt, vt, gt, wq, st_ref, mix_ref, near, tb, tl, tlt, ot,
    sb, rb, cb, rcb, tst, tstt, lg, xf, llg,
    p2, alone, pf, summed, r1, rdir, hall, dqa, dka, dva, acc,
    in_sem, out_sem, own_sem, w_send, w_recv, f_send, f_recv, b_send, b_recv, c_send, c_recv, r_send, r_recv, h_send, h_recv,
):
    me_s = lax.axis_index("seq")
    me_h = lax.axis_index("head")
    core = lax.rem(me_s, 2)
    right, left, across = lax.rem(me_h + 1, 4), lax.rem(me_h + 3, 4), lax.rem(me_h + 2, 4)

    def bit_of(bit):
        return lax.rem(lax.div(me_s, 1 << bit), 2)

    def flipped(bits):
        to = me_s
        for bit in bits:
            to = to + (1 << bit) - (2 << bit) * bit_of(bit)
        return to

    def partner(step):
        if step == 0:
            return flipped([0])
        low, j = (1, step) if step < 4 else (3, step - 3)
        return flipped([low + i for i in range(2) if j >> i & 1])

    def send(src, dst, send_sem, recv_sem, seq, head):
        copy = pltpu.make_async_remote_copy(
            src_ref=src, dst_ref=dst, send_sem=send_sem, recv_sem=recv_sem,
            device_id=(seq, head), device_id_type=MESH,
        )
        copy.start()
        return copy

    loads = []
    for n, (src, dst) in enumerate([(k_in, k_ref), (v_in, v_ref), (lw_in, lw_ref), (q_in, q_ref), (og_in, og_ref)]):
        loads.append(pltpu.make_async_copy(src, dst, in_sem.at[n]))
        loads[n].start()

    barrier = pltpu.get_barrier_semaphore()
    for other in (right, left, across):
        pl.semaphore_signal(barrier, inc=1, device_id=(me_s, other), device_id_type=MESH)
    for step in range(7):
        pl.semaphore_signal(barrier, inc=1, device_id=(partner(step), me_h), device_id_type=MESH)
    pl.semaphore_wait(barrier, 10)

    own = pltpu.make_async_copy(w_hbm.at[:, pl.ds(pl.multiple_of(me_h * 512, 512), 512)], wall.at[0], own_sem)
    half = pl.ds(pl.multiple_of(core * 128, 128), 128)
    w_copies = {}
    for k in (2, 1, 3):
        to = lax.rem(me_h + k, 4)
        w_copies[k] = send(
            w_hbm.at[half, pl.ds(pl.multiple_of(to * 512, 512), 512)], wall.at[k, half],
            w_send.at[k - 1], w_recv.at[k - 1], me_s, to)
    own.start()
    sibling = partner(0)
    f_copies = {}

    def forward_weights(k):
        w_copies[k].wait_recv()
        f_copies[k] = send(wall.at[k, half], wall.at[k, half], f_send.at[k - 1], f_recv.at[k - 1], sibling, me_h)

    row_id = lax.broadcasted_iota(jnp.int32, (BLK, BLK), 0)
    col_id = lax.broadcasted_iota(jnp.int32, (BLK, BLK), 1)
    apart = row_id ^ col_id
    level = jnp.zeros((BLK, BLK), jnp.int32)
    for bit in range(7):
        level = level + ((apart >> bit) > 0).astype(jnp.int32)
    lev_ref[...] = jnp.where(row_id <= col_id, level, -1)

    def cols_of(b):
        return pl.ds(pl.multiple_of(b * BLK, BLK), BLK)

    loads[0].wait()
    loads[1].wait()

    @pl.loop(0, 8)
    def _(b):
        cols = cols_of(b)
        k_all, v_all = k_ref[cols].reshape(BLK, 256), v_ref[cols].reshape(BLK, 256)
        for h in range(2):
            lanes = slice(h * 128, h * 128 + 128)
            kn[h, cols, :] = k_all[:, lanes]
            vn[h, cols, :] = v_all[:, lanes]
            kb, vb = k_all[:, lanes].T, v_all[:, lanes].T
            kt[h, :, cols] = kb
            vt[h, :, cols] = vb
            tb[h, b] = mm_nt(kb, vb)

    total = []
    for h in range(2):
        t = [tb[h, b] for b in range(8)]
        pairs = [t[2 * i] + t[2 * i + 1] for i in range(4)]
        quads = [pairs[0] + pairs[1], pairs[2] + pairs[3]]
        for slot, value in enumerate([t[0], t[2], t[4], t[6], pairs[0], pairs[2], quads[0]]):
            tl[h, slot] = value.astype(BF16)
            tlt[h, slot] = value.T.astype(BF16)
        xf[h] = quads[0] + quads[1]

    b_copies = {}

    def send_states(phase):
        for h in range(2):
            sb[phase, h] = xf[h].astype(BF16)
        for step in PHASES[phase]:
            b_copies[step] = send(sb.at[phase], rb.at[step], b_send.at[step], b_recv.at[step], partner(step), me_h)

    def keep_state(h, slot, value):
        kept = value * bit_of(slot).astype(F32)
        tst[h, slot * 128:slot * 128 + 128, :] = kept.astype(BF16)
        tstt[h, :, slot * 128:slot * 128 + 128] = kept.T.astype(BF16)

    def take_states(phase):
        for step in PHASES[phase]:
            b_copies[step].wait_recv()
        for h in range(2):
            got = [rb[step, h].astype(F32) for step in PHASES[phase]]
            if phase == 0:
                keep_state(h, 0, got[0])
                xf[h] = xf[h] + got[0]
            else:
                far = got[1] + got[2]
                keep_state(h, 2 * phase - 1, got[0])
                keep_state(h, 2 * phase, far)
                xf[h] = xf[h] + got[0] + far

    send_states(0)
    forward_weights(2)
    loads[2].wait()
    loads[3].wait()

    for h in range(2):
        for l in range(LOCAL_LEVELS + DEV_BITS):
            wsc[h, l:l + 1, :] = lw_ref[l, h:h + 1, :] * scale_of(l)

    @pl.loop(0, 8)
    def _(b):
        cols = cols_of(b)
        q_all = q_ref[cols].reshape(BLK, 256)
        for h in range(2):
            qb = q_all[:, h * 128:h * 128 + 128].T
            qt[h, :, cols] = qb
            qf = qb.astype(F32)
            for c in range(3 + DEV_BITS):
                wq[h, c, :, cols] = (qf * wsc[h, DIAG_LEVELS + c:DIAG_LEVELS + c + 1, cols]).astype(BF16)

    right_msgs, left_msgs = {}, {}

    def send_right(i, src, dst):
        right_msgs[i] = send(src, dst, r_send.at[i], r_recv.at[i], me_s, right)

    def send_left(i, src, dst):
        left_msgs[i] = send(src, dst, r_send.at[6 + i], r_recv.at[6 + i], me_s, left)

    def partial_grad(k, u, j):
        rows = slice(u * 512 + j * 256, u * 512 + j * 256 + 256)
        return mm_nt(wall[k], og_ref[rows, :])

    take_states(0)
    send_states(1)
    loads[4].wait()
    f_copies[2].wait_recv()
    for u in range(2):
        for j in range(2):
            part = partial_grad(2, u, j).astype(BF16)
            p2[0, u, :, j * 256:j * 256 + 256] = part[:128]
            p2[1, u, :, j * 256:j * 256 + 256] = part[128:]
        send_right(u, p2.at[0, u], r1.at[0, u])
        send_left(u, p2.at[1, u], r1.at[1, u])

    forward_weights(1)
    forward_weights(3)

    def diag_forward(b):
        cols = cols_of(b)
        for h in range(2):
            lev = lev_ref[...]
            mix = jnp.zeros((BLK, BLK), F32)
            for l in range(DIAG_LEVELS):
                mix = jnp.where(lev == l, wsc[h, l:l + 1, cols], mix)
            scores = mm(kn[h, cols, :], qt[h, :, cols])
            weighted = (mix * scores).astype(BF16)
            st_ref[h, b] = scores
            mix_ref[h, b] = mix
            near[h, b] = weighted
            ot[h, :, cols] = mm(vt[h, :, cols], weighted)

    pl.loop(0, 4)(diag_forward)
    f_copies[1].wait_recv()
    f_copies[3].wait_recv()
    for u in range(2):
        for j in range(2):
            at = slice(j * 256, j * 256 + 256)
            part = partial_grad(3, u, j)
            pf[0, u, :, at] = part[:128]
            alone[0, u, :, at] = part[128:].astype(BF16)
            part = partial_grad(1, u, j)
            alone[1, u, :, at] = part[:128].astype(BF16)
            pf[1, u, :, at] = part[128:]
        send_right(2 + u, alone.at[0, u], rdir.at[0, 1, u])
        send_left(2 + u, alone.at[1, u], rdir.at[1, 0, u])
    take_states(1)
    send_states(2)
    pl.loop(4, 8)(diag_forward)

    for u in range(2):
        right_msgs[u].wait_recv()
        summed[0, u] = (pf[0, u] + r1[0, u].astype(F32)).astype(BF16)
        send_right(4 + u, summed.at[0, u], rdir.at[0, 0, u])
        left_msgs[u].wait_recv()
        summed[1, u] = (pf[1, u] + r1[1, u].astype(F32)).astype(BF16)
        send_left(4 + u, summed.at[1, u], rdir.at[1, 1, u])

    for h in range(2):
        for slot, (c, first, size) in enumerate(LOCAL_PAIRS):
            at = slice(first * BLK, (first + size) * BLK)
            ot[h, :, at] = ot[h, :, at] + mm(tlt[h, slot], wq[h, c, :, at])

    own.wait()
    for u in range(2):
        for j in range(2):
            at = slice(j * 256, j * 256 + 256)
            part = partial_grad(0, u, j)
            pf[0, u, :, at] = part[:128]
            pf[1, u, :, at] = part[128:]
    take_states(2)

    @pl.loop(0, 8)
    def _(b):
        cols = cols_of(b)
        for h in range(2):
            far = mm(tstt[h], wq[h, 3:, :, cols].reshape(DEV_BITS * 128, BLK))
            hall[0, cols, h * 128:h * 128 + 128] = (ot[h, :, cols] + far).T.astype(BF16)

    h_copies = {}

    def send_heads(i, slot, part, to_slot, head):
        rows = slice(part * 512, part * 512 + 512)
        h_copies[i] = send(hall.at[slot, rows], hall.at[to_slot, rows], h_send.at[i], h_recv.at[i], me_s, head)

    send_heads(0, 0, 0, 1, right)
    send_heads(1, 0, 1, 3, left)
    send_heads(2, 0, 1, 1, right)
    send_heads(3, 0, 0, 3, left)

    for u in range(2):
        at = slice(u * 512, u * 512 + 512)
        right_msgs[2 + u].wait_recv()
        left_msgs[2 + u].wait_recv()
        right_msgs[4 + u].wait_recv()
        left_msgs[4 + u].wait_recv()
        for h in range(2):
            gt[h, :, at] = (pf[h, u] + rdir[0, h, u].astype(F32) + rdir[1, h, u].astype(F32)).astype(BF16)

    for h in range(2):
        grads = mm_nt(wq[h, 3:].reshape(DEV_BITS * 128, 1024), gt[h])
        for step in range(DEV_BITS):
            lg[h, step] = grads[step * 128:step * 128 + 128]
        xf[h] = jnp.zeros((128, 128), F32)

    c_copies = {}

    def send_grads(phase):
        for h in range(2):
            if phase == 0:
                cb[0, h] = (xf[h] + lg[h, 0] * bit_of(0).astype(F32)).astype(BF16)
            else:
                for i in range(2):
                    slot = 2 * phase - 1 + i
                    cb[slot, h] = (xf[h] + lg[h, slot] * bit_of(slot).astype(F32)).astype(BF16)
        for n, step in enumerate(PHASES[phase]):
            slot = 2 * phase - 1 + min(n, 1) if phase else 0
            c_copies[step] = send(cb.at[slot], rcb.at[step], c_send.at[step], c_recv.at[step], partner(step), me_h)

    def take_grads(phase):
        for step in PHASES[phase]:
            c_copies[step].wait_recv()
        for h in range(2):
            total_grad = xf[h]
            for step in PHASES[phase]:
                total_grad = total_grad + rcb[step, h].astype(F32)
            xf[h] = total_grad

    def diag_backward(b):
        cols = cols_of(b)
        for h in range(2):
            lev = lev_ref[...]
            gb = gt[h, :, cols]
            grad_scores = mm(vn[h, cols, :], gb)
            weighted = (mix_ref[h, b] * grad_scores).astype(BF16)
            product = grad_scores * st_ref[h, b]
            dqa[h, :, cols] = mm(kt[h, :, cols], weighted)
            dka[h, :, cols] = mm_nt(qt[h, :, cols], weighted)
            dva[h, :, cols] = mm_nt(gb, near[h, b])
            for l in range(DIAG_LEVELS):
                summed_l = jnp.sum(jnp.where(lev == l, product, 0.0), axis=0, keepdims=True)
                wg_ref[l, h:h + 1, cols] = summed_l * scale_of(l)

    def far_backward(b):
        cols = cols_of(b)
        for h in range(2):
            gb = gt[h, :, cols]
            qf = qt[h, :, cols].astype(F32)
            sums = dqa[h, :, cols]
            all_got = mm(tst[h], gb)
            for step in range(DEV_BITS):
                l = LOCAL_LEVELS + step
                got = all_got[step * 128:step * 128 + 128]
                sums = sums + got * wsc[h, l:l + 1, cols]
                wg_ref[l, h:h + 1, cols] = jnp.sum(got * qf, axis=0, keepdims=True) * scale_of(l)
            dqa[h, :, cols] = sums

    def local_backward(h):
        for l in range(DIAG_LEVELS, LOCAL_LEVELS):
            wg_ref[l, h:h + 1, :] = jnp.zeros((1, 1024), F32)
        for slot, (c, first, size) in enumerate(LOCAL_PAIRS):
            at = slice(first * BLK, (first + size) * BLK)
            l = DIAG_LEVELS + c
            gb = gt[h, :, at]
            got = mm(tl[h, slot], gb)
            dqa[h, :, at] = dqa[h, :, at] + got * wsc[h, l:l + 1, at]
            wg_ref[l, h:h + 1, at] = jnp.sum(got * qt[h, :, at].astype(F32), axis=0, keepdims=True) * scale_of(l)
            llg[h, slot] = mm_nt(wq[h, c, :, at], gb)

    send_grads(2)
    pl.loop(0, 8)(diag_backward)
    take_grads(2)
    send_grads(1)
    pl.loop(0, 8)(far_backward)
    h_copies[0].wait_recv()
    send_heads(4, 1, 0, 2, right)
    h_copies[1].wait_recv()
    send_heads(5, 3, 1, 2, left)
    take_grads(1)
    send_grads(0)
    for h in range(2):
        local_backward(h)

    stores = []

    def store(src, dst):
        stores.append(pltpu.make_async_copy(src, dst, out_sem.at[len(stores)]))
        stores[-1].start()

    store(wg_ref, wg_out)

    @pl.loop(0, 8)
    def _(b):
        cols = cols_of(b)
        both = jnp.concatenate([dqa[h, :, cols].T.astype(BF16) for h in range(2)], axis=1)
        dq_ref[cols] = both.reshape(BLK, 2, 128)

    store(dq_ref, dq_out)
    take_grads(0)

    for b in range(8):
        at = slice(b * BLK, b * BLK + BLK)
        dks, dvs = [], []
        for h in range(2):
            x = xf[h]
            for slot, (c, first, size) in enumerate(LOCAL_PAIRS):
                if first - size <= b < first:
                    x = x + llg[h, slot]
            dk = dka[h, :, at] + mm(x.astype(BF16), vt[h, :, at])
            dv = dva[h, :, at] + mm(x.T.astype(BF16), kt[h, :, at])
            dks.append(dk.T.astype(BF16))
            dvs.append(dv.T.astype(BF16))
        dk_ref[at] = jnp.concatenate(dks, axis=1).reshape(BLK, 2, 128)
        dv_ref[at] = jnp.concatenate(dvs, axis=1).reshape(BLK, 2, 128)

    store(dk_ref, dk_out)
    store(dv_ref, dv_out)

    @pl.loop(0, 4)
    def _(b):
        rows = pl.ds(pl.multiple_of(b * 256, 256), 256)
        acc[rows, :] = mm(hall[0, rows, :], wall[0])

    h_copies[2].wait_recv()
    h_copies[3].wait_recv()

    @pl.loop(0, 4)
    def _(b):
        rows = pl.ds(pl.multiple_of(b * 256, 256), 256)
        acc[rows, :] = acc[rows, :] + mm(hall[1, rows, :], wall[1]) + mm(hall[3, rows, :], wall[3])

    for part in range(2):
        h_copies[4 + part].wait_recv()
        for b in range(2 * part, 2 * part + 2):
            rows = slice(b * 256, b * 256 + 256)
            lo_ref[rows, :] = (acc[rows, :] + mm(hall[2, rows, :], wall[2])).astype(BF16)
            store(lo_ref.at[rows], lo_out.at[rows])

    for group in (w_copies, f_copies, right_msgs, left_msgs, h_copies, b_copies, c_copies):
        for copy in group.values():
            copy.wait_send()
    for copy in stores:
        copy.wait()


def copy_kernel(*refs):
    sources, targets, sems = refs[:5], refs[5:10], refs[10]
    copies = [pltpu.make_async_copy(a, b, sems.at[i]) for i, (a, b) in enumerate(zip(sources, targets))]
    for copy in copies:
        copy.start()
    for copy in copies:
        copy.wait()


def per_device(queries, key_rows, value_rows, level_weights, out_weight, out_grad):
    dma = pltpu.SemaphoreType.DMA
    vmem = pltpu.VMEM
    anywhere = pl.BlockSpec(memory_space=pl.ANY)
    hbm = pl.BlockSpec(memory_space=pltpu.HBM)
    stack = 3 + DEV_BITS
    shape = queries.shape
    shapes = (
        jax.ShapeDtypeStruct(out_grad.shape, BF16),
        jax.ShapeDtypeStruct(shape, BF16),
        jax.ShapeDtypeStruct(shape, BF16),
        jax.ShapeDtypeStruct(shape, BF16),
        jax.ShapeDtypeStruct(level_weights.shape, F32),
    )
    outs = pl.pallas_call(
        kernel,
        out_shape=shapes,
        in_specs=[hbm] * 6,
        out_specs=[anywhere] * 5,
        scratch_shapes=[
            vmem(shape, BF16), vmem(shape, BF16), vmem(shape, BF16),
            vmem(level_weights.shape, F32), vmem(out_grad.shape, BF16),
            vmem(out_grad.shape, BF16),
            vmem(shape, BF16), vmem(shape, BF16), vmem(shape, BF16),
            vmem(level_weights.shape, F32),
            vmem((2, 1024, 128), BF16), vmem((2, 1024, 128), BF16),
            vmem((4, 256, 512), BF16),
            vmem((2, LOCAL_LEVELS + DEV_BITS, 1024), F32),
            vmem((BLK, BLK), jnp.int32),
            vmem((2, 128, 1024), BF16),
            vmem((2, 128, 1024), BF16),
            vmem((2, 128, 1024), BF16),
            vmem((2, 128, 1024), BF16),
            vmem((2, stack, 128, 1024), BF16),
            vmem((2, 8, BLK, BLK), F32),
            vmem((2, 8, BLK, BLK), F32),
            vmem((2, 8, BLK, BLK), BF16),
            vmem((2, 8, 128, 128), F32),
            vmem((2, 7, 128, 128), BF16),
            vmem((2, 7, 128, 128), BF16),
            vmem((2, 128, 1024), F32),
            vmem((3, 2, 128, 128), BF16),
            vmem((7, 2, 128, 128), BF16),
            vmem((5, 2, 128, 128), BF16),
            vmem((7, 2, 128, 128), BF16),
            vmem((2, DEV_BITS * 128, 128), BF16),
            vmem((2, 128, DEV_BITS * 128), BF16),
            vmem((2, DEV_BITS, 128, 128), F32),
            vmem((2, 128, 128), F32),
            vmem((2, 7, 128, 128), F32),
            vmem((2, 2, 128, 512), BF16),
            vmem((2, 2, 128, 512), BF16),
            vmem((2, 2, 128, 512), F32),
            vmem((2, 2, 128, 512), BF16),
            vmem((2, 2, 128, 512), BF16),
            vmem((2, 2, 2, 128, 512), BF16),
            vmem((4, 1024, 256), BF16),
            vmem((2, 128, 1024), F32),
            vmem((2, 128, 1024), F32),
            vmem((2, 128, 1024), F32),
            vmem((1024, 512), F32),
            dma((5,)), dma((8,)), dma,
            dma((3,)), dma((3,)), dma((3,)), dma((3,)),
            dma((7,)), dma((7,)), dma((7,)), dma((7,)),
            dma((12,)), dma((12,)), dma((6,)), dma((6,)),
        ],
        compiler_params=pltpu.CompilerParams(
            collective_id=0, has_side_effects=True, vmem_limit_bytes=40 * 1024 * 1024),
        cost_estimate=pl.CostEstimate(flops=6 * 10**9, bytes_accessed=8 * 2**20, transcendentals=0),
    )(
        *(pltpu.with_memory_space_constraint(x, pltpu.HBM) for x in (
            queries, key_rows, value_rows, level_weights, out_weight.reshape(256, 2048), out_grad)),
    )
    return pl.pallas_call(
        copy_kernel,
        out_shape=shapes,
        in_specs=[anywhere] * 5,
        out_specs=[hbm] * 5,
        scratch_shapes=[dma((5,))],
        compiler_params=pltpu.CompilerParams(vmem_limit_bytes=2 * 1024 * 1024),
        cost_estimate=pl.CostEstimate(flops=0, bytes_accessed=6 * 2**20, transcendentals=0),
    )(*outs)


def solution(mesh):
    in_specs = (
        P("seq", "head", None),
        P("seq", "head", None),
        P("seq", "head", None),
        P(None, "head", "seq"),
        P("head", None, None),
        P("seq", "head"),
    )
    out_specs = (
        P("seq", "head"),
        P("seq", "head", None),
        P("seq", "head", None),
        P("seq", "head", None),
        P(None, "head", "seq"),
    )
    return jax.shard_map(
        per_device, mesh=mesh, in_specs=in_specs, out_specs=out_specs, check_vma=False
    )
```

```python
import functools

import jax
import jax.numpy as jnp
from jax import lax
from jax.experimental import pallas as pl
from jax.experimental.pallas import tpu as pltpu
from jax.sharding import PartitionSpec as P

MESH = pl.DeviceIdType.MESH
F32 = jnp.float32
BF16 = jnp.bfloat16
LEVEL_GAIN = 0.02
BLK = 128
DIAG_LEVELS = 8
DEV_BITS = 5
PHASES = ((0,), (1, 2, 3), (4, 5, 6))
LOCAL_LEVELS = 11


def scale_of(level):
    return LEVEL_GAIN * 2.0 ** (-0.5 * max(level - 1, 0))


LOCAL_PAIRS = [(0, 1, 1), (0, 3, 1), (0, 5, 1), (0, 7, 1), (1, 2, 2), (1, 6, 2), (2, 4, 4)]


def mm(a, b):
    return jnp.dot(a, b, preferred_element_type=F32)


def mm_nt(a, b):
    return lax.dot_general(a, b, (((1,), (1,)), ((), ())), preferred_element_type=F32)


def kernel(
    q_in, k_in, v_in, lw_in, w_hbm, og_in,
    lo_out, dq_out, dk_out, dv_out, wg_out,
    q_ref, k_ref, v_ref, lw_ref, og_ref, lo_ref, dq_ref, dk_ref, dv_ref, wg_ref, kn, vn,
    wall, wsc, lev_ref, qt, kt, vt, gt, wq, st_ref, mix_ref, near, tb, tl, tlt, ot,
    sb, rb, cb, rcb, tst, tstt, lg, xf, llg,
    p2, alone, pf, po, summed, r1, rdir, hall, dqa, dka, dva, acc,
    in_sem, out_sem, own_sem, w_send, w_recv, f_send, f_recv, b_send, b_recv, c_send, c_recv, r_send, r_recv, h_send, h_recv,
):
    me_s = lax.axis_index("seq")
    me_h = lax.axis_index("head")
    core = lax.rem(me_s, 2)
    right, left, across = lax.rem(me_h + 1, 4), lax.rem(me_h + 3, 4), lax.rem(me_h + 2, 4)

    def bit_of(bit):
        return lax.rem(lax.div(me_s, 1 << bit), 2)

    def flipped(bits):
        to = me_s
        for bit in bits:
            to = to + (1 << bit) - (2 << bit) * bit_of(bit)
        return to

    def partner(step):
        if step == 0:
            return flipped([0])
        low, j = (1, step) if step < 4 else (3, step - 3)
        return flipped([low + i for i in range(2) if j >> i & 1])

    def send(src, dst, send_sem, recv_sem, seq, head):
        copy = pltpu.make_async_remote_copy(
            src_ref=src, dst_ref=dst, send_sem=send_sem, recv_sem=recv_sem,
            device_id=(seq, head), device_id_type=MESH,
        )
        copy.start()
        return copy

    loads = []
    for n, (src, dst) in enumerate([(k_in, k_ref), (v_in, v_ref), (lw_in, lw_ref), (q_in, q_ref), (og_in, og_ref)]):
        loads.append(pltpu.make_async_copy(src, dst, in_sem.at[n]))
        loads[n].start()

    barrier = pltpu.get_barrier_semaphore()
    for other in (right, left, across):
        pl.semaphore_signal(barrier, inc=1, device_id=(me_s, other), device_id_type=MESH)
    for step in range(7):
        pl.semaphore_signal(barrier, inc=1, device_id=(partner(step), me_h), device_id_type=MESH)
    pl.semaphore_wait(barrier, 10)

    own = pltpu.make_async_copy(w_hbm.at[:, pl.ds(pl.multiple_of(me_h * 512, 512), 512)], wall.at[0], own_sem)
    half = pl.ds(pl.multiple_of(core * 128, 128), 128)
    w_copies = {}
    for k in (2, 1, 3):
        to = lax.rem(me_h + k, 4)
        w_copies[k] = send(
            w_hbm.at[half, pl.ds(pl.multiple_of(to * 512, 512), 512)], wall.at[k, half],
            w_send.at[k - 1], w_recv.at[k - 1], me_s, to)
    own.start()
    sibling = partner(0)
    f_copies = {}

    def forward_weights(k):
        w_copies[k].wait_recv()
        f_copies[k] = send(wall.at[k, half], wall.at[k, half], f_send.at[k - 1], f_recv.at[k - 1], sibling, me_h)

    row_id = lax.broadcasted_iota(jnp.int32, (BLK, BLK), 0)
    col_id = lax.broadcasted_iota(jnp.int32, (BLK, BLK), 1)
    apart = row_id ^ col_id
    level = jnp.zeros((BLK, BLK), jnp.int32)
    for bit in range(7):
        level = level + ((apart >> bit) > 0).astype(jnp.int32)
    lev_ref[...] = jnp.where(row_id <= col_id, level, -1)

    def cols_of(b):
        return pl.ds(pl.multiple_of(b * BLK, BLK), BLK)

    loads[0].wait()
    loads[1].wait()

    @pl.loop(0, 8, unroll=4)
    def _(b):
        cols = cols_of(b)
        k_all, v_all = k_ref[cols].reshape(BLK, 256), v_ref[cols].reshape(BLK, 256)
        for h in range(2):
            lanes = slice(h * 128, h * 128 + 128)
            kn[h, cols, :] = k_all[:, lanes]
            vn[h, cols, :] = v_all[:, lanes]
            kb, vb = k_all[:, lanes].T, v_all[:, lanes].T
            kt[h, :, cols] = kb
            vt[h, :, cols] = vb
            tb[h, b] = mm_nt(kb, vb)

    total = []
    for h in range(2):
        t = [tb[h, b] for b in range(8)]
        pairs = [t[2 * i] + t[2 * i + 1] for i in range(4)]
        quads = [pairs[0] + pairs[1], pairs[2] + pairs[3]]
        for slot, value in enumerate([t[0], t[2], t[4], t[6], pairs[0], pairs[2], quads[0]]):
            tl[h, slot] = value.astype(BF16)
            tlt[h, slot] = value.T.astype(BF16)
        xf[h] = quads[0] + quads[1]

    b_copies = {}

    def send_states(phase):
        for h in range(2):
            sb[phase, h] = xf[h].astype(BF16)
        for step in PHASES[phase]:
            b_copies[step] = send(sb.at[phase], rb.at[step], b_send.at[step], b_recv.at[step], partner(step), me_h)

    def keep_state(h, slot, value):
        kept = value * bit_of(slot).astype(F32)
        tst[h, slot * 128:slot * 128 + 128, :] = kept.astype(BF16)
        tstt[h, :, slot * 128:slot * 128 + 128] = kept.T.astype(BF16)

    def take_states(phase):
        for step in PHASES[phase]:
            b_copies[step].wait_recv()
        for h in range(2):
            got = [rb[step, h].astype(F32) for step in PHASES[phase]]
            if phase == 0:
                keep_state(h, 0, got[0])
                xf[h] = xf[h] + got[0]
            else:
                far = got[1] + got[2]
                keep_state(h, 2 * phase - 1, got[0])
                keep_state(h, 2 * phase, far)
                xf[h] = xf[h] + got[0] + far

    send_states(0)
    loads[2].wait()
    loads[3].wait()

    for h in range(2):
        for l in range(LOCAL_LEVELS + DEV_BITS):
            wsc[h, l:l + 1, :] = lw_ref[l, h:h + 1, :] * scale_of(l)

    take_states(0)
    send_states(1)

    @pl.loop(0, 8, unroll=4)
    def _(b):
        cols = cols_of(b)
        q_all = q_ref[cols].reshape(BLK, 256)
        for h in range(2):
            qb = q_all[:, h * 128:h * 128 + 128].T
            qt[h, :, cols] = qb
            qf = qb.astype(F32)
            for c in range(3 + DEV_BITS):
                wq[h, c, :, cols] = (qf * wsc[h, DIAG_LEVELS + c:DIAG_LEVELS + c + 1, cols]).astype(BF16)

    right_msgs, left_msgs = {}, {}

    def send_right(i, src, dst):
        right_msgs[i] = send(src, dst, r_send.at[i], r_recv.at[i], me_s, right)

    def send_left(i, src, dst):
        left_msgs[i] = send(src, dst, r_send.at[6 + i], r_recv.at[6 + i], me_s, left)

    def partial_grad(k, u, j):
        rows = slice(u * 512 + j * 256, u * 512 + j * 256 + 256)
        return mm_nt(wall[k], og_ref[rows, :])

    loads[4].wait()
    forward_weights(2)
    started = []

    def first_leg(head, to):
        rows = pl.ds(pl.multiple_of(head * 128, 128), 128)
        for u in range(2):
            p2[head, u] = mm_nt(wall[2, rows, :], og_ref[u * 512:u * 512 + 512, :]).astype(BF16)
            started.append(send(
                p2.at[head, u], r1.at[head, u], r_send.at[6 * head + u], r_recv.at[6 * head + u], me_s, to))

    def await_first(head, u):
        pltpu.make_async_remote_copy(
            src_ref=p2.at[head, u], dst_ref=r1.at[head, u], send_sem=r_send.at[6 * head + u],
            recv_sem=r_recv.at[6 * head + u], device_id=(me_s, left), device_id_type=MESH,
        ).wait_recv()

    first_leg(core, lax.rem(me_h + 1 + 2 * core, 4))
    f_copies[2].wait_recv()
    first_leg(1 - core, lax.rem(me_h + 3 - 2 * core, 4))

    def diag_forward(b):
        cols = cols_of(b)
        for h in range(2):
            lev = lev_ref[...]
            mix = jnp.zeros((BLK, BLK), F32)
            for l in range(DIAG_LEVELS):
                mix = jnp.where(lev == l, wsc[h, l:l + 1, cols], mix)
            scores = mm(kn[h, cols, :], qt[h, :, cols])
            weighted = (mix * scores).astype(BF16)
            st_ref[h, b] = scores
            mix_ref[h, b] = mix
            near[h, b] = weighted
            ot[h, :, cols] = mm(vt[h, :, cols], weighted)

    pl.loop(0, 4, unroll=4)(diag_forward)
    forward_weights(1)
    forward_weights(3)
    take_states(1)
    send_states(2)
    f_copies[1].wait_recv()
    f_copies[3].wait_recv()
    for u in range(2):
        for j in range(2):
            at = slice(j * 256, j * 256 + 256)
            part = partial_grad(3, u, j)
            pf[0, u, :, at] = part[:128]
            alone[0, u, :, at] = part[128:].astype(BF16)
            part = partial_grad(1, u, j)
            alone[1, u, :, at] = part[:128].astype(BF16)
            pf[1, u, :, at] = part[128:]
        send_right(2 + u, alone.at[0, u], rdir.at[0, 1, u])
        send_left(2 + u, alone.at[1, u], rdir.at[1, 0, u])
    pl.loop(4, 8, unroll=4)(diag_forward)

    for h in range(2):
        for slot, (c, first, size) in enumerate(LOCAL_PAIRS):
            at = slice(first * BLK, (first + size) * BLK)
            ot[h, :, at] = ot[h, :, at] + mm(tlt[h, slot], wq[h, c, :, at])

    own.wait()
    for u in range(2):
        for j in range(2):
            at = slice(j * 256, j * 256 + 256)
            part = partial_grad(0, u, j)
            po[0, u, :, at] = part[:128]
            po[1, u, :, at] = part[128:]
    for u in range(2):
        await_first(0, u)
        summed[0, u] = (pf[0, u] + r1[0, u].astype(F32)).astype(BF16)
        send_right(4 + u, summed.at[0, u], rdir.at[0, 0, u])
        await_first(1, u)
        summed[1, u] = (pf[1, u] + r1[1, u].astype(F32)).astype(BF16)
        send_left(4 + u, summed.at[1, u], rdir.at[1, 1, u])

    take_states(2)

    @pl.loop(0, 8, unroll=4)
    def _(b):
        cols = cols_of(b)
        for h in range(2):
            far = mm(tstt[h], wq[h, 3:, :, cols].reshape(DEV_BITS * 128, BLK))
            hall[0, cols, h * 128:h * 128 + 128] = (ot[h, :, cols] + far).T.astype(BF16)

    h_copies = {}

    def send_heads(i, slot, piece, to_slot, head):
        rows = slice(piece * 256, piece * 256 + 256)
        h_copies[i] = send(hall.at[slot, rows], hall.at[to_slot, rows], h_send.at[i], h_recv.at[i], me_s, head)

    for n in range(4):
        send_heads(n, 0, n, 1, right)
        send_heads(6 + n, 0, (n + 2) % 4, 3, left)

    def relay_heads(n):
        h_copies[n].wait_recv()
        send_heads(4 + n, 1, n, 2, right)
        h_copies[6 + n].wait_recv()
        send_heads(10 + n, 3, n + 2, 2, left)

    def take_head_grad(u):
        at = slice(u * 512, u * 512 + 512)
        right_msgs[2 + u].wait_recv()
        left_msgs[2 + u].wait_recv()
        right_msgs[4 + u].wait_recv()
        left_msgs[4 + u].wait_recv()
        for h in range(2):
            gt[h, :, at] = (po[h, u] + rdir[0, h, u].astype(F32) + rdir[1, h, u].astype(F32)).astype(BF16)
        for h in range(2):
            grads = mm_nt(wq[h, 3:, :, at].reshape(DEV_BITS * 128, 512), gt[h, :, at])
            for step in range(DEV_BITS):
                piece = grads[step * 128:step * 128 + 128]
                lg[h, step] = piece if u == 0 else lg[h, step] + piece

    for h in range(2):
        xf[h] = jnp.zeros((128, 128), F32)

    c_copies = {}

    def send_grads(phase):
        for h in range(2):
            if phase == 0:
                cb[0, h] = (xf[h] + lg[h, 0] * bit_of(0).astype(F32)).astype(BF16)
            else:
                for i in range(2):
                    slot = 2 * phase - 1 + i
                    cb[slot, h] = (xf[h] + lg[h, slot] * bit_of(slot).astype(F32)).astype(BF16)
        for n, step in enumerate(PHASES[phase]):
            slot = 2 * phase - 1 + min(n, 1) if phase else 0
            c_copies[step] = send(cb.at[slot], rcb.at[step], c_send.at[step], c_recv.at[step], partner(step), me_h)

    def take_grads(phase):
        for step in PHASES[phase]:
            c_copies[step].wait_recv()
        for h in range(2):
            total_grad = xf[h]
            for step in PHASES[phase]:
                total_grad = total_grad + rcb[step, h].astype(F32)
            xf[h] = total_grad

    def diag_backward(b):
        cols = cols_of(b)
        for h in range(2):
            lev = lev_ref[...]
            gb = gt[h, :, cols]
            grad_scores = mm(vn[h, cols, :], gb)
            weighted = (mix_ref[h, b] * grad_scores).astype(BF16)
            product = grad_scores * st_ref[h, b]
            dqa[h, :, cols] = mm(kt[h, :, cols], weighted)
            dka[h, :, cols] = mm_nt(qt[h, :, cols], weighted)
            dva[h, :, cols] = mm_nt(gb, near[h, b])
            for l in range(DIAG_LEVELS):
                summed_l = jnp.sum(jnp.where(lev == l, product, 0.0), axis=0, keepdims=True)
                wg_ref[l, h:h + 1, cols] = summed_l * scale_of(l)

    def far_backward(b):
        cols = cols_of(b)
        for h in range(2):
            gb = gt[h, :, cols]
            qf = qt[h, :, cols].astype(F32)
            sums = dqa[h, :, cols]
            all_got = mm(tst[h], gb)
            for step in range(DEV_BITS):
                l = LOCAL_LEVELS + step
                got = all_got[step * 128:step * 128 + 128]
                sums = sums + got * wsc[h, l:l + 1, cols]
                wg_ref[l, h:h + 1, cols] = jnp.sum(got * qf, axis=0, keepdims=True) * scale_of(l)
            dqa[h, :, cols] = sums

    def local_backward(h):
        for l in range(DIAG_LEVELS, LOCAL_LEVELS):
            wg_ref[l, h:h + 1, :] = jnp.zeros((1, 1024), F32)
        for slot, (c, first, size) in enumerate(LOCAL_PAIRS):
            at = slice(first * BLK, (first + size) * BLK)
            l = DIAG_LEVELS + c
            gb = gt[h, :, at]
            got = mm(tl[h, slot], gb)
            dqa[h, :, at] = dqa[h, :, at] + got * wsc[h, l:l + 1, at]
            wg_ref[l, h:h + 1, at] = jnp.sum(got * qt[h, :, at].astype(F32), axis=0, keepdims=True) * scale_of(l)
            llg[h, slot] = mm_nt(wq[h, c, :, at], gb)

    take_head_grad(0)
    pl.loop(0, 4, unroll=4)(diag_backward)
    take_head_grad(1)
    send_grads(2)
    pl.loop(0, 4, unroll=4)(far_backward)
    pl.loop(4, 8, unroll=4)(diag_backward)
    relay_heads(0)
    relay_heads(1)
    take_grads(2)
    send_grads(1)
    pl.loop(4, 8, unroll=4)(far_backward)
    for h in range(2):
        local_backward(h)

    stores = []

    def store(src, dst):
        stores.append(pltpu.make_async_copy(src, dst, out_sem.at[len(stores)]))
        stores[-1].start()

    store(wg_ref, wg_out)

    @pl.loop(0, 8, unroll=4)
    def _(b):
        cols = cols_of(b)
        both = jnp.concatenate([dqa[h, :, cols].T.astype(BF16) for h in range(2)], axis=1)
        dq_ref[cols] = both.reshape(BLK, 2, 128)

    store(dq_ref, dq_out)

    @pl.loop(0, 4, unroll=2)
    def _(b):
        rows = pl.ds(pl.multiple_of(b * 256, 256), 256)
        acc[rows, :] = mm(hall[0, rows, :], wall[0])

    take_grads(1)
    send_grads(0)
    for n in (2, 3):
        h_copies[n].wait_recv()
        h_copies[6 + n].wait_recv()

    @pl.loop(0, 4, unroll=2)
    def _(b):
        rows = pl.ds(pl.multiple_of(b * 256, 256), 256)
        acc[rows, :] = acc[rows, :] + mm(hall[1, rows, :], wall[1]) + mm(hall[3, rows, :], wall[3])

    take_grads(0)

    for b in range(8):
        at = slice(b * BLK, b * BLK + BLK)
        dks, dvs = [], []
        for h in range(2):
            x = xf[h]
            for slot, (c, first, size) in enumerate(LOCAL_PAIRS):
                if first - size <= b < first:
                    x = x + llg[h, slot]
            dk = dka[h, :, at] + mm(x.astype(BF16), vt[h, :, at])
            dv = dva[h, :, at] + mm(x.T.astype(BF16), kt[h, :, at])
            dks.append(dk.T.astype(BF16))
            dvs.append(dv.T.astype(BF16))
        dk_ref[at] = jnp.concatenate(dks, axis=1).reshape(BLK, 2, 128)
        dv_ref[at] = jnp.concatenate(dvs, axis=1).reshape(BLK, 2, 128)

    store(dk_ref, dk_out)
    store(dv_ref, dv_out)

    for n in range(2):
        for i, b in ((4 + n, n), (10 + n, n + 2)):
            h_copies[i].wait_recv()
            rows = slice(b * 256, b * 256 + 256)
            lo_ref[rows, :] = (acc[rows, :] + mm(hall[2, rows, :], wall[2])).astype(BF16)
            store(lo_ref.at[rows], lo_out.at[rows])

    for group in (w_copies, f_copies, right_msgs, left_msgs, h_copies, b_copies, c_copies):
        for copy in group.values():
            copy.wait_send()
    for copy in started:
        copy.wait_send()
    for copy in stores:
        copy.wait()


def copy_kernel(*refs):
    sources, targets, sems = refs[:5], refs[5:10], refs[10]
    copies = [pltpu.make_async_copy(a, b, sems.at[i]) for i, (a, b) in enumerate(zip(sources, targets))]
    for copy in copies:
        copy.start()
    for copy in copies:
        copy.wait()


def per_device(queries, key_rows, value_rows, level_weights, out_weight, out_grad):
    dma = pltpu.SemaphoreType.DMA
    vmem = pltpu.VMEM
    anywhere = pl.BlockSpec(memory_space=pl.ANY)
    hbm = pl.BlockSpec(memory_space=pltpu.HBM)
    stack = 3 + DEV_BITS
    shape = queries.shape
    shapes = (
        jax.ShapeDtypeStruct(out_grad.shape, BF16),
        jax.ShapeDtypeStruct(shape, BF16),
        jax.ShapeDtypeStruct(shape, BF16),
        jax.ShapeDtypeStruct(shape, BF16),
        jax.ShapeDtypeStruct(level_weights.shape, F32),
    )
    outs = pl.pallas_call(
        kernel,
        out_shape=shapes,
        in_specs=[hbm] * 6,
        out_specs=[anywhere] * 5,
        scratch_shapes=[
            vmem(shape, BF16), vmem(shape, BF16), vmem(shape, BF16),
            vmem(level_weights.shape, F32), vmem(out_grad.shape, BF16),
            vmem(out_grad.shape, BF16),
            vmem(shape, BF16), vmem(shape, BF16), vmem(shape, BF16),
            vmem(level_weights.shape, F32),
            vmem((2, 1024, 128), BF16), vmem((2, 1024, 128), BF16),
            vmem((4, 256, 512), BF16),
            vmem((2, LOCAL_LEVELS + DEV_BITS, 1024), F32),
            vmem((BLK, BLK), jnp.int32),
            vmem((2, 128, 1024), BF16),
            vmem((2, 128, 1024), BF16),
            vmem((2, 128, 1024), BF16),
            vmem((2, 128, 1024), BF16),
            vmem((2, stack, 128, 1024), BF16),
            vmem((2, 8, BLK, BLK), F32),
            vmem((2, 8, BLK, BLK), F32),
            vmem((2, 8, BLK, BLK), BF16),
            vmem((2, 8, 128, 128), F32),
            vmem((2, 7, 128, 128), BF16),
            vmem((2, 7, 128, 128), BF16),
            vmem((2, 128, 1024), F32),
            vmem((3, 2, 128, 128), BF16),
            vmem((7, 2, 128, 128), BF16),
            vmem((5, 2, 128, 128), BF16),
            vmem((7, 2, 128, 128), BF16),
            vmem((2, DEV_BITS * 128, 128), BF16),
            vmem((2, 128, DEV_BITS * 128), BF16),
            vmem((2, DEV_BITS, 128, 128), F32),
            vmem((2, 128, 128), F32),
            vmem((2, 7, 128, 128), F32),
            vmem((2, 2, 128, 512), BF16),
            vmem((2, 2, 128, 512), BF16),
            vmem((2, 2, 128, 512), F32),
            vmem((2, 2, 128, 512), F32),
            vmem((2, 2, 128, 512), BF16),
            vmem((2, 2, 128, 512), BF16),
            vmem((2, 2, 2, 128, 512), BF16),
            vmem((4, 1024, 256), BF16),
            vmem((2, 128, 1024), F32),
            vmem((2, 128, 1024), F32),
            vmem((2, 128, 1024), F32),
            vmem((1024, 512), F32),
            dma((5,)), dma((8,)), dma,
            dma((3,)), dma((3,)), dma((3,)), dma((3,)),
            dma((7,)), dma((7,)), dma((7,)), dma((7,)),
            dma((12,)), dma((12,)), dma((12,)), dma((12,)),
        ],
        compiler_params=pltpu.CompilerParams(
            collective_id=0, has_side_effects=True, vmem_limit_bytes=40 * 1024 * 1024),
        cost_estimate=pl.CostEstimate(flops=6 * 10**9, bytes_accessed=8 * 2**20, transcendentals=0),
    )(
        *(pltpu.with_memory_space_constraint(x, pltpu.HBM) for x in (
            queries, key_rows, value_rows, level_weights, out_weight.reshape(256, 2048), out_grad)),
    )
    return pl.pallas_call(
        copy_kernel,
        out_shape=shapes,
        in_specs=[anywhere] * 5,
        out_specs=[hbm] * 5,
        scratch_shapes=[dma((5,))],
        compiler_params=pltpu.CompilerParams(vmem_limit_bytes=2 * 1024 * 1024),
        cost_estimate=pl.CostEstimate(flops=0, bytes_accessed=6 * 2**20, transcendentals=0),
    )(*outs)


def solution(mesh):
    in_specs = (
        P("seq", "head", None),
        P("seq", "head", None),
        P("seq", "head", None),
        P(None, "head", "seq"),
        P("head", None, None),
        P("seq", "head"),
    )
    out_specs = (
        P("seq", "head"),
        P("seq", "head", None),
        P("seq", "head", None),
        P("seq", "head", None),
        P(None, "head", "seq"),
    )
    return jax.shard_map(
        per_device, mesh=mesh, in_specs=in_specs, out_specs=out_specs, check_vma=False
    )
```

```python
import functools

import jax
import jax.numpy as jnp
from jax import lax
from jax.experimental import pallas as pl
from jax.experimental.pallas import tpu as pltpu
from jax.sharding import PartitionSpec as P

MESH = pl.DeviceIdType.MESH
F32 = jnp.float32
BF16 = jnp.bfloat16
LEVEL_GAIN = 0.02
BLK = 128
DIAG_LEVELS = 8
DEV_BITS = 5
PHASES = ((0,), (1, 2, 3), (4, 5, 6))
LOCAL_LEVELS = 11


def scale_of(level):
    return LEVEL_GAIN * 2.0 ** (-0.5 * max(level - 1, 0))


LOCAL_PAIRS = [(0, 1, 1), (0, 3, 1), (0, 5, 1), (0, 7, 1), (1, 2, 2), (1, 6, 2), (2, 4, 4)]


def mm(a, b):
    return jnp.dot(a, b, preferred_element_type=F32)


def mm_nt(a, b):
    return lax.dot_general(a, b, (((1,), (1,)), ((), ())), preferred_element_type=F32)


def kernel(
    q_in, k_in, v_in, lw_in, w_hbm, og_in,
    lo_out, dq_out, dk_out, dv_out, wg_out,
    q_ref, k_ref, v_ref, lw_ref, og_ref, lo_ref, dq_ref, dk_ref, dv_ref, wg_ref, kn, vn,
    wall, wsc, lev_ref, qt, kt, vt, gt, wq, st_ref, mix_ref, near, tb, tl, tlt, ot,
    sb, rb, cb, rcb, tst, tstt, lg, xf, llg,
    p2, alone, pf, po, summed, r1, rdir, hall, dqa, dka, dva, acc,
    in_sem, out_sem, own_sem, w_send, w_recv, z_send, z_recv, f_send, f_recv, b_send, b_recv, c_send, c_recv, r_send, r_recv, h_send, h_recv,
):
    me_s = lax.axis_index("seq")
    me_h = lax.axis_index("head")
    core = lax.rem(me_s, 2)
    right, left, across = lax.rem(me_h + 1, 4), lax.rem(me_h + 3, 4), lax.rem(me_h + 2, 4)

    def bit_of(bit):
        return lax.rem(lax.div(me_s, 1 << bit), 2)

    def flipped(bits):
        to = me_s
        for bit in bits:
            to = to + (1 << bit) - (2 << bit) * bit_of(bit)
        return to

    def partner(step):
        if step == 0:
            return flipped([0])
        low, j = (1, step) if step < 4 else (3, step - 3)
        return flipped([low + i for i in range(2) if j >> i & 1])

    def send(src, dst, send_sem, recv_sem, seq, head):
        copy = pltpu.make_async_remote_copy(
            src_ref=src, dst_ref=dst, send_sem=send_sem, recv_sem=recv_sem,
            device_id=(seq, head), device_id_type=MESH,
        )
        copy.start()
        return copy

    loads = []
    for n, (src, dst) in enumerate([(k_in, k_ref), (v_in, v_ref), (lw_in, lw_ref), (q_in, q_ref), (og_in, og_ref)]):
        loads.append(pltpu.make_async_copy(src, dst, in_sem.at[n]))
        loads[n].start()

    barrier = pltpu.get_barrier_semaphore()
    for other in (right, left, across):
        pl.semaphore_signal(barrier, inc=1, device_id=(me_s, other), device_id_type=MESH)
    for step in range(7):
        pl.semaphore_signal(barrier, inc=1, device_id=(partner(step), me_h), device_id_type=MESH)
    pl.semaphore_wait(barrier, 10)

    own = pltpu.make_async_copy(w_hbm.at[:, pl.ds(pl.multiple_of(me_h * 512, 512), 512)], wall.at[0], own_sem)
    def rows_at(start, size):
        return pl.ds(pl.multiple_of(start, 32), size)

    def columns_of(k):
        return pl.ds(pl.multiple_of(lax.rem(me_h + k, 4) * 512, 512), 512)

    half = rows_at(core * 128, 128)
    eighth = rows_at(core * 128 + lax.div(me_s, 8) * 32, 32)
    w_copies = {}

    def send_weights(i, k, rows):
        w_copies[i] = send(
            w_hbm.at[rows, columns_of(k)], wall.at[k, rows], w_send.at[i], w_recv.at[i], me_s, lax.rem(me_h + k, 4))

    send_weights(0, 2, rows_at(core * 128, 64))
    send_weights(2, 1, eighth)
    send_weights(3, 3, eighth)
    send_weights(1, 2, rows_at(core * 128 + 64, 64))
    own.start()
    sibling = partner(0)
    f_copies = {}

    def to_sibling(i, k, rows):
        f_copies[i] = send(wall.at[k, rows], wall.at[k, rows], f_send.at[i], f_recv.at[i], sibling, me_h)

    z_copies = []

    def share_weights():
        for i, k in enumerate((1, 3)):
            w_copies[2 + i].wait_recv()
            for n in range(3):
                at = 3 * i + n
                z_copies.append(send(
                    wall.at[k, eighth], wall.at[k, eighth], z_send.at[at], z_recv.at[at], partner(4 + n), me_h))

    def forward_shared():
        for i, k in enumerate((1, 3)):
            for n in range(3):
                z_copies[3 * i + n].wait_recv()
            to_sibling(2 + i, k, half)

    row_id = lax.broadcasted_iota(jnp.int32, (BLK, BLK), 0)
    col_id = lax.broadcasted_iota(jnp.int32, (BLK, BLK), 1)
    apart = row_id ^ col_id
    level = jnp.zeros((BLK, BLK), jnp.int32)
    for bit in range(7):
        level = level + ((apart >> bit) > 0).astype(jnp.int32)
    lev_ref[...] = jnp.where(row_id <= col_id, level, -1)

    def cols_of(b):
        return pl.ds(pl.multiple_of(b * BLK, BLK), BLK)

    loads[0].wait()
    loads[1].wait()

    @pl.loop(0, 8, unroll=4)
    def _(b):
        cols = cols_of(b)
        k_all, v_all = k_ref[cols].reshape(BLK, 256), v_ref[cols].reshape(BLK, 256)
        for h in range(2):
            lanes = slice(h * 128, h * 128 + 128)
            kn[h, cols, :] = k_all[:, lanes]
            vn[h, cols, :] = v_all[:, lanes]
            kb, vb = k_all[:, lanes].T, v_all[:, lanes].T
            kt[h, :, cols] = kb
            vt[h, :, cols] = vb
            tb[h, b] = mm_nt(kb, vb)

    total = []
    for h in range(2):
        t = [tb[h, b] for b in range(8)]
        pairs = [t[2 * i] + t[2 * i + 1] for i in range(4)]
        quads = [pairs[0] + pairs[1], pairs[2] + pairs[3]]
        for slot, value in enumerate([t[0], t[2], t[4], t[6], pairs[0], pairs[2], quads[0]]):
            tl[h, slot] = value.astype(BF16)
            tlt[h, slot] = value.T.astype(BF16)
        xf[h] = quads[0] + quads[1]

    b_copies = {}

    def send_states(phase):
        for h in range(2):
            sb[phase, h] = xf[h].astype(BF16)
        for step in PHASES[phase]:
            b_copies[step] = send(sb.at[phase], rb.at[step], b_send.at[step], b_recv.at[step], partner(step), me_h)

    def keep_state(h, slot, value):
        kept = value * bit_of(slot).astype(F32)
        tst[h, slot * 128:slot * 128 + 128, :] = kept.astype(BF16)
        tstt[h, :, slot * 128:slot * 128 + 128] = kept.T.astype(BF16)

    def take_states(phase):
        for step in PHASES[phase]:
            b_copies[step].wait_recv()
        for h in range(2):
            got = [rb[step, h].astype(F32) for step in PHASES[phase]]
            if phase == 0:
                keep_state(h, 0, got[0])
                xf[h] = xf[h] + got[0]
            else:
                far = got[1] + got[2]
                keep_state(h, 2 * phase - 1, got[0])
                keep_state(h, 2 * phase, far)
                xf[h] = xf[h] + got[0] + far

    send_states(0)
    loads[2].wait()
    loads[3].wait()

    for h in range(2):
        for l in range(LOCAL_LEVELS + DEV_BITS):
            wsc[h, l:l + 1, :] = lw_ref[l, h:h + 1, :] * scale_of(l)

    take_states(0)
    send_states(1)

    @pl.loop(0, 8, unroll=4)
    def _(b):
        cols = cols_of(b)
        q_all = q_ref[cols].reshape(BLK, 256)
        for h in range(2):
            qb = q_all[:, h * 128:h * 128 + 128].T
            qt[h, :, cols] = qb
            qf = qb.astype(F32)
            for c in range(3 + DEV_BITS):
                wq[h, c, :, cols] = (qf * wsc[h, DIAG_LEVELS + c:DIAG_LEVELS + c + 1, cols]).astype(BF16)

    right_msgs, left_msgs = {}, {}

    def send_right(i, src, dst):
        right_msgs[i] = send(src, dst, r_send.at[i], r_recv.at[i], me_s, right)

    def send_left(i, src, dst):
        left_msgs[i] = send(src, dst, r_send.at[6 + i], r_recv.at[6 + i], me_s, left)

    def partial_grad(k, u, j):
        rows = slice(u * 512 + j * 256, u * 512 + j * 256 + 256)
        return mm_nt(wall[k], og_ref[rows, :])

    share_weights()
    loads[4].wait()
    started = []

    def first_leg(head, r, to):
        rows = rows_at(head * 128 + r * 64, 64)
        for u in range(2):
            at = slice(u * 512, u * 512 + 512)
            p2[head, r, :, at] = mm_nt(wall[2, rows, :], og_ref[at, :]).astype(BF16)
        i = 6 * head + r
        started.append(send(p2.at[head, r], r1.at[head, r], r_send.at[i], r_recv.at[i], me_s, to))

    def await_first(head):
        for r in range(2):
            pltpu.make_async_remote_copy(
                src_ref=p2.at[head, r], dst_ref=r1.at[head, r], send_sem=r_send.at[6 * head + r],
                recv_sem=r_recv.at[6 * head + r], device_id=(me_s, left), device_id_type=MESH,
            ).wait_recv()

    for r in range(2):
        w_copies[r].wait_recv()
        to_sibling(r, 2, rows_at(core * 128 + r * 64, 64))
        first_leg(core, r, lax.rem(me_h + 1 + 2 * core, 4))
    for r in range(2):
        f_copies[r].wait_recv()
        first_leg(1 - core, r, lax.rem(me_h + 3 - 2 * core, 4))

    def diag_forward(b):
        cols = cols_of(b)
        for h in range(2):
            lev = lev_ref[...]
            mix = jnp.zeros((BLK, BLK), F32)
            for l in range(DIAG_LEVELS):
                mix = jnp.where(lev == l, wsc[h, l:l + 1, cols], mix)
            scores = mm(kn[h, cols, :], qt[h, :, cols])
            weighted = (mix * scores).astype(BF16)
            st_ref[h, b] = scores
            mix_ref[h, b] = mix
            near[h, b] = weighted
            ot[h, :, cols] = mm(vt[h, :, cols], weighted)

    pl.loop(0, 4, unroll=4)(diag_forward)
    take_states(1)
    send_states(2)
    forward_shared()

    def second_leg(head, k, to):
        rows = rows_at(head * 128, 128)
        for u in range(2):
            alone[head, u] = mm_nt(wall[k, rows, :], og_ref[u * 512:u * 512 + 512, :]).astype(BF16)
            i = 8 - 6 * head + u
            started.append(send(
                alone.at[head, u], rdir.at[head, head, u], r_send.at[i], r_recv.at[i], me_s, to))

    def await_second(head, u):
        i = 8 - 6 * head + u
        pltpu.make_async_remote_copy(
            src_ref=alone.at[head, u], dst_ref=rdir.at[head, head, u], send_sem=r_send.at[i], recv_sem=r_recv.at[i],
            device_id=(me_s, left), device_id_type=MESH,
        ).wait_recv()

    second_leg(core, 1 + 2 * core, lax.rem(me_h + 3 + 2 * core, 4))
    f_copies[2].wait_recv()
    f_copies[3].wait_recv()
    second_leg(1 - core, 3 - 2 * core, lax.rem(me_h + 1 + 2 * core, 4))
    for u in range(2):
        for head, k in ((0, 3), (1, 1)):
            pf[head, u] = mm_nt(wall[k, head * 128:head * 128 + 128, :], og_ref[u * 512:u * 512 + 512, :])
    pl.loop(4, 8, unroll=4)(diag_forward)

    for h in range(2):
        for slot, (c, first, size) in enumerate(LOCAL_PAIRS):
            at = slice(first * BLK, (first + size) * BLK)
            ot[h, :, at] = ot[h, :, at] + mm(tlt[h, slot], wq[h, c, :, at])

    own.wait()
    for u in range(2):
        for j in range(2):
            at = slice(j * 256, j * 256 + 256)
            part = partial_grad(0, u, j)
            po[0, u, :, at] = part[:128]
            po[1, u, :, at] = part[128:]
    await_first(0)
    await_first(1)
    for u in range(2):
        at = slice(u * 512, u * 512 + 512)
        for head in range(2):
            for r in range(2):
                rows = slice(r * 64, r * 64 + 64)
                summed[head, u, rows, :] = (pf[head, u, rows, :] + r1[head, r, :, at].astype(F32)).astype(BF16)
        send_right(4 + u, summed.at[0, u], rdir.at[1, 0, u])
        send_left(4 + u, summed.at[1, u], rdir.at[0, 1, u])
    take_states(2)

    @pl.loop(0, 8, unroll=4)
    def _(b):
        cols = cols_of(b)
        for h in range(2):
            far = mm(tstt[h], wq[h, 3:, :, cols].reshape(DEV_BITS * 128, BLK))
            hall[0, cols, h * 128:h * 128 + 128] = (ot[h, :, cols] + far).T.astype(BF16)

    h_copies = {}

    def send_heads(i, slot, piece, to_slot, head):
        rows = slice(piece * 256, piece * 256 + 256)
        h_copies[i] = send(hall.at[slot, rows], hall.at[to_slot, rows], h_send.at[i], h_recv.at[i], me_s, head)

    for n in range(4):
        send_heads(n, 0, n, 1, right)
        send_heads(6 + n, 0, (n + 2) % 4, 3, left)

    def relay_heads(n):
        h_copies[n].wait_recv()
        send_heads(4 + n, 1, n, 2, right)
        h_copies[6 + n].wait_recv()
        send_heads(10 + n, 3, n + 2, 2, left)

    def take_head_grad(u):
        at = slice(u * 512, u * 512 + 512)
        await_second(0, u)
        await_second(1, u)
        right_msgs[4 + u].wait_recv()
        left_msgs[4 + u].wait_recv()
        for h in range(2):
            gt[h, :, at] = (po[h, u] + rdir[0, h, u].astype(F32) + rdir[1, h, u].astype(F32)).astype(BF16)
        for h in range(2):
            grads = mm_nt(wq[h, 3:, :, at].reshape(DEV_BITS * 128, 512), gt[h, :, at])
            for step in range(DEV_BITS):
                piece = grads[step * 128:step * 128 + 128]
                lg[h, step] = piece if u == 0 else lg[h, step] + piece

    for h in range(2):
        xf[h] = jnp.zeros((128, 128), F32)

    c_copies = {}

    def send_grads(phase):
        for h in range(2):
            if phase == 0:
                cb[0, h] = (xf[h] + lg[h, 0] * bit_of(0).astype(F32)).astype(BF16)
            else:
                for i in range(2):
                    slot = 2 * phase - 1 + i
                    cb[slot, h] = (xf[h] + lg[h, slot] * bit_of(slot).astype(F32)).astype(BF16)
        for n, step in enumerate(PHASES[phase]):
            slot = 2 * phase - 1 + min(n, 1) if phase else 0
            c_copies[step] = send(cb.at[slot], rcb.at[step], c_send.at[step], c_recv.at[step], partner(step), me_h)

    def take_grads(phase):
        for step in PHASES[phase]:
            c_copies[step].wait_recv()
        for h in range(2):
            total_grad = xf[h]
            for step in PHASES[phase]:
                total_grad = total_grad + rcb[step, h].astype(F32)
            xf[h] = total_grad

    def diag_backward(b):
        cols = cols_of(b)
        for h in range(2):
            lev = lev_ref[...]
            gb = gt[h, :, cols]
            grad_scores = mm(vn[h, cols, :], gb)
            weighted = (mix_ref[h, b] * grad_scores).astype(BF16)
            product = grad_scores * st_ref[h, b]
            dqa[h, :, cols] = mm(kt[h, :, cols], weighted)
            dka[h, :, cols] = mm_nt(qt[h, :, cols], weighted)
            dva[h, :, cols] = mm_nt(gb, near[h, b])
            for l in range(DIAG_LEVELS):
                summed_l = jnp.sum(jnp.where(lev == l, product, 0.0), axis=0, keepdims=True)
                wg_ref[l, h:h + 1, cols] = summed_l * scale_of(l)

    def far_backward(b):
        cols = cols_of(b)
        for h in range(2):
            gb = gt[h, :, cols]
            qf = qt[h, :, cols].astype(F32)
            sums = dqa[h, :, cols]
            all_got = mm(tst[h], gb)
            for step in range(DEV_BITS):
                l = LOCAL_LEVELS + step
                got = all_got[step * 128:step * 128 + 128]
                sums = sums + got * wsc[h, l:l + 1, cols]
                wg_ref[l, h:h + 1, cols] = jnp.sum(got * qf, axis=0, keepdims=True) * scale_of(l)
            dqa[h, :, cols] = sums

    def local_backward(h):
        for l in range(DIAG_LEVELS, LOCAL_LEVELS):
            wg_ref[l, h:h + 1, :] = jnp.zeros((1, 1024), F32)
        for slot, (c, first, size) in enumerate(LOCAL_PAIRS):
            at = slice(first * BLK, (first + size) * BLK)
            l = DIAG_LEVELS + c
            gb = gt[h, :, at]
            got = mm(tl[h, slot], gb)
            dqa[h, :, at] = dqa[h, :, at] + got * wsc[h, l:l + 1, at]
            wg_ref[l, h:h + 1, at] = jnp.sum(got * qt[h, :, at].astype(F32), axis=0, keepdims=True) * scale_of(l)
            llg[h, slot] = mm_nt(wq[h, c, :, at], gb)

    take_head_grad(0)
    pl.loop(0, 4, unroll=4)(diag_backward)
    take_head_grad(1)
    send_grads(2)
    pl.loop(0, 4, unroll=4)(far_backward)
    pl.loop(4, 8, unroll=4)(diag_backward)
    relay_heads(0)
    relay_heads(1)
    take_grads(2)
    send_grads(1)
    pl.loop(4, 8, unroll=4)(far_backward)
    for h in range(2):
        local_backward(h)

    stores = []

    def store(src, dst):
        stores.append(pltpu.make_async_copy(src, dst, out_sem.at[len(stores)]))
        stores[-1].start()

    store(wg_ref, wg_out)

    @pl.loop(0, 8, unroll=4)
    def _(b):
        cols = cols_of(b)
        both = jnp.concatenate([dqa[h, :, cols].T.astype(BF16) for h in range(2)], axis=1)
        dq_ref[cols] = both.reshape(BLK, 2, 128)

    store(dq_ref, dq_out)

    @pl.loop(0, 4, unroll=2)
    def _(b):
        rows = pl.ds(pl.multiple_of(b * 256, 256), 256)
        acc[rows, :] = mm(hall[0, rows, :], wall[0])

    take_grads(1)
    send_grads(0)
    for n in (2, 3):
        h_copies[n].wait_recv()
        h_copies[6 + n].wait_recv()

    @pl.loop(0, 4, unroll=2)
    def _(b):
        rows = pl.ds(pl.multiple_of(b * 256, 256), 256)
        acc[rows, :] = acc[rows, :] + mm(hall[1, rows, :], wall[1]) + mm(hall[3, rows, :], wall[3])

    take_grads(0)

    for b in range(8):
        at = slice(b * BLK, b * BLK + BLK)
        dks, dvs = [], []
        for h in range(2):
            x = xf[h]
            for slot, (c, first, size) in enumerate(LOCAL_PAIRS):
                if first - size <= b < first:
                    x = x + llg[h, slot]
            dk = dka[h, :, at] + mm(x.astype(BF16), vt[h, :, at])
            dv = dva[h, :, at] + mm(x.T.astype(BF16), kt[h, :, at])
            dks.append(dk.T.astype(BF16))
            dvs.append(dv.T.astype(BF16))
        dk_ref[at] = jnp.concatenate(dks, axis=1).reshape(BLK, 2, 128)
        dv_ref[at] = jnp.concatenate(dvs, axis=1).reshape(BLK, 2, 128)

    store(dk_ref, dk_out)
    store(dv_ref, dv_out)

    for n in range(2):
        for i, b in ((4 + n, n), (10 + n, n + 2)):
            h_copies[i].wait_recv()
            rows = slice(b * 256, b * 256 + 256)
            lo_ref[rows, :] = (acc[rows, :] + mm(hall[2, rows, :], wall[2])).astype(BF16)
            store(lo_ref.at[rows], lo_out.at[rows])

    for group in (w_copies, f_copies, dict(enumerate(z_copies)), right_msgs, left_msgs, h_copies, b_copies, c_copies):
        for copy in group.values():
            copy.wait_send()
    for copy in started:
        copy.wait_send()
    for copy in stores:
        copy.wait()


def copy_kernel(*refs):
    sources, targets, sems = refs[:5], refs[5:10], refs[10]
    copies = [pltpu.make_async_copy(a, b, sems.at[i]) for i, (a, b) in enumerate(zip(sources, targets))]
    for copy in copies:
        copy.start()
    for copy in copies:
        copy.wait()


def per_device(queries, key_rows, value_rows, level_weights, out_weight, out_grad):
    dma = pltpu.SemaphoreType.DMA
    vmem = pltpu.VMEM
    anywhere = pl.BlockSpec(memory_space=pl.ANY)
    hbm = pl.BlockSpec(memory_space=pltpu.HBM)
    stack = 3 + DEV_BITS
    shape = queries.shape
    shapes = (
        jax.ShapeDtypeStruct(out_grad.shape, BF16),
        jax.ShapeDtypeStruct(shape, BF16),
        jax.ShapeDtypeStruct(shape, BF16),
        jax.ShapeDtypeStruct(shape, BF16),
        jax.ShapeDtypeStruct(level_weights.shape, F32),
    )
    outs = pl.pallas_call(
        kernel,
        out_shape=shapes,
        in_specs=[hbm] * 6,
        out_specs=[anywhere] * 5,
        scratch_shapes=[
            vmem(shape, BF16), vmem(shape, BF16), vmem(shape, BF16),
            vmem(level_weights.shape, F32), vmem(out_grad.shape, BF16),
            vmem(out_grad.shape, BF16),
            vmem(shape, BF16), vmem(shape, BF16), vmem(shape, BF16),
            vmem(level_weights.shape, F32),
            vmem((2, 1024, 128), BF16), vmem((2, 1024, 128), BF16),
            vmem((4, 256, 512), BF16),
            vmem((2, LOCAL_LEVELS + DEV_BITS, 1024), F32),
            vmem((BLK, BLK), jnp.int32),
            vmem((2, 128, 1024), BF16),
            vmem((2, 128, 1024), BF16),
            vmem((2, 128, 1024), BF16),
            vmem((2, 128, 1024), BF16),
            vmem((2, stack, 128, 1024), BF16),
            vmem((2, 8, BLK, BLK), F32),
            vmem((2, 8, BLK, BLK), F32),
            vmem((2, 8, BLK, BLK), BF16),
            vmem((2, 8, 128, 128), F32),
            vmem((2, 7, 128, 128), BF16),
            vmem((2, 7, 128, 128), BF16),
            vmem((2, 128, 1024), F32),
            vmem((3, 2, 128, 128), BF16),
            vmem((7, 2, 128, 128), BF16),
            vmem((5, 2, 128, 128), BF16),
            vmem((7, 2, 128, 128), BF16),
            vmem((2, DEV_BITS * 128, 128), BF16),
            vmem((2, 128, DEV_BITS * 128), BF16),
            vmem((2, DEV_BITS, 128, 128), F32),
            vmem((2, 128, 128), F32),
            vmem((2, 7, 128, 128), F32),
            vmem((2, 2, 64, 1024), BF16),
            vmem((2, 2, 128, 512), BF16),
            vmem((2, 2, 128, 512), F32),
            vmem((2, 2, 128, 512), F32),
            vmem((2, 2, 128, 512), BF16),
            vmem((2, 2, 64, 1024), BF16),
            vmem((2, 2, 2, 128, 512), BF16),
            vmem((4, 1024, 256), BF16),
            vmem((2, 128, 1024), F32),
            vmem((2, 128, 1024), F32),
            vmem((2, 128, 1024), F32),
            vmem((1024, 512), F32),
            dma((5,)), dma((8,)), dma,
            dma((4,)), dma((4,)), dma((6,)), dma((6,)), dma((4,)), dma((4,)),
            dma((7,)), dma((7,)), dma((7,)), dma((7,)),
            dma((12,)), dma((12,)), dma((12,)), dma((12,)),
        ],
        compiler_params=pltpu.CompilerParams(
            collective_id=0, has_side_effects=True, vmem_limit_bytes=40 * 1024 * 1024),
        cost_estimate=pl.CostEstimate(flops=6 * 10**9, bytes_accessed=8 * 2**20, transcendentals=0),
    )(
        *(pltpu.with_memory_space_constraint(x, pltpu.HBM) for x in (
            queries, key_rows, value_rows, level_weights, out_weight.reshape(256, 2048), out_grad)),
    )
    return pl.pallas_call(
        copy_kernel,
        out_shape=shapes,
        in_specs=[anywhere] * 5,
        out_specs=[hbm] * 5,
        scratch_shapes=[dma((5,))],
        compiler_params=pltpu.CompilerParams(vmem_limit_bytes=2 * 1024 * 1024),
        cost_estimate=pl.CostEstimate(flops=0, bytes_accessed=6 * 2**20, transcendentals=0),
    )(*outs)


def solution(mesh):
    in_specs = (
        P("seq", "head", None),
        P("seq", "head", None),
        P("seq", "head", None),
        P(None, "head", "seq"),
        P("head", None, None),
        P("seq", "head"),
    )
    out_specs = (
        P("seq", "head"),
        P("seq", "head", None),
        P("seq", "head", None),
        P("seq", "head", None),
        P(None, "head", "seq"),
    )
    return jax.shard_map(
        per_device, mesh=mesh, in_specs=in_specs, out_specs=out_specs, check_vma=False
    )
```

```python
import functools

import jax
import jax.numpy as jnp
from jax import lax
from jax.experimental import pallas as pl
from jax.experimental.pallas import tpu as pltpu
from jax.sharding import PartitionSpec as P

MESH = pl.DeviceIdType.MESH
F32 = jnp.float32
BF16 = jnp.bfloat16
LEVEL_GAIN = 0.02
BLK = 128
DIAG_LEVELS = 8
DEV_BITS = 5
PHASES = ((0,), (1, 2, 3), (4, 5, 6))
LOCAL_LEVELS = 11


def scale_of(level):
    return LEVEL_GAIN * 2.0 ** (-0.5 * max(level - 1, 0))


LOCAL_PAIRS = [(0, 1, 1), (0, 3, 1), (0, 5, 1), (0, 7, 1), (1, 2, 2), (1, 6, 2), (2, 4, 4)]


def mm(a, b):
    return jnp.dot(a, b, preferred_element_type=F32)


def mm_nt(a, b):
    return lax.dot_general(a, b, (((1,), (1,)), ((), ())), preferred_element_type=F32)


def kernel(
    q_in, k_in, v_in, lw_in, w_hbm, og_in,
    lo_out, dq_out, dk_out, dv_out, wg_out,
    q_ref, k_ref, v_ref, lw_ref, og_ref, lo_ref, dq_ref, dk_ref, dv_ref, wg_ref, kn, vn,
    wall, wsc, lev_ref, qt, kt, vt, gt, wq, st_ref, mix_ref, near, tb, tl, tlt, ot,
    sb, rb, cb, rcb, tst, tstt, lg, xf, llg,
    p2, alone, pf, po, summed, r1, ra, rb_sum, hall, dqa, dka, dva, acc,
    in_sem, out_sem, own_sem, w_send, w_recv, z_send, z_recv, f_send, f_recv, b_send, b_recv, c_send, c_recv, a_send, a_recv, r_send, r_recv, h_send, h_recv,
):
    me_s = lax.axis_index("seq")
    me_h = lax.axis_index("head")
    core = lax.rem(me_s, 2)
    right, left, across = lax.rem(me_h + 1, 4), lax.rem(me_h + 3, 4), lax.rem(me_h + 2, 4)

    def bit_of(bit):
        return lax.rem(lax.div(me_s, 1 << bit), 2)

    def flipped(bits):
        to = me_s
        for bit in bits:
            to = to + (1 << bit) - (2 << bit) * bit_of(bit)
        return to

    def partner(step):
        if step == 0:
            return flipped([0])
        low, j = (1, step) if step < 4 else (3, step - 3)
        return flipped([low + i for i in range(2) if j >> i & 1])

    def send(src, dst, send_sem, recv_sem, seq, head):
        copy = pltpu.make_async_remote_copy(
            src_ref=src, dst_ref=dst, send_sem=send_sem, recv_sem=recv_sem,
            device_id=(seq, head), device_id_type=MESH,
        )
        copy.start()
        return copy

    loads = []
    for n, (src, dst) in enumerate([(k_in, k_ref), (v_in, v_ref), (lw_in, lw_ref), (q_in, q_ref), (og_in, og_ref)]):
        loads.append(pltpu.make_async_copy(src, dst, in_sem.at[n]))
        loads[n].start()

    barrier = pltpu.get_barrier_semaphore()
    for other in (right, left, across):
        pl.semaphore_signal(barrier, inc=1, device_id=(me_s, other), device_id_type=MESH)
    for step in range(7):
        pl.semaphore_signal(barrier, inc=1, device_id=(partner(step), me_h), device_id_type=MESH)
    pl.semaphore_wait(barrier, 10)

    own = pltpu.make_async_copy(w_hbm.at[:, pl.ds(pl.multiple_of(me_h * 512, 512), 512)], wall.at[0], own_sem)
    def rows_at(start, size):
        return pl.ds(pl.multiple_of(start, 32), size)

    def columns_of(k):
        return pl.ds(pl.multiple_of(lax.rem(me_h + k, 4) * 512, 512), 512)

    half = rows_at(core * 128, 128)
    eighth = rows_at(core * 128 + lax.div(me_s, 8) * 32, 32)
    w_copies = {}

    def send_weights(i, k, rows):
        w_copies[i] = send(
            w_hbm.at[rows, columns_of(k)], wall.at[k, rows], w_send.at[i], w_recv.at[i], me_s, lax.rem(me_h + k, 4))

    direct, shared = 1 + 2 * core, (2, 3 - 2 * core)
    send_weights(0, direct, rows_at(core * 128, 64))
    send_weights(2, shared[0], eighth)
    send_weights(3, shared[1], eighth)
    send_weights(1, direct, rows_at(core * 128 + 64, 64))
    own.start()
    sibling = partner(0)
    f_copies = {}

    def to_sibling(i, k, rows):
        f_copies[i] = send(wall.at[k, rows], wall.at[k, rows], f_send.at[i], f_recv.at[i], sibling, me_h)

    z_copies = []

    def share_weights():
        for i, k in enumerate(shared):
            w_copies[2 + i].wait_recv()
            for n in range(3):
                at = 3 * i + n
                z_copies.append(send(
                    wall.at[k, eighth], wall.at[k, eighth], z_send.at[at], z_recv.at[at], partner(4 + n), me_h))

    def forward_shared(i):
        for n in range(3):
            z_copies[3 * i + n].wait_recv()
        to_sibling(2 + i, shared[i], half)

    row_id = lax.broadcasted_iota(jnp.int32, (BLK, BLK), 0)
    col_id = lax.broadcasted_iota(jnp.int32, (BLK, BLK), 1)
    apart = row_id ^ col_id
    level = jnp.zeros((BLK, BLK), jnp.int32)
    for bit in range(7):
        level = level + ((apart >> bit) > 0).astype(jnp.int32)
    lev_ref[...] = jnp.where(row_id <= col_id, level, -1)

    def cols_of(b):
        return pl.ds(pl.multiple_of(b * BLK, BLK), BLK)

    loads[0].wait()
    loads[1].wait()

    @pl.loop(0, 8, unroll=4)
    def _(b):
        cols = cols_of(b)
        k_all, v_all = k_ref[cols].reshape(BLK, 256), v_ref[cols].reshape(BLK, 256)
        for h in range(2):
            lanes = slice(h * 128, h * 128 + 128)
            kn[h, cols, :] = k_all[:, lanes]
            vn[h, cols, :] = v_all[:, lanes]
            kb, vb = k_all[:, lanes].T, v_all[:, lanes].T
            kt[h, :, cols] = kb
            vt[h, :, cols] = vb
            tb[h, b] = mm_nt(kb, vb)

    total = []
    for h in range(2):
        t = [tb[h, b] for b in range(8)]
        pairs = [t[2 * i] + t[2 * i + 1] for i in range(4)]
        quads = [pairs[0] + pairs[1], pairs[2] + pairs[3]]
        for slot, value in enumerate([t[0], t[2], t[4], t[6], pairs[0], pairs[2], quads[0]]):
            tl[h, slot] = value.astype(BF16)
            tlt[h, slot] = value.T.astype(BF16)
        xf[h] = quads[0] + quads[1]

    b_copies = {}

    def send_states(phase):
        for h in range(2):
            sb[phase, h] = xf[h].astype(BF16)
        for step in PHASES[phase]:
            b_copies[step] = send(sb.at[phase], rb.at[step], b_send.at[step], b_recv.at[step], partner(step), me_h)

    def keep_state(h, slot, value):
        kept = value * bit_of(slot).astype(F32)
        tst[h, slot * 128:slot * 128 + 128, :] = kept.astype(BF16)
        tstt[h, :, slot * 128:slot * 128 + 128] = kept.T.astype(BF16)

    def take_states(phase):
        for step in PHASES[phase]:
            b_copies[step].wait_recv()
        for h in range(2):
            got = [rb[step, h].astype(F32) for step in PHASES[phase]]
            if phase == 0:
                keep_state(h, 0, got[0])
                xf[h] = xf[h] + got[0]
            else:
                far = got[1] + got[2]
                keep_state(h, 2 * phase - 1, got[0])
                keep_state(h, 2 * phase, far)
                xf[h] = xf[h] + got[0] + far

    send_states(0)
    loads[2].wait()
    loads[3].wait()

    for h in range(2):
        for l in range(LOCAL_LEVELS + DEV_BITS):
            wsc[h, l:l + 1, :] = lw_ref[l, h:h + 1, :] * scale_of(l)

    take_states(0)
    send_states(1)

    @pl.loop(0, 8, unroll=4)
    def _(b):
        cols = cols_of(b)
        q_all = q_ref[cols].reshape(BLK, 256)
        for h in range(2):
            qb = q_all[:, h * 128:h * 128 + 128].T
            qt[h, :, cols] = qb
            qf = qb.astype(F32)
            for c in range(3 + DEV_BITS):
                wq[h, c, :, cols] = (qf * wsc[h, DIAG_LEVELS + c:DIAG_LEVELS + c + 1, cols]).astype(BF16)

    right_msgs, left_msgs = {}, {}

    def send_right(i, src, dst):
        right_msgs[i] = send(src, dst, r_send.at[2 + i], r_recv.at[2 + i], me_s, right)

    def send_left(i, src, dst):
        left_msgs[i] = send(src, dst, r_send.at[6 + i], r_recv.at[6 + i], me_s, left)

    def partial_grad(k, u, j):
        rows = slice(u * 512 + j * 256, u * 512 + j * 256 + 256)
        return mm_nt(wall[k], og_ref[rows, :])

    loads[4].wait()
    started = []

    def straight_leg(head, k, r, to):
        rows = rows_at(head * 128 + r * 64, 64)
        for u in range(2):
            alone[head, r, u] = mm_nt(wall[k, rows, :], og_ref[u * 512:u * 512 + 512, :]).astype(BF16)
            i = 4 * head + 2 * r + u
            started.append(send(alone.at[head, r, u], ra.at[head, r, u], a_send.at[i], a_recv.at[i], me_s, to))

    def await_straight(head, u):
        for r in range(2):
            i = 4 * head + 2 * r + u
            pltpu.make_async_remote_copy(
                src_ref=alone.at[head, r, u], dst_ref=ra.at[head, r, u], send_sem=a_send.at[i], recv_sem=a_recv.at[i],
                device_id=(me_s, left), device_id_type=MESH,
            ).wait_recv()

    for r in range(2):
        w_copies[r].wait_recv()
        to_sibling(r, direct, rows_at(core * 128 + r * 64, 64))
        straight_leg(core, direct, r, lax.rem(me_h + 3 + 2 * core, 4))
        if r == 0:
            share_weights()
    for r in range(2):
        f_copies[r].wait_recv()
        straight_leg(1 - core, 3 - 2 * core, r, lax.rem(me_h + 1 + 2 * core, 4))

    def diag_forward(b):
        cols = cols_of(b)
        for h in range(2):
            lev = lev_ref[...]
            mix = jnp.zeros((BLK, BLK), F32)
            for l in range(DIAG_LEVELS):
                mix = jnp.where(lev == l, wsc[h, l:l + 1, cols], mix)
            scores = mm(kn[h, cols, :], qt[h, :, cols])
            weighted = (mix * scores).astype(BF16)
            st_ref[h, b] = scores
            mix_ref[h, b] = mix
            near[h, b] = weighted
            ot[h, :, cols] = mm(vt[h, :, cols], weighted)

    pl.loop(0, 4, unroll=4)(diag_forward)
    take_states(1)
    send_states(2)
    forward_shared(0)

    def relay_leg(head, u, to):
        rows = rows_at(head * 128, 128)
        p2[head, u] = mm_nt(wall[2, rows, :], og_ref[u * 512:u * 512 + 512, :]).astype(BF16)
        i = 4 * head + u
        started.append(send(p2.at[head, u], r1.at[head, u], r_send.at[i], r_recv.at[i], me_s, to))

    def await_relay(head, u):
        i = 4 * head + u
        pltpu.make_async_remote_copy(
            src_ref=p2.at[head, u], dst_ref=r1.at[head, u], send_sem=r_send.at[i], recv_sem=r_recv.at[i],
            device_id=(me_s, left), device_id_type=MESH,
        ).wait_recv()

    for u in range(2):
        relay_leg(core, u, lax.rem(me_h + 1 + 2 * core, 4))
        if u == 0:
            f_copies[2].wait_recv()
            forward_shared(1)
        relay_leg(1 - core, u, lax.rem(me_h + 3 - 2 * core, 4))
    f_copies[3].wait_recv()
    for u in range(2):
        for head, k in ((0, 3), (1, 1)):
            pf[head, u] = mm_nt(wall[k, head * 128:head * 128 + 128, :], og_ref[u * 512:u * 512 + 512, :])
    pl.loop(4, 8, unroll=4)(diag_forward)

    for h in range(2):
        for slot, (c, first, size) in enumerate(LOCAL_PAIRS):
            at = slice(first * BLK, (first + size) * BLK)
            ot[h, :, at] = ot[h, :, at] + mm(tlt[h, slot], wq[h, c, :, at])

    own.wait()
    for u in range(2):
        for j in range(2):
            at = slice(j * 256, j * 256 + 256)
            part = partial_grad(0, u, j)
            po[0, u, :, at] = part[:128]
            po[1, u, :, at] = part[128:]
    for u in range(2):
        await_relay(0, u)
        summed[0, u] = (pf[0, u] + r1[0, u].astype(F32)).astype(BF16)
        send_right(u, summed.at[0, u], rb_sum.at[0, u])
        await_relay(1, u)
        summed[1, u] = (pf[1, u] + r1[1, u].astype(F32)).astype(BF16)
        send_left(u, summed.at[1, u], rb_sum.at[1, u])
    take_states(2)

    @pl.loop(0, 8, unroll=4)
    def _(b):
        cols = cols_of(b)
        for h in range(2):
            far = mm(tstt[h], wq[h, 3:, :, cols].reshape(DEV_BITS * 128, BLK))
            hall[0, cols, h * 128:h * 128 + 128] = (ot[h, :, cols] + far).T.astype(BF16)

    h_copies = {}

    def send_heads(i, slot, start, size, to_slot, head):
        rows = slice(start, start + size)
        h_copies[i] = send(hall.at[slot, rows], hall.at[to_slot, rows], h_send.at[i], h_recv.at[i], me_s, head)

    for n in range(4):
        send_heads(n, 0, n * 256, 256, 1, right)
        send_heads(8 + n, 0, (n + 2) % 4 * 256, 256, 3, left)

    def relay_heads(n):
        h_copies[n].wait_recv()
        for half_piece in range(2):
            send_heads(4 + 2 * n + half_piece, 1, n * 256 + half_piece * 128, 128, 2, right)
        h_copies[8 + n].wait_recv()
        for half_piece in range(2):
            send_heads(12 + 2 * n + half_piece, 3, 512 + n * 256 + half_piece * 128, 128, 2, left)

    def take_head_grad(u):
        at = slice(u * 512, u * 512 + 512)
        await_straight(0, u)
        await_straight(1, u)
        right_msgs[u].wait_recv()
        left_msgs[u].wait_recv()
        for h in range(2):
            for r in range(2):
                rows = slice(r * 64, r * 64 + 64)
                gt[h, rows, at] = (
                    po[h, u, rows, :] + ra[h, r, u].astype(F32) + rb_sum[h, u, rows, :].astype(F32)).astype(BF16)
        for h in range(2):
            grads = mm_nt(wq[h, 3:, :, at].reshape(DEV_BITS * 128, 512), gt[h, :, at])
            for step in range(DEV_BITS):
                piece = grads[step * 128:step * 128 + 128]
                lg[h, step] = piece if u == 0 else lg[h, step] + piece

    for h in range(2):
        xf[h] = jnp.zeros((128, 128), F32)

    c_copies = {}

    def send_grads(phase):
        for h in range(2):
            if phase == 0:
                cb[0, h] = (xf[h] + lg[h, 0] * bit_of(0).astype(F32)).astype(BF16)
            else:
                for i in range(2):
                    slot = 2 * phase - 1 + i
                    cb[slot, h] = (xf[h] + lg[h, slot] * bit_of(slot).astype(F32)).astype(BF16)
        for n, step in enumerate(PHASES[phase]):
            slot = 2 * phase - 1 + min(n, 1) if phase else 0
            c_copies[step] = send(cb.at[slot], rcb.at[step], c_send.at[step], c_recv.at[step], partner(step), me_h)

    def take_grads(phase):
        for step in PHASES[phase]:
            c_copies[step].wait_recv()
        for h in range(2):
            total_grad = xf[h]
            for step in PHASES[phase]:
                total_grad = total_grad + rcb[step, h].astype(F32)
            xf[h] = total_grad

    def diag_backward(b):
        cols = cols_of(b)
        for h in range(2):
            lev = lev_ref[...]
            gb = gt[h, :, cols]
            grad_scores = mm(vn[h, cols, :], gb)
            weighted = (mix_ref[h, b] * grad_scores).astype(BF16)
            product = grad_scores * st_ref[h, b]
            dqa[h, :, cols] = mm(kt[h, :, cols], weighted)
            dka[h, :, cols] = mm_nt(qt[h, :, cols], weighted)
            dva[h, :, cols] = mm_nt(gb, near[h, b])
            for l in range(DIAG_LEVELS):
                summed_l = jnp.sum(jnp.where(lev == l, product, 0.0), axis=0, keepdims=True)
                wg_ref[l, h:h + 1, cols] = summed_l * scale_of(l)

    def far_backward(b):
        cols = cols_of(b)
        for h in range(2):
            gb = gt[h, :, cols]
            qf = qt[h, :, cols].astype(F32)
            sums = dqa[h, :, cols]
            all_got = mm(tst[h], gb)
            for step in range(DEV_BITS):
                l = LOCAL_LEVELS + step
                got = all_got[step * 128:step * 128 + 128]
                sums = sums + got * wsc[h, l:l + 1, cols]
                wg_ref[l, h:h + 1, cols] = jnp.sum(got * qf, axis=0, keepdims=True) * scale_of(l)
            dqa[h, :, cols] = sums

    def local_backward(h):
        for l in range(DIAG_LEVELS, LOCAL_LEVELS):
            wg_ref[l, h:h + 1, :] = jnp.zeros((1, 1024), F32)
        for slot, (c, first, size) in enumerate(LOCAL_PAIRS):
            at = slice(first * BLK, (first + size) * BLK)
            l = DIAG_LEVELS + c
            gb = gt[h, :, at]
            got = mm(tl[h, slot], gb)
            dqa[h, :, at] = dqa[h, :, at] + got * wsc[h, l:l + 1, at]
            wg_ref[l, h:h + 1, at] = jnp.sum(got * qt[h, :, at].astype(F32), axis=0, keepdims=True) * scale_of(l)
            llg[h, slot] = mm_nt(wq[h, c, :, at], gb)

    take_head_grad(0)
    pl.loop(0, 4, unroll=4)(diag_backward)
    take_head_grad(1)
    send_grads(2)
    pl.loop(0, 4, unroll=4)(far_backward)
    pl.loop(4, 8, unroll=4)(diag_backward)
    relay_heads(0)
    relay_heads(1)
    take_grads(2)
    send_grads(1)
    pl.loop(4, 8, unroll=4)(far_backward)
    for h in range(2):
        local_backward(h)

    stores = []

    def store(src, dst):
        stores.append(pltpu.make_async_copy(src, dst, out_sem.at[len(stores)]))
        stores[-1].start()

    store(wg_ref, wg_out)

    @pl.loop(0, 8, unroll=4)
    def _(b):
        cols = cols_of(b)
        both = jnp.concatenate([dqa[h, :, cols].T.astype(BF16) for h in range(2)], axis=1)
        dq_ref[cols] = both.reshape(BLK, 2, 128)

    store(dq_ref, dq_out)

    @pl.loop(0, 4, unroll=2)
    def _(b):
        rows = pl.ds(pl.multiple_of(b * 256, 256), 256)
        acc[rows, :] = mm(hall[0, rows, :], wall[0])

    take_grads(1)
    send_grads(0)
    for n in (2, 3):
        h_copies[n].wait_recv()
        h_copies[8 + n].wait_recv()

    @pl.loop(0, 4, unroll=2)
    def _(b):
        rows = pl.ds(pl.multiple_of(b * 256, 256), 256)
        acc[rows, :] = acc[rows, :] + mm(hall[1, rows, :], wall[1]) + mm(hall[3, rows, :], wall[3])

    take_grads(0)

    for b in range(8):
        at = slice(b * BLK, b * BLK + BLK)
        dks, dvs = [], []
        for h in range(2):
            x = xf[h]
            for slot, (c, first, size) in enumerate(LOCAL_PAIRS):
                if first - size <= b < first:
                    x = x + llg[h, slot]
            dk = dka[h, :, at] + mm(x.astype(BF16), vt[h, :, at])
            dv = dva[h, :, at] + mm(x.T.astype(BF16), kt[h, :, at])
            dks.append(dk.T.astype(BF16))
            dvs.append(dv.T.astype(BF16))
        dk_ref[at] = jnp.concatenate(dks, axis=1).reshape(BLK, 2, 128)
        dv_ref[at] = jnp.concatenate(dvs, axis=1).reshape(BLK, 2, 128)

    store(dk_ref, dk_out)
    store(dv_ref, dv_out)

    for n in range(4):
        for i, b in ((4 + n, n), (12 + n, n + 4)):
            h_copies[i].wait_recv()
            rows = slice(b * 128, b * 128 + 128)
            lo_ref[rows, :] = (acc[rows, :] + mm(hall[2, rows, :], wall[2])).astype(BF16)
            store(lo_ref.at[rows], lo_out.at[rows])

    for group in (w_copies, f_copies, dict(enumerate(z_copies)), right_msgs, left_msgs, h_copies, b_copies, c_copies):
        for copy in group.values():
            copy.wait_send()
    for copy in started:
        copy.wait_send()
    for copy in stores:
        copy.wait()


def copy_kernel(*refs):
    sources, targets, sems = refs[:5], refs[5:10], refs[10]
    copies = [pltpu.make_async_copy(a, b, sems.at[i]) for i, (a, b) in enumerate(zip(sources, targets))]
    for copy in copies:
        copy.start()
    for copy in copies:
        copy.wait()


def per_device(queries, key_rows, value_rows, level_weights, out_weight, out_grad):
    dma = pltpu.SemaphoreType.DMA
    vmem = pltpu.VMEM
    anywhere = pl.BlockSpec(memory_space=pl.ANY)
    hbm = pl.BlockSpec(memory_space=pltpu.HBM)
    stack = 3 + DEV_BITS
    shape = queries.shape
    shapes = (
        jax.ShapeDtypeStruct(out_grad.shape, BF16),
        jax.ShapeDtypeStruct(shape, BF16),
        jax.ShapeDtypeStruct(shape, BF16),
        jax.ShapeDtypeStruct(shape, BF16),
        jax.ShapeDtypeStruct(level_weights.shape, F32),
    )
    outs = pl.pallas_call(
        kernel,
        out_shape=shapes,
        in_specs=[hbm] * 6,
        out_specs=[anywhere] * 5,
        scratch_shapes=[
            vmem(shape, BF16), vmem(shape, BF16), vmem(shape, BF16),
            vmem(level_weights.shape, F32), vmem(out_grad.shape, BF16),
            vmem(out_grad.shape, BF16),
            vmem(shape, BF16), vmem(shape, BF16), vmem(shape, BF16),
            vmem(level_weights.shape, F32),
            vmem((2, 1024, 128), BF16), vmem((2, 1024, 128), BF16),
            vmem((4, 256, 512), BF16),
            vmem((2, LOCAL_LEVELS + DEV_BITS, 1024), F32),
            vmem((BLK, BLK), jnp.int32),
            vmem((2, 128, 1024), BF16),
            vmem((2, 128, 1024), BF16),
            vmem((2, 128, 1024), BF16),
            vmem((2, 128, 1024), BF16),
            vmem((2, stack, 128, 1024), BF16),
            vmem((2, 8, BLK, BLK), F32),
            vmem((2, 8, BLK, BLK), F32),
            vmem((2, 8, BLK, BLK), BF16),
            vmem((2, 8, 128, 128), F32),
            vmem((2, 7, 128, 128), BF16),
            vmem((2, 7, 128, 128), BF16),
            vmem((2, 128, 1024), F32),
            vmem((3, 2, 128, 128), BF16),
            vmem((7, 2, 128, 128), BF16),
            vmem((5, 2, 128, 128), BF16),
            vmem((7, 2, 128, 128), BF16),
            vmem((2, DEV_BITS * 128, 128), BF16),
            vmem((2, 128, DEV_BITS * 128), BF16),
            vmem((2, DEV_BITS, 128, 128), F32),
            vmem((2, 128, 128), F32),
            vmem((2, 7, 128, 128), F32),
            vmem((2, 2, 128, 512), BF16),
            vmem((2, 2, 2, 64, 512), BF16),
            vmem((2, 2, 128, 512), F32),
            vmem((2, 2, 128, 512), F32),
            vmem((2, 2, 128, 512), BF16),
            vmem((2, 2, 128, 512), BF16),
            vmem((2, 2, 2, 64, 512), BF16),
            vmem((2, 2, 128, 512), BF16),
            vmem((4, 1024, 256), BF16),
            vmem((2, 128, 1024), F32),
            vmem((2, 128, 1024), F32),
            vmem((2, 128, 1024), F32),
            vmem((1024, 512), F32),
            dma((5,)), dma((12,)), dma,
            dma((4,)), dma((4,)), dma((6,)), dma((6,)), dma((4,)), dma((4,)),
            dma((7,)), dma((7,)), dma((7,)), dma((7,)),
            dma((8,)), dma((8,)), dma((8,)), dma((8,)), dma((16,)), dma((16,)),
        ],
        compiler_params=pltpu.CompilerParams(
            collective_id=0, has_side_effects=True, vmem_limit_bytes=40 * 1024 * 1024),
        cost_estimate=pl.CostEstimate(flops=6 * 10**9, bytes_accessed=8 * 2**20, transcendentals=0),
    )(
        *(pltpu.with_memory_space_constraint(x, pltpu.HBM) for x in (
            queries, key_rows, value_rows, level_weights, out_weight.reshape(256, 2048), out_grad)),
    )
    return pl.pallas_call(
        copy_kernel,
        out_shape=shapes,
        in_specs=[anywhere] * 5,
        out_specs=[hbm] * 5,
        scratch_shapes=[dma((5,))],
        compiler_params=pltpu.CompilerParams(vmem_limit_bytes=2 * 1024 * 1024),
        cost_estimate=pl.CostEstimate(flops=0, bytes_accessed=6 * 2**20, transcendentals=0),
    )(*outs)


def solution(mesh):
    in_specs = (
        P("seq", "head", None),
        P("seq", "head", None),
        P("seq", "head", None),
        P(None, "head", "seq"),
        P("head", None, None),
        P("seq", "head"),
    )
    out_specs = (
        P("seq", "head"),
        P("seq", "head", None),
        P("seq", "head", None),
        P("seq", "head", None),
        P(None, "head", "seq"),
    )
    return jax.shard_map(
        per_device, mesh=mesh, in_specs=in_specs, out_specs=out_specs, check_vma=False
    )
```

```python
import functools

import jax
import jax.numpy as jnp
from jax import lax
from jax.experimental import pallas as pl
from jax.experimental.pallas import tpu as pltpu
from jax.sharding import PartitionSpec as P

MESH = pl.DeviceIdType.MESH
F32 = jnp.float32
BF16 = jnp.bfloat16
LEVEL_GAIN = 0.02
BLK = 128
DIAG_LEVELS = 8
DEV_BITS = 5
PHASES = ((0,), (1, 2, 3), (4, 5, 6))
LOCAL_LEVELS = 11


def scale_of(level):
    return LEVEL_GAIN * 2.0 ** (-0.5 * max(level - 1, 0))


LOCAL_PAIRS = [(0, 1, 1), (0, 3, 1), (0, 5, 1), (0, 7, 1), (1, 2, 2), (1, 6, 2), (2, 4, 4)]


def mm(a, b):
    return jnp.dot(a, b, preferred_element_type=F32)


def mm_nt(a, b):
    return lax.dot_general(a, b, (((1,), (1,)), ((), ())), preferred_element_type=F32)


def kernel(
    q_in, k_in, v_in, lw_in, w_hbm, og_in,
    lo_out, dq_out, dk_out, dv_out, wg_out,
    q_ref, k_ref, v_ref, lw_ref, og_ref, lo_ref, dq_ref, dk_ref, dv_ref, wg_ref, kn, vn,
    wall, wsc, lev_ref, qt, kt, vt, gt, wq, st_ref, mix_ref, near, tb, tl, tlt, ot,
    sb, rb, cb, rcb, cs, cr, dkn, dvn, tst, tstt, lg, xf, llg,
    p2, alone, pf, po, summed, r1, rdir, hall, dqa, dka, dva, acc,
    in_sem, out_sem, own_sem, w_send, w_recv, z_send, z_recv, f_send, f_recv, b_send, b_recv, c_send, c_recv, r_send, r_recv, h_send, h_recv,
):
    me_s = lax.axis_index("seq")
    me_h = lax.axis_index("head")
    core = lax.rem(me_s, 2)
    right, left, across = lax.rem(me_h + 1, 4), lax.rem(me_h + 3, 4), lax.rem(me_h + 2, 4)

    def bit_of(bit):
        return lax.rem(lax.div(me_s, 1 << bit), 2)

    def flipped(bits):
        to = me_s
        for bit in bits:
            to = to + (1 << bit) - (2 << bit) * bit_of(bit)
        return to

    def partner(step):
        if step == 0:
            return flipped([0])
        low, j = (1, step) if step < 4 else (3, step - 3)
        return flipped([low + i for i in range(2) if j >> i & 1])

    def send(src, dst, send_sem, recv_sem, seq, head):
        copy = pltpu.make_async_remote_copy(
            src_ref=src, dst_ref=dst, send_sem=send_sem, recv_sem=recv_sem,
            device_id=(seq, head), device_id_type=MESH,
        )
        copy.start()
        return copy

    loads = []
    for n, (src, dst) in enumerate([(k_in, k_ref), (v_in, v_ref), (lw_in, lw_ref), (q_in, q_ref), (og_in, og_ref)]):
        loads.append(pltpu.make_async_copy(src, dst, in_sem.at[n]))
        loads[n].start()

    barrier = pltpu.get_barrier_semaphore()
    for other in (right, left, across):
        pl.semaphore_signal(barrier, inc=1, device_id=(me_s, other), device_id_type=MESH)
    for step in range(7):
        pl.semaphore_signal(barrier, inc=1, device_id=(partner(step), me_h), device_id_type=MESH)
    pl.semaphore_wait(barrier, 10)

    own = pltpu.make_async_copy(w_hbm.at[:, pl.ds(pl.multiple_of(me_h * 512, 512), 512)], wall.at[0], own_sem)
    def rows_at(start, size):
        return pl.ds(pl.multiple_of(start, 32), size)

    def columns_of(k):
        return pl.ds(pl.multiple_of(lax.rem(me_h + k, 4) * 512, 512), 512)

    half = rows_at(core * 128, 128)
    eighth = rows_at(core * 128 + lax.div(me_s, 8) * 32, 32)
    w_copies = {}

    def send_weights(i, k, rows):
        w_copies[i] = send(
            w_hbm.at[rows, columns_of(k)], wall.at[k, rows], w_send.at[i], w_recv.at[i], me_s, lax.rem(me_h + k, 4))

    send_weights(0, 2, rows_at(core * 128, 64))
    send_weights(2, 1, eighth)
    send_weights(3, 3, eighth)
    send_weights(1, 2, rows_at(core * 128 + 64, 64))
    own.start()
    sibling = partner(0)
    f_copies = {}

    def to_sibling(i, k, rows):
        f_copies[i] = send(wall.at[k, rows], wall.at[k, rows], f_send.at[i], f_recv.at[i], sibling, me_h)

    z_copies = []

    def share_weights():
        for i, k in enumerate((1, 3)):
            w_copies[2 + i].wait_recv()
            for n in range(3):
                at = 3 * i + n
                z_copies.append(send(
                    wall.at[k, eighth], wall.at[k, eighth], z_send.at[at], z_recv.at[at], partner(4 + n), me_h))

    def forward_shared():
        for i, k in enumerate((1, 3)):
            for n in range(3):
                z_copies[3 * i + n].wait_recv()
            to_sibling(2 + i, k, half)

    row_id = lax.broadcasted_iota(jnp.int32, (BLK, BLK), 0)
    col_id = lax.broadcasted_iota(jnp.int32, (BLK, BLK), 1)
    apart = row_id ^ col_id
    level = jnp.zeros((BLK, BLK), jnp.int32)
    for bit in range(7):
        level = level + ((apart >> bit) > 0).astype(jnp.int32)
    lev_ref[...] = jnp.where(row_id <= col_id, level, -1)

    def cols_of(b):
        return pl.ds(pl.multiple_of(b * BLK, BLK), BLK)

    loads[0].wait()
    loads[1].wait()

    @pl.loop(0, 8, unroll=4)
    def _(b):
        cols = cols_of(b)
        k_all, v_all = k_ref[cols].reshape(BLK, 256), v_ref[cols].reshape(BLK, 256)
        for h in range(2):
            lanes = slice(h * 128, h * 128 + 128)
            kn[h, cols, :] = k_all[:, lanes]
            vn[h, cols, :] = v_all[:, lanes]
            kb, vb = k_all[:, lanes].T, v_all[:, lanes].T
            kt[h, :, cols] = kb
            vt[h, :, cols] = vb
            tb[h, b] = mm_nt(kb, vb)

    total = []
    for h in range(2):
        t = [tb[h, b] for b in range(8)]
        pairs = [t[2 * i] + t[2 * i + 1] for i in range(4)]
        quads = [pairs[0] + pairs[1], pairs[2] + pairs[3]]
        for slot, value in enumerate([t[0], t[2], t[4], t[6], pairs[0], pairs[2], quads[0]]):
            tl[h, slot] = value.astype(BF16)
            tlt[h, slot] = value.T.astype(BF16)
        xf[h] = quads[0] + quads[1]

    b_copies = {}

    def send_states(phase):
        for h in range(2):
            sb[phase, h] = xf[h].astype(BF16)
        for step in PHASES[phase]:
            b_copies[step] = send(sb.at[phase], rb.at[step], b_send.at[step], b_recv.at[step], partner(step), me_h)

    def keep_state(h, slot, value):
        kept = value * bit_of(slot).astype(F32)
        tst[h, slot * 128:slot * 128 + 128, :] = kept.astype(BF16)
        tstt[h, :, slot * 128:slot * 128 + 128] = kept.T.astype(BF16)

    def take_states(phase):
        for step in PHASES[phase]:
            b_copies[step].wait_recv()
        for h in range(2):
            got = [rb[step, h].astype(F32) for step in PHASES[phase]]
            if phase == 0:
                keep_state(h, 0, got[0])
                xf[h] = xf[h] + got[0]
            else:
                far = got[1] + got[2]
                keep_state(h, 2 * phase - 1, got[0])
                keep_state(h, 2 * phase, far)
                xf[h] = xf[h] + got[0] + far

    send_states(0)
    loads[2].wait()
    loads[3].wait()

    for h in range(2):
        for l in range(LOCAL_LEVELS + DEV_BITS):
            wsc[h, l:l + 1, :] = lw_ref[l, h:h + 1, :] * scale_of(l)

    take_states(0)
    send_states(1)

    @pl.loop(0, 8, unroll=4)
    def _(b):
        cols = cols_of(b)
        q_all = q_ref[cols].reshape(BLK, 256)
        for h in range(2):
            qb = q_all[:, h * 128:h * 128 + 128].T
            qt[h, :, cols] = qb
            qf = qb.astype(F32)
            for c in range(3 + DEV_BITS):
                wq[h, c, :, cols] = (qf * wsc[h, DIAG_LEVELS + c:DIAG_LEVELS + c + 1, cols]).astype(BF16)

    right_msgs, left_msgs = {}, {}

    def send_right(i, src, dst):
        right_msgs[i] = send(src, dst, r_send.at[i], r_recv.at[i], me_s, right)

    def send_left(i, src, dst):
        left_msgs[i] = send(src, dst, r_send.at[6 + i], r_recv.at[6 + i], me_s, left)

    def partial_grad(k, u, j):
        rows = slice(u * 512 + j * 256, u * 512 + j * 256 + 256)
        return mm_nt(wall[k], og_ref[rows, :])

    share_weights()
    loads[4].wait()
    started = []

    def first_leg(head, r, to):
        rows = rows_at(head * 128 + r * 64, 64)
        for u in range(2):
            at = slice(u * 512, u * 512 + 512)
            p2[head, r, :, at] = mm_nt(wall[2, rows, :], og_ref[at, :]).astype(BF16)
        i = 6 * head + r
        started.append(send(p2.at[head, r], r1.at[head, r], r_send.at[i], r_recv.at[i], me_s, to))

    def await_first(head):
        for r in range(2):
            pltpu.make_async_remote_copy(
                src_ref=p2.at[head, r], dst_ref=r1.at[head, r], send_sem=r_send.at[6 * head + r],
                recv_sem=r_recv.at[6 * head + r], device_id=(me_s, left), device_id_type=MESH,
            ).wait_recv()

    for r in range(2):
        w_copies[r].wait_recv()
        to_sibling(r, 2, rows_at(core * 128 + r * 64, 64))
        first_leg(core, r, lax.rem(me_h + 1 + 2 * core, 4))
    for r in range(2):
        f_copies[r].wait_recv()
        first_leg(1 - core, r, lax.rem(me_h + 3 - 2 * core, 4))

    def diag_forward(b):
        cols = cols_of(b)
        for h in range(2):
            lev = lev_ref[...]
            mix = jnp.zeros((BLK, BLK), F32)
            for l in range(DIAG_LEVELS):
                mix = jnp.where(lev == l, wsc[h, l:l + 1, cols], mix)
            scores = mm(kn[h, cols, :], qt[h, :, cols])
            weighted = (mix * scores).astype(BF16)
            st_ref[h, b] = scores
            mix_ref[h, b] = mix
            near[h, b] = weighted
            ot[h, :, cols] = mm(vt[h, :, cols], weighted)

    pl.loop(0, 4, unroll=4)(diag_forward)
    take_states(1)
    send_states(2)
    forward_shared()

    def second_leg(head, k, to):
        rows = rows_at(head * 128, 128)
        for u in range(2):
            alone[head, u] = mm_nt(wall[k, rows, :], og_ref[u * 512:u * 512 + 512, :]).astype(BF16)
            i = 8 - 6 * head + u
            started.append(send(
                alone.at[head, u], rdir.at[head, head, u], r_send.at[i], r_recv.at[i], me_s, to))

    def await_second(head, u):
        i = 8 - 6 * head + u
        pltpu.make_async_remote_copy(
            src_ref=alone.at[head, u], dst_ref=rdir.at[head, head, u], send_sem=r_send.at[i], recv_sem=r_recv.at[i],
            device_id=(me_s, left), device_id_type=MESH,
        ).wait_recv()

    second_leg(core, 1 + 2 * core, lax.rem(me_h + 3 + 2 * core, 4))
    f_copies[2].wait_recv()
    f_copies[3].wait_recv()
    second_leg(1 - core, 3 - 2 * core, lax.rem(me_h + 1 + 2 * core, 4))
    for u in range(2):
        for head, k in ((0, 3), (1, 1)):
            pf[head, u] = mm_nt(wall[k, head * 128:head * 128 + 128, :], og_ref[u * 512:u * 512 + 512, :])
    pl.loop(4, 8, unroll=4)(diag_forward)

    for h in range(2):
        for slot, (c, first, size) in enumerate(LOCAL_PAIRS):
            at = slice(first * BLK, (first + size) * BLK)
            ot[h, :, at] = ot[h, :, at] + mm(tlt[h, slot], wq[h, c, :, at])

    own.wait()
    for u in range(2):
        for j in range(2):
            at = slice(j * 256, j * 256 + 256)
            part = partial_grad(0, u, j)
            po[0, u, :, at] = part[:128]
            po[1, u, :, at] = part[128:]
    await_first(0)
    await_first(1)
    for u in range(2):
        at = slice(u * 512, u * 512 + 512)
        for head in range(2):
            for r in range(2):
                rows = slice(r * 64, r * 64 + 64)
                summed[head, u, rows, :] = (pf[head, u, rows, :] + r1[head, r, :, at].astype(F32)).astype(BF16)
        send_right(4 + u, summed.at[0, u], rdir.at[1, 0, u])
        send_left(4 + u, summed.at[1, u], rdir.at[0, 1, u])
    take_states(2)

    @pl.loop(0, 8, unroll=4)
    def _(b):
        cols = cols_of(b)
        for h in range(2):
            far = mm(tstt[h], wq[h, 3:, :, cols].reshape(DEV_BITS * 128, BLK))
            hall[0, cols, h * 128:h * 128 + 128] = (ot[h, :, cols] + far).T.astype(BF16)

    h_copies = {}

    def send_heads(i, slot, piece, to_slot, head):
        rows = slice(piece * 256, piece * 256 + 256)
        h_copies[i] = send(hall.at[slot, rows], hall.at[to_slot, rows], h_send.at[i], h_recv.at[i], me_s, head)

    for n in range(4):
        send_heads(n, 0, n, 1, right)
        send_heads(6 + n, 0, (n + 2) % 4, 3, left)

    def relay_heads(n):
        h_copies[n].wait_recv()
        send_heads(4 + n, 1, n, 2, right)
        h_copies[6 + n].wait_recv()
        send_heads(10 + n, 3, n + 2, 2, left)

    def take_head_grad(u):
        at = slice(u * 512, u * 512 + 512)
        await_second(0, u)
        await_second(1, u)
        right_msgs[4 + u].wait_recv()
        left_msgs[4 + u].wait_recv()
        for h in range(2):
            gt[h, :, at] = (po[h, u] + rdir[0, h, u].astype(F32) + rdir[1, h, u].astype(F32)).astype(BF16)
        for h in range(2):
            grads = mm_nt(wq[h, 3:, :, at].reshape(DEV_BITS * 128, 512), gt[h, :, at])
            for step in range(DEV_BITS):
                piece = grads[step * 128:step * 128 + 128]
                lg[h, step] = piece if u == 0 else lg[h, step] + piece

    c_copies = {}

    def swap_shares():
        other = 1 - core
        for n, slot in enumerate((3, 4, 1, 2)):
            cs[n] = lg[other, slot].astype(BF16)
        for h in range(2):
            cs[4 + h] = lg[h, 0].astype(BF16)
        for n, (start, size) in enumerate(((0, 2), (2, 4))):
            at = slice(start, start + size)
            c_copies[7 + n] = send(cs.at[at], cr.at[at], c_send.at[7 + n], c_recv.at[7 + n], sibling, me_h)

    def share_of(slot, n):
        return (lg[core, slot] + cr[n].astype(F32)) * bit_of(slot).astype(F32)

    def pass_on(phase):
        for n, step in enumerate(PHASES[phase]):
            c_copies[step] = send(
                cb.at[2 * phase - 2 + min(n, 1)], rcb.at[step], c_send.at[step], c_recv.at[step], partner(step), me_h)

    def await_steps(phase):
        got = None
        for step in PHASES[phase]:
            c_copies[step].wait_recv()
            piece = rcb[step].astype(F32)
            got = piece if got is None else got + piece
        return got

    def grads_to_z():
        c_copies[7].wait_recv()
        cb[2] = share_of(3, 0).astype(BF16)
        cb[3] = share_of(4, 1).astype(BF16)
        pass_on(2)

    def grads_to_y():
        c_copies[8].wait_recv()
        got = await_steps(2)
        xf[0] = got
        cb[0] = (got + share_of(1, 2)).astype(BF16)
        cb[1] = (got + share_of(2, 3)).astype(BF16)
        pass_on(1)

    def swap_results():
        got = xf[0] + await_steps(1)
        xf[0] = got
        cb[4] = got.astype(BF16)
        c_copies[0] = send(cb.at[4], rcb.at[0], c_send.at[0], c_recv.at[0], sibling, me_h)

    def final_grads():
        c_copies[0].wait_recv()
        mine = xf[0]
        theirs = rcb[0].astype(F32)
        second = core.astype(F32)
        first = 1.0 - second
        near_share = (1 - bit_of(0)).astype(F32)
        return [
            mine * first + theirs * second + cr[4].astype(F32) * near_share,
            mine * second + theirs * first + cr[5].astype(F32) * near_share,
        ]

    def diag_backward(b):
        cols = cols_of(b)
        for h in range(2):
            lev = lev_ref[...]
            gb = gt[h, :, cols]
            grad_scores = mm(vn[h, cols, :], gb)
            weighted = (mix_ref[h, b] * grad_scores).astype(BF16)
            product = grad_scores * st_ref[h, b]
            dqa[h, :, cols] = mm(kt[h, :, cols], weighted)
            dka[h, :, cols] = mm_nt(qt[h, :, cols], weighted)
            dva[h, :, cols] = mm_nt(gb, near[h, b])
            for l in range(DIAG_LEVELS):
                summed_l = jnp.sum(jnp.where(lev == l, product, 0.0), axis=0, keepdims=True)
                wg_ref[l, h:h + 1, cols] = summed_l * scale_of(l)

    def far_backward(b):
        cols = cols_of(b)
        for h in range(2):
            gb = gt[h, :, cols]
            qf = qt[h, :, cols].astype(F32)
            sums = dqa[h, :, cols]
            all_got = mm(tst[h], gb)
            for step in range(DEV_BITS):
                l = LOCAL_LEVELS + step
                got = all_got[step * 128:step * 128 + 128]
                sums = sums + got * wsc[h, l:l + 1, cols]
                wg_ref[l, h:h + 1, cols] = jnp.sum(got * qf, axis=0, keepdims=True) * scale_of(l)
            dqa[h, :, cols] = sums

    def local_backward(h):
        for l in range(DIAG_LEVELS, LOCAL_LEVELS):
            wg_ref[l, h:h + 1, :] = jnp.zeros((1, 1024), F32)
        for slot, (c, first, size) in enumerate(LOCAL_PAIRS):
            at = slice(first * BLK, (first + size) * BLK)
            l = DIAG_LEVELS + c
            gb = gt[h, :, at]
            got = mm(tl[h, slot], gb)
            dqa[h, :, at] = dqa[h, :, at] + got * wsc[h, l:l + 1, at]
            wg_ref[l, h:h + 1, at] = jnp.sum(got * qt[h, :, at].astype(F32), axis=0, keepdims=True) * scale_of(l)
            llg[h, slot] = mm_nt(wq[h, c, :, at], gb)

    take_head_grad(0)
    pl.loop(0, 4, unroll=4)(diag_backward)
    take_head_grad(1)
    swap_shares()
    pl.loop(0, 4, unroll=4)(far_backward)
    grads_to_z()
    pl.loop(4, 8, unroll=4)(diag_backward)
    relay_heads(0)
    relay_heads(1)
    for h in range(2):
        local_backward(h)
    grads_to_y()
    pl.loop(4, 8, unroll=4)(far_backward)

    stores = []

    def store(src, dst):
        stores.append(pltpu.make_async_copy(src, dst, out_sem.at[len(stores)]))
        stores[-1].start()

    store(wg_ref, wg_out)

    @pl.loop(0, 8, unroll=4)
    def _(b):
        cols = cols_of(b)
        both = jnp.concatenate([dqa[h, :, cols].T.astype(BF16) for h in range(2)], axis=1)
        dq_ref[cols] = both.reshape(BLK, 2, 128)

    store(dq_ref, dq_out)

    @pl.loop(0, 4, unroll=2)
    def _(b):
        rows = pl.ds(pl.multiple_of(b * 256, 256), 256)
        acc[rows, :] = mm(hall[0, rows, :], wall[0])

    for b in range(8):
        at = slice(b * BLK, b * BLK + BLK)
        for h in range(2):
            dk, dv = dka[h, :, at], dva[h, :, at]
            parts = [llg[h, slot] for slot, (c, first, size) in enumerate(LOCAL_PAIRS) if first - size <= b < first]
            if parts:
                x = functools.reduce(lambda a, p: a + p, parts)
                dk = dk + mm(x.astype(BF16), vt[h, :, at])
                dv = dv + mm(x.T.astype(BF16), kt[h, :, at])
            dkn[h, at, :] = dk.T
            dvn[h, at, :] = dv.T

    swap_results()
    for n in (2, 3):
        h_copies[n].wait_recv()
        h_copies[6 + n].wait_recv()

    @pl.loop(0, 4, unroll=2)
    def _(b):
        rows = pl.ds(pl.multiple_of(b * 256, 256), 256)
        acc[rows, :] = acc[rows, :] + mm(hall[1, rows, :], wall[1]) + mm(hall[3, rows, :], wall[3])

    late = [x.astype(BF16) for x in final_grads()]
    for b in range(4):
        at = slice(b * 256, b * 256 + 256)
        dk = [(dkn[h, at, :] + mm_nt(vn[h, at, :], late[h])).astype(BF16) for h in range(2)]
        dv = [(dvn[h, at, :] + mm(kn[h, at, :], late[h])).astype(BF16) for h in range(2)]
        dk_ref[at] = jnp.concatenate(dk, axis=1).reshape(256, 2, 128)
        dv_ref[at] = jnp.concatenate(dv, axis=1).reshape(256, 2, 128)

    store(dk_ref, dk_out)
    store(dv_ref, dv_out)

    for n in range(2):
        for i, b in ((4 + n, n), (10 + n, n + 2)):
            h_copies[i].wait_recv()
            rows = slice(b * 256, b * 256 + 256)
            lo_ref[rows, :] = (acc[rows, :] + mm(hall[2, rows, :], wall[2])).astype(BF16)
            store(lo_ref.at[rows], lo_out.at[rows])

    for group in (w_copies, f_copies, dict(enumerate(z_copies)), right_msgs, left_msgs, h_copies, b_copies, c_copies):
        for copy in group.values():
            copy.wait_send()
    for copy in started:
        copy.wait_send()
    for copy in stores:
        copy.wait()


def copy_kernel(*refs):
    sources, targets, sems = refs[:5], refs[5:10], refs[10]
    copies = [pltpu.make_async_copy(a, b, sems.at[i]) for i, (a, b) in enumerate(zip(sources, targets))]
    for copy in copies:
        copy.start()
    for copy in copies:
        copy.wait()


def per_device(queries, key_rows, value_rows, level_weights, out_weight, out_grad):
    dma = pltpu.SemaphoreType.DMA
    vmem = pltpu.VMEM
    anywhere = pl.BlockSpec(memory_space=pl.ANY)
    hbm = pl.BlockSpec(memory_space=pltpu.HBM)
    stack = 3 + DEV_BITS
    shape = queries.shape
    shapes = (
        jax.ShapeDtypeStruct(out_grad.shape, BF16),
        jax.ShapeDtypeStruct(shape, BF16),
        jax.ShapeDtypeStruct(shape, BF16),
        jax.ShapeDtypeStruct(shape, BF16),
        jax.ShapeDtypeStruct(level_weights.shape, F32),
    )
    outs = pl.pallas_call(
        kernel,
        out_shape=shapes,
        in_specs=[hbm] * 6,
        out_specs=[anywhere] * 5,
        scratch_shapes=[
            vmem(shape, BF16), vmem(shape, BF16), vmem(shape, BF16),
            vmem(level_weights.shape, F32), vmem(out_grad.shape, BF16),
            vmem(out_grad.shape, BF16),
            vmem(shape, BF16), vmem(shape, BF16), vmem(shape, BF16),
            vmem(level_weights.shape, F32),
            vmem((2, 1024, 128), BF16), vmem((2, 1024, 128), BF16),
            vmem((4, 256, 512), BF16),
            vmem((2, LOCAL_LEVELS + DEV_BITS, 1024), F32),
            vmem((BLK, BLK), jnp.int32),
            vmem((2, 128, 1024), BF16),
            vmem((2, 128, 1024), BF16),
            vmem((2, 128, 1024), BF16),
            vmem((2, 128, 1024), BF16),
            vmem((2, stack, 128, 1024), BF16),
            vmem((2, 8, BLK, BLK), F32),
            vmem((2, 8, BLK, BLK), F32),
            vmem((2, 8, BLK, BLK), BF16),
            vmem((2, 8, 128, 128), F32),
            vmem((2, 7, 128, 128), BF16),
            vmem((2, 7, 128, 128), BF16),
            vmem((2, 128, 1024), F32),
            vmem((3, 2, 128, 128), BF16),
            vmem((7, 2, 128, 128), BF16),
            vmem((5, 128, 128), BF16),
            vmem((7, 128, 128), BF16),
            vmem((6, 128, 128), BF16),
            vmem((6, 128, 128), BF16),
            vmem((2, 1024, 128), F32),
            vmem((2, 1024, 128), F32),
            vmem((2, DEV_BITS * 128, 128), BF16),
            vmem((2, 128, DEV_BITS * 128), BF16),
            vmem((2, DEV_BITS, 128, 128), F32),
            vmem((2, 128, 128), F32),
            vmem((2, 7, 128, 128), F32),
            vmem((2, 2, 64, 1024), BF16),
            vmem((2, 2, 128, 512), BF16),
            vmem((2, 2, 128, 512), F32),
            vmem((2, 2, 128, 512), F32),
            vmem((2, 2, 128, 512), BF16),
            vmem((2, 2, 64, 1024), BF16),
            vmem((2, 2, 2, 128, 512), BF16),
            vmem((4, 1024, 256), BF16),
            vmem((2, 128, 1024), F32),
            vmem((2, 128, 1024), F32),
            vmem((2, 128, 1024), F32),
            vmem((1024, 512), F32),
            dma((5,)), dma((8,)), dma,
            dma((4,)), dma((4,)), dma((6,)), dma((6,)), dma((4,)), dma((4,)),
            dma((7,)), dma((7,)), dma((9,)), dma((9,)),
            dma((12,)), dma((12,)), dma((12,)), dma((12,)),
        ],
        compiler_params=pltpu.CompilerParams(
            collective_id=0, has_side_effects=True, vmem_limit_bytes=40 * 1024 * 1024),
        cost_estimate=pl.CostEstimate(flops=6 * 10**9, bytes_accessed=8 * 2**20, transcendentals=0),
    )(
        *(pltpu.with_memory_space_constraint(x, pltpu.HBM) for x in (
            queries, key_rows, value_rows, level_weights, out_weight.reshape(256, 2048), out_grad)),
    )
    return pl.pallas_call(
        copy_kernel,
        out_shape=shapes,
        in_specs=[anywhere] * 5,
        out_specs=[hbm] * 5,
        scratch_shapes=[dma((5,))],
        compiler_params=pltpu.CompilerParams(vmem_limit_bytes=2 * 1024 * 1024),
        cost_estimate=pl.CostEstimate(flops=0, bytes_accessed=6 * 2**20, transcendentals=0),
    )(*outs)


def solution(mesh):
    in_specs = (
        P("seq", "head", None),
        P("seq", "head", None),
        P("seq", "head", None),
        P(None, "head", "seq"),
        P("head", None, None),
        P("seq", "head"),
    )
    out_specs = (
        P("seq", "head"),
        P("seq", "head", None),
        P("seq", "head", None),
        P("seq", "head", None),
        P(None, "head", "seq"),
    )
    return jax.shard_map(
        per_device, mesh=mesh, in_specs=in_specs, out_specs=out_specs, check_vma=False
    )
```

```python
import functools

import jax
import jax.numpy as jnp
from jax import lax
from jax.experimental import pallas as pl
from jax.experimental.pallas import tpu as pltpu
from jax.sharding import PartitionSpec as P

MESH = pl.DeviceIdType.MESH
F32 = jnp.float32
BF16 = jnp.bfloat16
LEVEL_GAIN = 0.02
BLK = 128
DIAG_LEVELS = 8
DEV_BITS = 5
PHASES = ((0,), (1, 2, 3), (4, 5, 6))
LOCAL_LEVELS = 11


def scale_of(level):
    return LEVEL_GAIN * 2.0 ** (-0.5 * max(level - 1, 0))


LOCAL_PAIRS = [(0, 1, 1), (0, 3, 1), (0, 5, 1), (0, 7, 1), (1, 2, 2), (1, 6, 2), (2, 4, 4)]


def mm(a, b):
    return jnp.dot(a, b, preferred_element_type=F32)


def mm_nt(a, b):
    return lax.dot_general(a, b, (((1,), (1,)), ((), ())), preferred_element_type=F32)


def kernel(
    q_in, k_in, v_in, lw_in, w_hbm, og_in,
    lo_out, dq_out, dk_out, dv_out, wg_out,
    q_ref, k_ref, v_ref, lw_ref, og_ref, lo_ref, dq_ref, dk_ref, dv_ref, wg_ref, kn, vn,
    wall, wsc, lev_ref, qt, kt, vt, gt, wq, st_ref, mix_ref, near, tb, tl, tlt, ot,
    sb, rb, cb, rcb, cs, cr, dkn, dvn, tst, tstt, lg, xf, llg,
    p2, alone, pf, po, summed, r1, ra, rb_sum, hall, dqa, dka, dva, acc,
    in_sem, out_sem, own_sem, w_send, w_recv, z_send, z_recv, f_send, f_recv, b_send, b_recv, c_send, c_recv, a_send, a_recv, r_send, r_recv, h_send, h_recv,
):
    me_s = lax.axis_index("seq")
    me_h = lax.axis_index("head")
    core = lax.rem(me_s, 2)
    right, left, across = lax.rem(me_h + 1, 4), lax.rem(me_h + 3, 4), lax.rem(me_h + 2, 4)

    def bit_of(bit):
        return lax.rem(lax.div(me_s, 1 << bit), 2)

    def flipped(bits):
        to = me_s
        for bit in bits:
            to = to + (1 << bit) - (2 << bit) * bit_of(bit)
        return to

    def partner(step):
        if step == 0:
            return flipped([0])
        low, j = (1, step) if step < 4 else (3, step - 3)
        return flipped([low + i for i in range(2) if j >> i & 1])

    def send(src, dst, send_sem, recv_sem, seq, head):
        copy = pltpu.make_async_remote_copy(
            src_ref=src, dst_ref=dst, send_sem=send_sem, recv_sem=recv_sem,
            device_id=(seq, head), device_id_type=MESH,
        )
        copy.start()
        return copy

    loads = []
    for n, (src, dst) in enumerate([(k_in, k_ref), (v_in, v_ref), (lw_in, lw_ref), (q_in, q_ref), (og_in, og_ref)]):
        loads.append(pltpu.make_async_copy(src, dst, in_sem.at[n]))
        loads[n].start()

    barrier = pltpu.get_barrier_semaphore()
    for other in (right, left, across):
        pl.semaphore_signal(barrier, inc=1, device_id=(me_s, other), device_id_type=MESH)
    for step in range(7):
        pl.semaphore_signal(barrier, inc=1, device_id=(partner(step), me_h), device_id_type=MESH)
    pl.semaphore_wait(barrier, 10)

    own = pltpu.make_async_copy(w_hbm.at[:, pl.ds(pl.multiple_of(me_h * 512, 512), 512)], wall.at[0], own_sem)
    def rows_at(start, size):
        return pl.ds(pl.multiple_of(start, 32), size)

    def columns_of(k):
        return pl.ds(pl.multiple_of(lax.rem(me_h + k, 4) * 512, 512), 512)

    half = rows_at(core * 128, 128)
    eighth = rows_at(core * 128 + lax.div(me_s, 8) * 32, 32)
    w_copies = {}

    def send_weights(i, k, rows):
        w_copies[i] = send(
            w_hbm.at[rows, columns_of(k)], wall.at[k, rows], w_send.at[i], w_recv.at[i], me_s, lax.rem(me_h + k, 4))

    direct, shared = 1 + 2 * core, (2, 3 - 2 * core)
    send_weights(0, direct, rows_at(core * 128, 64))
    send_weights(2, shared[0], eighth)
    send_weights(3, shared[1], eighth)
    send_weights(1, direct, rows_at(core * 128 + 64, 64))
    own.start()
    sibling = partner(0)
    f_copies = {}

    def to_sibling(i, k, rows):
        f_copies[i] = send(wall.at[k, rows], wall.at[k, rows], f_send.at[i], f_recv.at[i], sibling, me_h)

    z_copies = []

    def share_weights():
        for i, k in enumerate(shared):
            w_copies[2 + i].wait_recv()
            for n in range(3):
                at = 3 * i + n
                z_copies.append(send(
                    wall.at[k, eighth], wall.at[k, eighth], z_send.at[at], z_recv.at[at], partner(4 + n), me_h))

    def forward_shared(i):
        for n in range(3):
            z_copies[3 * i + n].wait_recv()
        to_sibling(2 + i, shared[i], half)

    row_id = lax.broadcasted_iota(jnp.int32, (BLK, BLK), 0)
    col_id = lax.broadcasted_iota(jnp.int32, (BLK, BLK), 1)
    apart = row_id ^ col_id
    level = jnp.zeros((BLK, BLK), jnp.int32)
    for bit in range(7):
        level = level + ((apart >> bit) > 0).astype(jnp.int32)
    lev_ref[...] = jnp.where(row_id <= col_id, level, -1)

    def cols_of(b):
        return pl.ds(pl.multiple_of(b * BLK, BLK), BLK)

    loads[0].wait()
    loads[1].wait()

    @pl.loop(0, 8, unroll=4)
    def _(b):
        cols = cols_of(b)
        k_all, v_all = k_ref[cols].reshape(BLK, 256), v_ref[cols].reshape(BLK, 256)
        for h in range(2):
            lanes = slice(h * 128, h * 128 + 128)
            kn[h, cols, :] = k_all[:, lanes]
            vn[h, cols, :] = v_all[:, lanes]
            kb, vb = k_all[:, lanes].T, v_all[:, lanes].T
            kt[h, :, cols] = kb
            vt[h, :, cols] = vb
            tb[h, b] = mm_nt(kb, vb)

    total = []
    for h in range(2):
        t = [tb[h, b] for b in range(8)]
        pairs = [t[2 * i] + t[2 * i + 1] for i in range(4)]
        quads = [pairs[0] + pairs[1], pairs[2] + pairs[3]]
        for slot, value in enumerate([t[0], t[2], t[4], t[6], pairs[0], pairs[2], quads[0]]):
            tl[h, slot] = value.astype(BF16)
            tlt[h, slot] = value.T.astype(BF16)
        xf[h] = quads[0] + quads[1]

    b_copies = {}

    def send_states(phase):
        for h in range(2):
            sb[phase, h] = xf[h].astype(BF16)
        for step in PHASES[phase]:
            b_copies[step] = send(sb.at[phase], rb.at[step], b_send.at[step], b_recv.at[step], partner(step), me_h)

    def keep_state(h, slot, value):
        kept = value * bit_of(slot).astype(F32)
        tst[h, slot * 128:slot * 128 + 128, :] = kept.astype(BF16)
        tstt[h, :, slot * 128:slot * 128 + 128] = kept.T.astype(BF16)

    def take_states(phase):
        for step in PHASES[phase]:
            b_copies[step].wait_recv()
        for h in range(2):
            got = [rb[step, h].astype(F32) for step in PHASES[phase]]
            if phase == 0:
                keep_state(h, 0, got[0])
                xf[h] = xf[h] + got[0]
            else:
                far = got[1] + got[2]
                keep_state(h, 2 * phase - 1, got[0])
                keep_state(h, 2 * phase, far)
                xf[h] = xf[h] + got[0] + far

    send_states(0)
    right_msgs, left_msgs = {}, {}

    def send_right(i, src, dst):
        right_msgs[i] = send(src, dst, r_send.at[2 + i], r_recv.at[2 + i], me_s, right)

    def send_left(i, src, dst):
        left_msgs[i] = send(src, dst, r_send.at[6 + i], r_recv.at[6 + i], me_s, left)

    def partial_grad(k, u, j):
        rows = slice(u * 512 + j * 256, u * 512 + j * 256 + 256)
        return mm_nt(wall[k], og_ref[rows, :])

    loads[4].wait()
    started = []

    def straight_leg(head, k, r, to):
        rows = rows_at(head * 128 + r * 64, 64)
        for u in range(2):
            alone[head, r, u] = mm_nt(wall[k, rows, :], og_ref[u * 512:u * 512 + 512, :]).astype(BF16)
            i = 4 * head + 2 * r + u
            started.append(send(alone.at[head, r, u], ra.at[head, r, u], a_send.at[i], a_recv.at[i], me_s, to))

    def await_straight(head, u):
        for r in range(2):
            i = 4 * head + 2 * r + u
            pltpu.make_async_remote_copy(
                src_ref=alone.at[head, r, u], dst_ref=ra.at[head, r, u], send_sem=a_send.at[i], recv_sem=a_recv.at[i],
                device_id=(me_s, left), device_id_type=MESH,
            ).wait_recv()

    for r in range(2):
        w_copies[r].wait_recv()
        to_sibling(r, direct, rows_at(core * 128 + r * 64, 64))
        straight_leg(core, direct, r, lax.rem(me_h + 3 + 2 * core, 4))
        if r == 0:
            share_weights()
    take_states(0)
    send_states(1)
    for r in range(2):
        f_copies[r].wait_recv()
        straight_leg(1 - core, 3 - 2 * core, r, lax.rem(me_h + 1 + 2 * core, 4))

    loads[2].wait()
    loads[3].wait()

    for h in range(2):
        for l in range(LOCAL_LEVELS + DEV_BITS):
            wsc[h, l:l + 1, :] = lw_ref[l, h:h + 1, :] * scale_of(l)

    @pl.loop(0, 8, unroll=4)
    def _(b):
        cols = cols_of(b)
        q_all = q_ref[cols].reshape(BLK, 256)
        for h in range(2):
            qb = q_all[:, h * 128:h * 128 + 128].T
            qt[h, :, cols] = qb
            qf = qb.astype(F32)
            for c in range(3 + DEV_BITS):
                wq[h, c, :, cols] = (qf * wsc[h, DIAG_LEVELS + c:DIAG_LEVELS + c + 1, cols]).astype(BF16)

    def diag_forward(b):
        cols = cols_of(b)
        for h in range(2):
            lev = lev_ref[...]
            mix = jnp.zeros((BLK, BLK), F32)
            for l in range(DIAG_LEVELS):
                mix = jnp.where(lev == l, wsc[h, l:l + 1, cols], mix)
            scores = mm(kn[h, cols, :], qt[h, :, cols])
            weighted = (mix * scores).astype(BF16)
            st_ref[h, b] = scores
            mix_ref[h, b] = mix
            near[h, b] = weighted
            ot[h, :, cols] = mm(vt[h, :, cols], weighted)

    pl.loop(0, 4, unroll=4)(diag_forward)
    forward_shared(0)

    def relay_leg(head, u, to):
        rows = rows_at(head * 128, 128)
        p2[head, u] = mm_nt(wall[2, rows, :], og_ref[u * 512:u * 512 + 512, :]).astype(BF16)
        i = 4 * head + u
        started.append(send(p2.at[head, u], r1.at[head, u], r_send.at[i], r_recv.at[i], me_s, to))

    def await_relay(head, u):
        i = 4 * head + u
        pltpu.make_async_remote_copy(
            src_ref=p2.at[head, u], dst_ref=r1.at[head, u], send_sem=r_send.at[i], recv_sem=r_recv.at[i],
            device_id=(me_s, left), device_id_type=MESH,
        ).wait_recv()

    for u in range(2):
        relay_leg(core, u, lax.rem(me_h + 1 + 2 * core, 4))
        if u == 0:
            f_copies[2].wait_recv()
            forward_shared(1)
        relay_leg(1 - core, u, lax.rem(me_h + 3 - 2 * core, 4))
        if u == 0:
            take_states(1)
            send_states(2)
    f_copies[3].wait_recv()
    for u in range(2):
        for head, k in ((0, 3), (1, 1)):
            pf[head, u] = mm_nt(wall[k, head * 128:head * 128 + 128, :], og_ref[u * 512:u * 512 + 512, :])
    pl.loop(4, 8, unroll=4)(diag_forward)

    for h in range(2):
        for slot, (c, first, size) in enumerate(LOCAL_PAIRS):
            at = slice(first * BLK, (first + size) * BLK)
            ot[h, :, at] = ot[h, :, at] + mm(tlt[h, slot], wq[h, c, :, at])

    own.wait()
    for u in range(2):
        for j in range(2):
            at = slice(j * 256, j * 256 + 256)
            part = partial_grad(0, u, j)
            po[0, u, :, at] = part[:128]
            po[1, u, :, at] = part[128:]
    for u in range(2):
        await_relay(0, u)
        summed[0, u] = (pf[0, u] + r1[0, u].astype(F32)).astype(BF16)
        send_right(u, summed.at[0, u], rb_sum.at[0, u])
        await_relay(1, u)
        summed[1, u] = (pf[1, u] + r1[1, u].astype(F32)).astype(BF16)
        send_left(u, summed.at[1, u], rb_sum.at[1, u])
    take_states(2)

    @pl.loop(0, 8, unroll=4)
    def _(b):
        cols = cols_of(b)
        for h in range(2):
            far = mm(tstt[h], wq[h, 3:, :, cols].reshape(DEV_BITS * 128, BLK))
            hall[0, cols, h * 128:h * 128 + 128] = (ot[h, :, cols] + far).T.astype(BF16)

    h_copies = {}

    def send_heads(i, slot, piece, to_slot, head):
        rows = slice(piece * 256, piece * 256 + 256)
        h_copies[i] = send(hall.at[slot, rows], hall.at[to_slot, rows], h_send.at[i], h_recv.at[i], me_s, head)

    for n in range(4):
        send_heads(n, 0, n, 1, right)
        send_heads(6 + n, 0, (n + 2) % 4, 3, left)

    def relay_heads(n):
        h_copies[n].wait_recv()
        send_heads(4 + n, 1, n, 2, right)
        h_copies[6 + n].wait_recv()
        send_heads(10 + n, 3, n + 2, 2, left)

    def take_head_grad(u):
        at = slice(u * 512, u * 512 + 512)
        await_straight(0, u)
        await_straight(1, u)
        right_msgs[u].wait_recv()
        left_msgs[u].wait_recv()
        for h in range(2):
            for r in range(2):
                rows = slice(r * 64, r * 64 + 64)
                gt[h, rows, at] = (
                    po[h, u, rows, :] + ra[h, r, u].astype(F32) + rb_sum[h, u, rows, :].astype(F32)).astype(BF16)
        for h in range(2):
            grads = mm_nt(wq[h, 3:, :, at].reshape(DEV_BITS * 128, 512), gt[h, :, at])
            for step in range(DEV_BITS):
                piece = grads[step * 128:step * 128 + 128]
                lg[h, step] = piece if u == 0 else lg[h, step] + piece

    c_copies = {}

    def swap_shares():
        other = 1 - core
        for n, slot in enumerate((3, 4, 1, 2)):
            cs[n] = lg[other, slot].astype(BF16)
        for h in range(2):
            cs[4 + h] = lg[h, 0].astype(BF16)
        for n, (start, size) in enumerate(((0, 2), (2, 4))):
            at = slice(start, start + size)
            c_copies[7 + n] = send(cs.at[at], cr.at[at], c_send.at[7 + n], c_recv.at[7 + n], sibling, me_h)

    def share_of(slot, n):
        return (lg[core, slot] + cr[n].astype(F32)) * bit_of(slot).astype(F32)

    def pass_on(phase):
        for n, step in enumerate(PHASES[phase]):
            c_copies[step] = send(
                cb.at[2 * phase - 2 + min(n, 1)], rcb.at[step], c_send.at[step], c_recv.at[step], partner(step), me_h)

    def await_steps(phase):
        got = None
        for step in PHASES[phase]:
            c_copies[step].wait_recv()
            piece = rcb[step].astype(F32)
            got = piece if got is None else got + piece
        return got

    def grads_to_z():
        c_copies[7].wait_recv()
        cb[2] = share_of(3, 0).astype(BF16)
        cb[3] = share_of(4, 1).astype(BF16)
        pass_on(2)

    def grads_to_y():
        c_copies[8].wait_recv()
        got = await_steps(2)
        xf[0] = got
        cb[0] = (got + share_of(1, 2)).astype(BF16)
        cb[1] = (got + share_of(2, 3)).astype(BF16)
        pass_on(1)

    def swap_results():
        got = xf[0] + await_steps(1)
        xf[0] = got
        cb[4] = got.astype(BF16)
        c_copies[0] = send(cb.at[4], rcb.at[0], c_send.at[0], c_recv.at[0], sibling, me_h)

    def final_grads():
        c_copies[0].wait_recv()
        mine = xf[0]
        theirs = rcb[0].astype(F32)
        second = core.astype(F32)
        first = 1.0 - second
        near_share = (1 - bit_of(0)).astype(F32)
        return [
            mine * first + theirs * second + cr[4].astype(F32) * near_share,
            mine * second + theirs * first + cr[5].astype(F32) * near_share,
        ]

    def diag_backward(b):
        cols = cols_of(b)
        for h in range(2):
            lev = lev_ref[...]
            gb = gt[h, :, cols]
            grad_scores = mm(vn[h, cols, :], gb)
            weighted = (mix_ref[h, b] * grad_scores).astype(BF16)
            product = grad_scores * st_ref[h, b]
            dqa[h, :, cols] = mm(kt[h, :, cols], weighted)
            dka[h, :, cols] = mm_nt(qt[h, :, cols], weighted)
            dva[h, :, cols] = mm_nt(gb, near[h, b])
            for l in range(DIAG_LEVELS):
                summed_l = jnp.sum(jnp.where(lev == l, product, 0.0), axis=0, keepdims=True)
                wg_ref[l, h:h + 1, cols] = summed_l * scale_of(l)

    def far_backward(b):
        cols = cols_of(b)
        for h in range(2):
            gb = gt[h, :, cols]
            qf = qt[h, :, cols].astype(F32)
            sums = dqa[h, :, cols]
            all_got = mm(tst[h], gb)
            for step in range(DEV_BITS):
                l = LOCAL_LEVELS + step
                got = all_got[step * 128:step * 128 + 128]
                sums = sums + got * wsc[h, l:l + 1, cols]
                wg_ref[l, h:h + 1, cols] = jnp.sum(got * qf, axis=0, keepdims=True) * scale_of(l)
            dqa[h, :, cols] = sums

    def local_backward(h):
        for l in range(DIAG_LEVELS, LOCAL_LEVELS):
            wg_ref[l, h:h + 1, :] = jnp.zeros((1, 1024), F32)
        for slot, (c, first, size) in enumerate(LOCAL_PAIRS):
            at = slice(first * BLK, (first + size) * BLK)
            l = DIAG_LEVELS + c
            gb = gt[h, :, at]
            got = mm(tl[h, slot], gb)
            dqa[h, :, at] = dqa[h, :, at] + got * wsc[h, l:l + 1, at]
            wg_ref[l, h:h + 1, at] = jnp.sum(got * qt[h, :, at].astype(F32), axis=0, keepdims=True) * scale_of(l)
            llg[h, slot] = mm_nt(wq[h, c, :, at], gb)

    take_head_grad(0)
    pl.loop(0, 4, unroll=4)(diag_backward)
    take_head_grad(1)
    swap_shares()
    pl.loop(0, 4, unroll=4)(far_backward)
    grads_to_z()
    pl.loop(4, 8, unroll=4)(diag_backward)
    relay_heads(0)
    relay_heads(1)
    for h in range(2):
        local_backward(h)
    grads_to_y()
    pl.loop(4, 8, unroll=4)(far_backward)

    stores = []

    def store(src, dst):
        stores.append(pltpu.make_async_copy(src, dst, out_sem.at[len(stores)]))
        stores[-1].start()

    store(wg_ref, wg_out)

    @pl.loop(0, 8, unroll=4)
    def _(b):
        cols = cols_of(b)
        both = jnp.concatenate([dqa[h, :, cols].T.astype(BF16) for h in range(2)], axis=1)
        dq_ref[cols] = both.reshape(BLK, 2, 128)

    store(dq_ref, dq_out)

    @pl.loop(0, 4, unroll=2)
    def _(b):
        rows = pl.ds(pl.multiple_of(b * 256, 256), 256)
        acc[rows, :] = mm(hall[0, rows, :], wall[0])

    for b in range(8):
        at = slice(b * BLK, b * BLK + BLK)
        for h in range(2):
            dk, dv = dka[h, :, at], dva[h, :, at]
            parts = [llg[h, slot] for slot, (c, first, size) in enumerate(LOCAL_PAIRS) if first - size <= b < first]
            if parts:
                x = functools.reduce(lambda a, p: a + p, parts)
                dk = dk + mm(x.astype(BF16), vt[h, :, at])
                dv = dv + mm(x.T.astype(BF16), kt[h, :, at])
            dkn[h, at, :] = dk.T
            dvn[h, at, :] = dv.T

    swap_results()
    for n in (2, 3):
        h_copies[n].wait_recv()
        h_copies[6 + n].wait_recv()

    @pl.loop(0, 4, unroll=2)
    def _(b):
        rows = pl.ds(pl.multiple_of(b * 256, 256), 256)
        acc[rows, :] = acc[rows, :] + mm(hall[1, rows, :], wall[1]) + mm(hall[3, rows, :], wall[3])

    late = [x.astype(BF16) for x in final_grads()]
    for b in range(4):
        at = slice(b * 256, b * 256 + 256)
        dk = [(dkn[h, at, :] + mm_nt(vn[h, at, :], late[h])).astype(BF16) for h in range(2)]
        dv = [(dvn[h, at, :] + mm(kn[h, at, :], late[h])).astype(BF16) for h in range(2)]
        dk_ref[at] = jnp.concatenate(dk, axis=1).reshape(256, 2, 128)
        dv_ref[at] = jnp.concatenate(dv, axis=1).reshape(256, 2, 128)

    store(dk_ref, dk_out)
    store(dv_ref, dv_out)

    for n in range(2):
        for i, b in ((4 + n, n), (10 + n, n + 2)):
            h_copies[i].wait_recv()
            rows = slice(b * 256, b * 256 + 256)
            lo_ref[rows, :] = (acc[rows, :] + mm(hall[2, rows, :], wall[2])).astype(BF16)
            store(lo_ref.at[rows], lo_out.at[rows])

    for group in (w_copies, f_copies, dict(enumerate(z_copies)), right_msgs, left_msgs, h_copies, b_copies, c_copies):
        for copy in group.values():
            copy.wait_send()
    for copy in started:
        copy.wait_send()
    for copy in stores:
        copy.wait()


def copy_kernel(*refs):
    sources, targets, sems = refs[:5], refs[5:10], refs[10]
    copies = [pltpu.make_async_copy(a, b, sems.at[i]) for i, (a, b) in enumerate(zip(sources, targets))]
    for copy in copies:
        copy.start()
    for copy in copies:
        copy.wait()


def per_device(queries, key_rows, value_rows, level_weights, out_weight, out_grad):
    dma = pltpu.SemaphoreType.DMA
    vmem = pltpu.VMEM
    anywhere = pl.BlockSpec(memory_space=pl.ANY)
    hbm = pl.BlockSpec(memory_space=pltpu.HBM)
    stack = 3 + DEV_BITS
    shape = queries.shape
    shapes = (
        jax.ShapeDtypeStruct(out_grad.shape, BF16),
        jax.ShapeDtypeStruct(shape, BF16),
        jax.ShapeDtypeStruct(shape, BF16),
        jax.ShapeDtypeStruct(shape, BF16),
        jax.ShapeDtypeStruct(level_weights.shape, F32),
    )
    outs = pl.pallas_call(
        kernel,
        out_shape=shapes,
        in_specs=[hbm] * 6,
        out_specs=[anywhere] * 5,
        scratch_shapes=[
            vmem(shape, BF16), vmem(shape, BF16), vmem(shape, BF16),
            vmem(level_weights.shape, F32), vmem(out_grad.shape, BF16),
            vmem(out_grad.shape, BF16),
            vmem(shape, BF16), vmem(shape, BF16), vmem(shape, BF16),
            vmem(level_weights.shape, F32),
            vmem((2, 1024, 128), BF16), vmem((2, 1024, 128), BF16),
            vmem((4, 256, 512), BF16),
            vmem((2, LOCAL_LEVELS + DEV_BITS, 1024), F32),
            vmem((BLK, BLK), jnp.int32),
            vmem((2, 128, 1024), BF16),
            vmem((2, 128, 1024), BF16),
            vmem((2, 128, 1024), BF16),
            vmem((2, 128, 1024), BF16),
            vmem((2, stack, 128, 1024), BF16),
            vmem((2, 8, BLK, BLK), F32),
            vmem((2, 8, BLK, BLK), F32),
            vmem((2, 8, BLK, BLK), BF16),
            vmem((2, 8, 128, 128), F32),
            vmem((2, 7, 128, 128), BF16),
            vmem((2, 7, 128, 128), BF16),
            vmem((2, 128, 1024), F32),
            vmem((3, 2, 128, 128), BF16),
            vmem((7, 2, 128, 128), BF16),
            vmem((5, 128, 128), BF16),
            vmem((7, 128, 128), BF16),
            vmem((6, 128, 128), BF16),
            vmem((6, 128, 128), BF16),
            vmem((2, 1024, 128), F32),
            vmem((2, 1024, 128), F32),
            vmem((2, DEV_BITS * 128, 128), BF16),
            vmem((2, 128, DEV_BITS * 128), BF16),
            vmem((2, DEV_BITS, 128, 128), F32),
            vmem((2, 128, 128), F32),
            vmem((2, 7, 128, 128), F32),
            vmem((2, 2, 128, 512), BF16),
            vmem((2, 2, 2, 64, 512), BF16),
            vmem((2, 2, 128, 512), F32),
            vmem((2, 2, 128, 512), F32),
            vmem((2, 2, 128, 512), BF16),
            vmem((2, 2, 128, 512), BF16),
            vmem((2, 2, 2, 64, 512), BF16),
            vmem((2, 2, 128, 512), BF16),
            vmem((4, 1024, 256), BF16),
            vmem((2, 128, 1024), F32),
            vmem((2, 128, 1024), F32),
            vmem((2, 128, 1024), F32),
            vmem((1024, 512), F32),
            dma((5,)), dma((8,)), dma,
            dma((4,)), dma((4,)), dma((6,)), dma((6,)), dma((4,)), dma((4,)),
            dma((7,)), dma((7,)), dma((9,)), dma((9,)),
            dma((8,)), dma((8,)), dma((8,)), dma((8,)), dma((12,)), dma((12,)),
        ],
        compiler_params=pltpu.CompilerParams(
            collective_id=0, has_side_effects=True, vmem_limit_bytes=40 * 1024 * 1024),
        cost_estimate=pl.CostEstimate(flops=6 * 10**9, bytes_accessed=8 * 2**20, transcendentals=0),
    )(
        *(pltpu.with_memory_space_constraint(x, pltpu.HBM) for x in (
            queries, key_rows, value_rows, level_weights, out_weight.reshape(256, 2048), out_grad)),
    )
    return pl.pallas_call(
        copy_kernel,
        out_shape=shapes,
        in_specs=[anywhere] * 5,
        out_specs=[hbm] * 5,
        scratch_shapes=[dma((5,))],
        compiler_params=pltpu.CompilerParams(vmem_limit_bytes=2 * 1024 * 1024),
        cost_estimate=pl.CostEstimate(flops=0, bytes_accessed=6 * 2**20, transcendentals=0),
    )(*outs)


def solution(mesh):
    in_specs = (
        P("seq", "head", None),
        P("seq", "head", None),
        P("seq", "head", None),
        P(None, "head", "seq"),
        P("head", None, None),
        P("seq", "head"),
    )
    out_specs = (
        P("seq", "head"),
        P("seq", "head", None),
        P("seq", "head", None),
        P("seq", "head", None),
        P(None, "head", "seq"),
    )
    return jax.shard_map(
        per_device, mesh=mesh, in_specs=in_specs, out_specs=out_specs, check_vma=False
    )
```

```python
import functools

import jax
import jax.numpy as jnp
from jax import lax
from jax.experimental import pallas as pl
from jax.experimental.pallas import tpu as pltpu
from jax.sharding import PartitionSpec as P

MESH = pl.DeviceIdType.MESH
F32 = jnp.float32
BF16 = jnp.bfloat16
LEVEL_GAIN = 0.02
BLK = 128
DIAG_LEVELS = 8
DEV_BITS = 5
PHASES = ((0,), (1, 2, 3), (4, 5, 6))
LOCAL_LEVELS = 11


def scale_of(level):
    return LEVEL_GAIN * 2.0 ** (-0.5 * max(level - 1, 0))


LOCAL_PAIRS = [(0, 1, 1), (0, 3, 1), (0, 5, 1), (0, 7, 1), (1, 2, 2), (1, 6, 2), (2, 4, 4)]


def mm(a, b):
    return jnp.dot(a, b, preferred_element_type=F32)


def mm_nt(a, b):
    return lax.dot_general(a, b, (((1,), (1,)), ((), ())), preferred_element_type=F32)


def kernel(
    q_in, k_in, v_in, lw_in, w_hbm, og_in,
    lo_out, dq_out, dk_out, dv_out, wg_out,
    q_ref, k_ref, v_ref, lw_ref, og_ref, lo_ref, dq_ref, dk_ref, dv_ref, wg_ref, kn, vn,
    wall, wsc, lev_ref, qt, kt, vt, gt, wq, st_ref, mix_ref, near, tb, tl, tlt, ot,
    sb, rb, cb, rcb, cs, cr, dkn, dvn, tst, tstt, lg, xf, llg,
    p2, alone, pf, po, summed, r1, ra, rb_sum, hall, dqa, dka, dva, acc,
    in_sem, out_sem, own_sem, w_send, w_recv, z_send, z_recv, f_send, f_recv, b_send, b_recv, c_send, c_recv, a_send, a_recv, r_send, r_recv, h_send, h_recv,
):
    me_s = lax.axis_index("seq")
    me_h = lax.axis_index("head")
    core = lax.rem(me_s, 2)
    right, left, across = lax.rem(me_h + 1, 4), lax.rem(me_h + 3, 4), lax.rem(me_h + 2, 4)

    def bit_of(bit):
        return lax.rem(lax.div(me_s, 1 << bit), 2)

    def flipped(bits):
        to = me_s
        for bit in bits:
            to = to + (1 << bit) - (2 << bit) * bit_of(bit)
        return to

    def partner(step):
        if step == 0:
            return flipped([0])
        low, j = (1, step) if step < 4 else (3, step - 3)
        return flipped([low + i for i in range(2) if j >> i & 1])

    def send(src, dst, send_sem, recv_sem, seq, head):
        copy = pltpu.make_async_remote_copy(
            src_ref=src, dst_ref=dst, send_sem=send_sem, recv_sem=recv_sem,
            device_id=(seq, head), device_id_type=MESH,
        )
        copy.start()
        return copy

    loads = []
    for n, (src, dst) in enumerate([(k_in, k_ref), (v_in, v_ref), (lw_in, lw_ref), (q_in, q_ref), (og_in, og_ref)]):
        loads.append(pltpu.make_async_copy(src, dst, in_sem.at[n]))
        loads[n].start()

    barrier = pltpu.get_barrier_semaphore()
    for other in (right, left, across):
        pl.semaphore_signal(barrier, inc=1, device_id=(me_s, other), device_id_type=MESH)
    for step in range(7):
        pl.semaphore_signal(barrier, inc=1, device_id=(partner(step), me_h), device_id_type=MESH)
    pl.semaphore_wait(barrier, 10)

    own = pltpu.make_async_copy(w_hbm.at[:, pl.ds(pl.multiple_of(me_h * 512, 512), 512)], wall.at[0], own_sem)
    def rows_at(start, size):
        return pl.ds(pl.multiple_of(start, 32), size)

    def columns_of(k):
        return pl.ds(pl.multiple_of(lax.rem(me_h + k, 4) * 512, 512), 512)

    half = rows_at(core * 128, 128)
    eighth = rows_at(core * 128 + lax.div(me_s, 8) * 32, 32)
    w_copies = {}

    def send_weights(i, k, rows):
        w_copies[i] = send(
            w_hbm.at[rows, columns_of(k)], wall.at[k, rows], w_send.at[i], w_recv.at[i], me_s, lax.rem(me_h + k, 4))

    direct, shared = 1 + 2 * core, (2, 3 - 2 * core)
    send_weights(0, direct, rows_at(core * 128, 64))
    send_weights(2, shared[0], eighth)
    send_weights(3, shared[1], eighth)
    send_weights(1, direct, rows_at(core * 128 + 64, 64))
    own.start()
    sibling = partner(0)
    f_copies = {}

    def to_sibling(i, k, rows):
        f_copies[i] = send(wall.at[k, rows], wall.at[k, rows], f_send.at[i], f_recv.at[i], sibling, me_h)

    z_copies = []

    def share_weights():
        for i, k in enumerate(shared):
            w_copies[2 + i].wait_recv()
            for n in range(3):
                at = 3 * i + n
                z_copies.append(send(
                    wall.at[k, eighth], wall.at[k, eighth], z_send.at[at], z_recv.at[at], partner(4 + n), me_h))

    def forward_shared(i):
        for n in range(3):
            z_copies[3 * i + n].wait_recv()
        to_sibling(2 + i, shared[i], half)

    row_id = lax.broadcasted_iota(jnp.int32, (BLK, BLK), 0)
    col_id = lax.broadcasted_iota(jnp.int32, (BLK, BLK), 1)
    apart = row_id ^ col_id
    level = jnp.zeros((BLK, BLK), jnp.int32)
    for bit in range(7):
        level = level + ((apart >> bit) > 0).astype(jnp.int32)
    lev_ref[...] = jnp.where(row_id <= col_id, level, -1)

    def cols_of(b):
        return pl.ds(pl.multiple_of(b * BLK, BLK), BLK)

    loads[0].wait()
    loads[1].wait()

    @pl.loop(0, 8, unroll=4)
    def _(b):
        cols = cols_of(b)
        k_all, v_all = k_ref[cols].reshape(BLK, 256), v_ref[cols].reshape(BLK, 256)
        for h in range(2):
            lanes = slice(h * 128, h * 128 + 128)
            kn[h, cols, :] = k_all[:, lanes]
            vn[h, cols, :] = v_all[:, lanes]
            kb, vb = k_all[:, lanes].T, v_all[:, lanes].T
            kt[h, :, cols] = kb
            vt[h, :, cols] = vb
            tb[h, b] = mm_nt(kb, vb)

    total = []
    for h in range(2):
        t = [tb[h, b] for b in range(8)]
        pairs = [t[2 * i] + t[2 * i + 1] for i in range(4)]
        quads = [pairs[0] + pairs[1], pairs[2] + pairs[3]]
        for slot, value in enumerate([t[0], t[2], t[4], t[6], pairs[0], pairs[2], quads[0]]):
            tl[h, slot] = value.astype(BF16)
            tlt[h, slot] = value.T.astype(BF16)
        xf[h] = quads[0] + quads[1]

    b_copies = {}

    def send_states(phase):
        for h in range(2):
            sb[phase, h] = xf[h].astype(BF16)
        for step in PHASES[phase]:
            b_copies[step] = send(sb.at[phase], rb.at[step], b_send.at[step], b_recv.at[step], partner(step), me_h)

    def keep_state(h, slot, value):
        kept = value * bit_of(slot).astype(F32)
        tst[h, slot * 128:slot * 128 + 128, :] = kept.astype(BF16)
        tstt[h, :, slot * 128:slot * 128 + 128] = kept.T.astype(BF16)

    def take_states(phase):
        for step in PHASES[phase]:
            b_copies[step].wait_recv()
        for h in range(2):
            got = [rb[step, h].astype(F32) for step in PHASES[phase]]
            if phase == 0:
                keep_state(h, 0, got[0])
                xf[h] = xf[h] + got[0]
            else:
                far = got[1] + got[2]
                keep_state(h, 2 * phase - 1, got[0])
                keep_state(h, 2 * phase, far)
                xf[h] = xf[h] + got[0] + far

    send_states(0)
    right_msgs, left_msgs = {}, {}

    def send_right(i, src, dst):
        right_msgs[i] = send(src, dst, r_send.at[2 + i], r_recv.at[2 + i], me_s, right)

    def send_left(i, src, dst):
        left_msgs[i] = send(src, dst, r_send.at[6 + i], r_recv.at[6 + i], me_s, left)

    def partial_grad(k, u, j):
        rows = slice(u * 512 + j * 256, u * 512 + j * 256 + 256)
        return mm_nt(wall[k], og_ref[rows, :])

    loads[4].wait()
    started = []

    def straight_leg(head, k, r, to):
        rows = rows_at(head * 128 + r * 64, 64)
        for u in range(2):
            alone[head, r, u] = mm_nt(wall[k, rows, :], og_ref[u * 512:u * 512 + 512, :]).astype(BF16)
            i = 4 * head + 2 * r + u
            started.append(send(alone.at[head, r, u], ra.at[head, r, u], a_send.at[i], a_recv.at[i], me_s, to))

    def await_straight(head, u):
        for r in range(2):
            i = 4 * head + 2 * r + u
            pltpu.make_async_remote_copy(
                src_ref=alone.at[head, r, u], dst_ref=ra.at[head, r, u], send_sem=a_send.at[i], recv_sem=a_recv.at[i],
                device_id=(me_s, left), device_id_type=MESH,
            ).wait_recv()

    for r in range(2):
        w_copies[r].wait_recv()
        to_sibling(r, direct, rows_at(core * 128 + r * 64, 64))
        straight_leg(core, direct, r, lax.rem(me_h + 3 + 2 * core, 4))
        if r == 0:
            share_weights()
    take_states(0)
    send_states(1)
    for r in range(2):
        f_copies[r].wait_recv()
        straight_leg(1 - core, 3 - 2 * core, r, lax.rem(me_h + 1 + 2 * core, 4))

    loads[2].wait()
    loads[3].wait()

    for h in range(2):
        for l in range(LOCAL_LEVELS + DEV_BITS):
            wsc[h, l:l + 1, :] = lw_ref[l, h:h + 1, :] * scale_of(l)

    @pl.loop(0, 8, unroll=4)
    def _(b):
        cols = cols_of(b)
        q_all = q_ref[cols].reshape(BLK, 256)
        for h in range(2):
            qb = q_all[:, h * 128:h * 128 + 128].T
            qt[h, :, cols] = qb
            qf = qb.astype(F32)
            for c in range(3 + DEV_BITS):
                wq[h, c, :, cols] = (qf * wsc[h, DIAG_LEVELS + c:DIAG_LEVELS + c + 1, cols]).astype(BF16)

    def diag_forward(b):
        cols = cols_of(b)
        for h in range(2):
            lev = lev_ref[...]
            mix = jnp.zeros((BLK, BLK), F32)
            for l in range(DIAG_LEVELS):
                mix = jnp.where(lev == l, wsc[h, l:l + 1, cols], mix)
            scores = mm(kn[h, cols, :], qt[h, :, cols])
            weighted = (mix * scores).astype(BF16)
            st_ref[h, b] = scores
            mix_ref[h, b] = mix
            near[h, b] = weighted
            ot[h, :, cols] = mm(vt[h, :, cols], weighted)

    pl.loop(0, 4, unroll=4)(diag_forward)
    forward_shared(0)

    def relay_leg(head, u, to):
        rows = rows_at(head * 128, 128)
        p2[head, u] = mm_nt(wall[2, rows, :], og_ref[u * 512:u * 512 + 512, :]).astype(BF16)
        i = 4 * head + u
        started.append(send(p2.at[head, u], r1.at[head, u], r_send.at[i], r_recv.at[i], me_s, to))

    def await_relay(head, u):
        i = 4 * head + u
        pltpu.make_async_remote_copy(
            src_ref=p2.at[head, u], dst_ref=r1.at[head, u], send_sem=r_send.at[i], recv_sem=r_recv.at[i],
            device_id=(me_s, left), device_id_type=MESH,
        ).wait_recv()

    for u in range(2):
        relay_leg(core, u, lax.rem(me_h + 1 + 2 * core, 4))
        if u == 0:
            f_copies[2].wait_recv()
            forward_shared(1)
        relay_leg(1 - core, u, lax.rem(me_h + 3 - 2 * core, 4))
        if u == 0:
            take_states(1)
            send_states(2)
    f_copies[3].wait_recv()
    for u in range(2):
        for head, k in ((0, 3), (1, 1)):
            pf[head, u] = mm_nt(wall[k, head * 128:head * 128 + 128, :], og_ref[u * 512:u * 512 + 512, :])
    pl.loop(4, 8, unroll=4)(diag_forward)

    for u in range(2):
        await_relay(0, u)
        summed[0, u] = (pf[0, u] + r1[0, u].astype(F32)).astype(BF16)
        send_right(u, summed.at[0, u], rb_sum.at[0, u])
        await_relay(1, u)
        summed[1, u] = (pf[1, u] + r1[1, u].astype(F32)).astype(BF16)
        send_left(u, summed.at[1, u], rb_sum.at[1, u])
    for h in range(2):
        for slot, (c, first, size) in enumerate(LOCAL_PAIRS):
            at = slice(first * BLK, (first + size) * BLK)
            ot[h, :, at] = ot[h, :, at] + mm(tlt[h, slot], wq[h, c, :, at])

    own.wait()
    for u in range(2):
        for j in range(2):
            at = slice(j * 256, j * 256 + 256)
            part = partial_grad(0, u, j)
            po[0, u, :, at] = part[:128]
            po[1, u, :, at] = part[128:]
    take_states(2)

    @pl.loop(0, 8, unroll=4)
    def _(b):
        cols = cols_of(b)
        for h in range(2):
            far = mm(tstt[h], wq[h, 3:, :, cols].reshape(DEV_BITS * 128, BLK))
            hall[0, cols, h * 128:h * 128 + 128] = (ot[h, :, cols] + far).T.astype(BF16)

    h_copies = {}

    def send_heads(i, slot, piece, to_slot, head):
        rows = slice(piece * 256, piece * 256 + 256)
        h_copies[i] = send(hall.at[slot, rows], hall.at[to_slot, rows], h_send.at[i], h_recv.at[i], me_s, head)

    for n in range(4):
        send_heads(n, 0, n, 1, right)
        send_heads(6 + n, 0, (n + 2) % 4, 3, left)

    def relay_heads(n):
        h_copies[n].wait_recv()
        send_heads(4 + n, 1, n, 2, right)
        h_copies[6 + n].wait_recv()
        send_heads(10 + n, 3, n + 2, 2, left)

    def take_head_grad(u):
        at = slice(u * 512, u * 512 + 512)
        await_straight(0, u)
        await_straight(1, u)
        right_msgs[u].wait_recv()
        left_msgs[u].wait_recv()
        for h in range(2):
            for r in range(2):
                rows = slice(r * 64, r * 64 + 64)
                gt[h, rows, at] = (
                    po[h, u, rows, :] + ra[h, r, u].astype(F32) + rb_sum[h, u, rows, :].astype(F32)).astype(BF16)
        for h in range(2):
            grads = mm_nt(wq[h, 3:, :, at].reshape(DEV_BITS * 128, 512), gt[h, :, at])
            for step in range(DEV_BITS):
                piece = grads[step * 128:step * 128 + 128]
                lg[h, step] = piece if u == 0 else lg[h, step] + piece

    c_copies = {}

    def swap_shares():
        other = 1 - core
        for n, slot in enumerate((3, 4, 1, 2)):
            cs[n] = lg[other, slot].astype(BF16)
        for h in range(2):
            cs[4 + h] = lg[h, 0].astype(BF16)
        for n, (start, size) in enumerate(((0, 2), (2, 4))):
            at = slice(start, start + size)
            c_copies[7 + n] = send(cs.at[at], cr.at[at], c_send.at[7 + n], c_recv.at[7 + n], sibling, me_h)

    def share_of(slot, n):
        return (lg[core, slot] + cr[n].astype(F32)) * bit_of(slot).astype(F32)

    def pass_on(phase):
        for n, step in enumerate(PHASES[phase]):
            c_copies[step] = send(
                cb.at[2 * phase - 2 + min(n, 1)], rcb.at[step], c_send.at[step], c_recv.at[step], partner(step), me_h)

    def await_steps(phase):
        got = None
        for step in PHASES[phase]:
            c_copies[step].wait_recv()
            piece = rcb[step].astype(F32)
            got = piece if got is None else got + piece
        return got

    def grads_to_z():
        c_copies[7].wait_recv()
        cb[2] = share_of(3, 0).astype(BF16)
        cb[3] = share_of(4, 1).astype(BF16)
        pass_on(2)

    def grads_to_y():
        c_copies[8].wait_recv()
        got = await_steps(2)
        xf[0] = got
        cb[0] = (got + share_of(1, 2)).astype(BF16)
        cb[1] = (got + share_of(2, 3)).astype(BF16)
        pass_on(1)

    def swap_results():
        got = xf[0] + await_steps(1)
        xf[0] = got
        cb[4] = got.astype(BF16)
        c_copies[0] = send(cb.at[4], rcb.at[0], c_send.at[0], c_recv.at[0], sibling, me_h)

    def final_grads():
        c_copies[0].wait_recv()
        mine = xf[0]
        theirs = rcb[0].astype(F32)
        second = core.astype(F32)
        first = 1.0 - second
        near_share = (1 - bit_of(0)).astype(F32)
        return [
            mine * first + theirs * second + cr[4].astype(F32) * near_share,
            mine * second + theirs * first + cr[5].astype(F32) * near_share,
        ]

    def diag_backward(b):
        cols = cols_of(b)
        for h in range(2):
            lev = lev_ref[...]
            gb = gt[h, :, cols]
            grad_scores = mm(vn[h, cols, :], gb)
            weighted = (mix_ref[h, b] * grad_scores).astype(BF16)
            product = grad_scores * st_ref[h, b]
            dqa[h, :, cols] = mm(kt[h, :, cols], weighted)
            dka[h, :, cols] = mm_nt(qt[h, :, cols], weighted)
            dva[h, :, cols] = mm_nt(gb, near[h, b])
            for l in range(DIAG_LEVELS):
                summed_l = jnp.sum(jnp.where(lev == l, product, 0.0), axis=0, keepdims=True)
                wg_ref[l, h:h + 1, cols] = summed_l * scale_of(l)

    def far_backward(b):
        cols = cols_of(b)
        for h in range(2):
            gb = gt[h, :, cols]
            qf = qt[h, :, cols].astype(F32)
            sums = dqa[h, :, cols]
            all_got = mm(tst[h], gb)
            for step in range(DEV_BITS):
                l = LOCAL_LEVELS + step
                got = all_got[step * 128:step * 128 + 128]
                sums = sums + got * wsc[h, l:l + 1, cols]
                wg_ref[l, h:h + 1, cols] = jnp.sum(got * qf, axis=0, keepdims=True) * scale_of(l)
            dqa[h, :, cols] = sums

    def local_backward(h):
        for l in range(DIAG_LEVELS, LOCAL_LEVELS):
            wg_ref[l, h:h + 1, :] = jnp.zeros((1, 1024), F32)
        for slot, (c, first, size) in enumerate(LOCAL_PAIRS):
            at = slice(first * BLK, (first + size) * BLK)
            l = DIAG_LEVELS + c
            gb = gt[h, :, at]
            got = mm(tl[h, slot], gb)
            dqa[h, :, at] = dqa[h, :, at] + got * wsc[h, l:l + 1, at]
            wg_ref[l, h:h + 1, at] = jnp.sum(got * qt[h, :, at].astype(F32), axis=0, keepdims=True) * scale_of(l)
            llg[h, slot] = mm_nt(wq[h, c, :, at], gb)

    take_head_grad(0)
    pl.loop(0, 4, unroll=4)(diag_backward)
    take_head_grad(1)
    swap_shares()
    pl.loop(0, 4, unroll=4)(far_backward)
    grads_to_z()
    pl.loop(4, 8, unroll=4)(diag_backward)
    relay_heads(0)
    relay_heads(1)
    for h in range(2):
        local_backward(h)
    grads_to_y()
    pl.loop(4, 8, unroll=4)(far_backward)

    stores = []

    def store(src, dst):
        stores.append(pltpu.make_async_copy(src, dst, out_sem.at[len(stores)]))
        stores[-1].start()

    store(wg_ref, wg_out)

    @pl.loop(0, 8, unroll=4)
    def _(b):
        cols = cols_of(b)
        both = jnp.concatenate([dqa[h, :, cols].T.astype(BF16) for h in range(2)], axis=1)
        dq_ref[cols] = both.reshape(BLK, 2, 128)

    store(dq_ref, dq_out)

    @pl.loop(0, 4, unroll=2)
    def _(b):
        rows = pl.ds(pl.multiple_of(b * 256, 256), 256)
        acc[rows, :] = mm(hall[0, rows, :], wall[0])

    for b in range(8):
        at = slice(b * BLK, b * BLK + BLK)
        for h in range(2):
            dk, dv = dka[h, :, at], dva[h, :, at]
            parts = [llg[h, slot] for slot, (c, first, size) in enumerate(LOCAL_PAIRS) if first - size <= b < first]
            if parts:
                x = functools.reduce(lambda a, p: a + p, parts)
                dk = dk + mm(x.astype(BF16), vt[h, :, at])
                dv = dv + mm(x.T.astype(BF16), kt[h, :, at])
            dkn[h, at, :] = dk.T
            dvn[h, at, :] = dv.T

    swap_results()
    for n in (2, 3):
        h_copies[n].wait_recv()
        h_copies[6 + n].wait_recv()

    @pl.loop(0, 4, unroll=2)
    def _(b):
        rows = pl.ds(pl.multiple_of(b * 256, 256), 256)
        acc[rows, :] = acc[rows, :] + mm(hall[1, rows, :], wall[1]) + mm(hall[3, rows, :], wall[3])

    late = [x.astype(BF16) for x in final_grads()]
    for b in range(4):
        at = slice(b * 256, b * 256 + 256)
        dk = [(dkn[h, at, :] + mm_nt(vn[h, at, :], late[h])).astype(BF16) for h in range(2)]
        dv = [(dvn[h, at, :] + mm(kn[h, at, :], late[h])).astype(BF16) for h in range(2)]
        dk_ref[at] = jnp.concatenate(dk, axis=1).reshape(256, 2, 128)
        dv_ref[at] = jnp.concatenate(dv, axis=1).reshape(256, 2, 128)

    store(dk_ref, dk_out)
    store(dv_ref, dv_out)

    for n in range(2):
        for i, b in ((4 + n, n), (10 + n, n + 2)):
            h_copies[i].wait_recv()
            rows = slice(b * 256, b * 256 + 256)
            lo_ref[rows, :] = (acc[rows, :] + mm(hall[2, rows, :], wall[2])).astype(BF16)
            store(lo_ref.at[rows], lo_out.at[rows])

    for group in (w_copies, f_copies, dict(enumerate(z_copies)), right_msgs, left_msgs, h_copies, b_copies, c_copies):
        for copy in group.values():
            copy.wait_send()
    for copy in started:
        copy.wait_send()
    for copy in stores:
        copy.wait()


def copy_kernel(*refs):
    sources, targets, sems = refs[:5], refs[5:10], refs[10]
    copies = [pltpu.make_async_copy(a, b, sems.at[i]) for i, (a, b) in enumerate(zip(sources, targets))]
    for copy in copies:
        copy.start()
    for copy in copies:
        copy.wait()


def per_device(queries, key_rows, value_rows, level_weights, out_weight, out_grad):
    dma = pltpu.SemaphoreType.DMA
    vmem = pltpu.VMEM
    anywhere = pl.BlockSpec(memory_space=pl.ANY)
    hbm = pl.BlockSpec(memory_space=pltpu.HBM)
    stack = 3 + DEV_BITS
    shape = queries.shape
    shapes = (
        jax.ShapeDtypeStruct(out_grad.shape, BF16),
        jax.ShapeDtypeStruct(shape, BF16),
        jax.ShapeDtypeStruct(shape, BF16),
        jax.ShapeDtypeStruct(shape, BF16),
        jax.ShapeDtypeStruct(level_weights.shape, F32),
    )
    outs = pl.pallas_call(
        kernel,
        out_shape=shapes,
        in_specs=[hbm] * 6,
        out_specs=[anywhere] * 5,
        scratch_shapes=[
            vmem(shape, BF16), vmem(shape, BF16), vmem(shape, BF16),
            vmem(level_weights.shape, F32), vmem(out_grad.shape, BF16),
            vmem(out_grad.shape, BF16),
            vmem(shape, BF16), vmem(shape, BF16), vmem(shape, BF16),
            vmem(level_weights.shape, F32),
            vmem((2, 1024, 128), BF16), vmem((2, 1024, 128), BF16),
            vmem((4, 256, 512), BF16),
            vmem((2, LOCAL_LEVELS + DEV_BITS, 1024), F32),
            vmem((BLK, BLK), jnp.int32),
            vmem((2, 128, 1024), BF16),
            vmem((2, 128, 1024), BF16),
            vmem((2, 128, 1024), BF16),
            vmem((2, 128, 1024), BF16),
            vmem((2, stack, 128, 1024), BF16),
            vmem((2, 8, BLK, BLK), F32),
            vmem((2, 8, BLK, BLK), F32),
            vmem((2, 8, BLK, BLK), BF16),
            vmem((2, 8, 128, 128), F32),
            vmem((2, 7, 128, 128), BF16),
            vmem((2, 7, 128, 128), BF16),
            vmem((2, 128, 1024), F32),
            vmem((3, 2, 128, 128), BF16),
            vmem((7, 2, 128, 128), BF16),
            vmem((5, 128, 128), BF16),
            vmem((7, 128, 128), BF16),
            vmem((6, 128, 128), BF16),
            vmem((6, 128, 128), BF16),
            vmem((2, 1024, 128), F32),
            vmem((2, 1024, 128), F32),
            vmem((2, DEV_BITS * 128, 128), BF16),
            vmem((2, 128, DEV_BITS * 128), BF16),
            vmem((2, DEV_BITS, 128, 128), F32),
            vmem((2, 128, 128), F32),
            vmem((2, 7, 128, 128), F32),
            vmem((2, 2, 128, 512), BF16),
            vmem((2, 2, 2, 64, 512), BF16),
            vmem((2, 2, 128, 512), F32),
            vmem((2, 2, 128, 512), F32),
            vmem((2, 2, 128, 512), BF16),
            vmem((2, 2, 128, 512), BF16),
            vmem((2, 2, 2, 64, 512), BF16),
            vmem((2, 2, 128, 512), BF16),
            vmem((4, 1024, 256), BF16),
            vmem((2, 128, 1024), F32),
            vmem((2, 128, 1024), F32),
            vmem((2, 128, 1024), F32),
            vmem((1024, 512), F32),
            dma((5,)), dma((8,)), dma,
            dma((4,)), dma((4,)), dma((6,)), dma((6,)), dma((4,)), dma((4,)),
            dma((7,)), dma((7,)), dma((9,)), dma((9,)),
            dma((8,)), dma((8,)), dma((8,)), dma((8,)), dma((12,)), dma((12,)),
        ],
        compiler_params=pltpu.CompilerParams(
            collective_id=0, has_side_effects=True, vmem_limit_bytes=40 * 1024 * 1024),
        cost_estimate=pl.CostEstimate(flops=6 * 10**9, bytes_accessed=8 * 2**20, transcendentals=0),
    )(
        *(pltpu.with_memory_space_constraint(x, pltpu.HBM) for x in (
            queries, key_rows, value_rows, level_weights, out_weight.reshape(256, 2048), out_grad)),
    )
    return pl.pallas_call(
        copy_kernel,
        out_shape=shapes,
        in_specs=[anywhere] * 5,
        out_specs=[hbm] * 5,
        scratch_shapes=[dma((5,))],
        compiler_params=pltpu.CompilerParams(vmem_limit_bytes=2 * 1024 * 1024),
        cost_estimate=pl.CostEstimate(flops=0, bytes_accessed=6 * 2**20, transcendentals=0),
    )(*outs)


def solution(mesh):
    in_specs = (
        P("seq", "head", None),
        P("seq", "head", None),
        P("seq", "head", None),
        P(None, "head", "seq"),
        P("head", None, None),
        P("seq", "head"),
    )
    out_specs = (
        P("seq", "head"),
        P("seq", "head", None),
        P("seq", "head", None),
        P("seq", "head", None),
        P(None, "head", "seq"),
    )
    return jax.shard_map(
        per_device, mesh=mesh, in_specs=in_specs, out_specs=out_specs, check_vma=False
    )
```
